32 devices in a mesh: dp: 8 (over z, x), tensor: 4 (over y, core).
Axes of the slice: x: 2, y: 2, z: 4, core: 2. Of those that a mesh axis runs over, the one named last changes fastest.
Arguments:
- tokens: bfloat16 [12608, 768], P(('dp', 'tensor')), may hold values from -6 to 6
- teacher: bfloat16 [12608, 768], P(('dp', 'tensor')), may hold values from -6 to 6
- valid_mask: int32 [64, 197], P('dp'), may hold values from 0 to 1, as said below
- expert_ids: int32 [12608, 2], P(('dp', 'tensor')), may hold values from 0 to 7, all different within a row; in each aligned block of 394 rows (0 to 393, 394 to 787, ...) at most 123 rows name the same one
- attn_gain: bfloat16 [768], P('dp'), may hold values from 0.5 to 1.5
- attn_shift: bfloat16 [768], P('dp'), may hold values from -1.5 to 1.5
- qkv_weight: bfloat16 [768, 3, 768], P('dp', None, 'tensor'), may hold values from -0.21875 to 0.21875
- proj_weight: bfloat16 [768, 768], P('dp', 'tensor'), may hold values from -1.5 to 1.5
- moe_gain: bfloat16 [768], P('dp'), may hold values from 0.5 to 1.5
- moe_shift: bfloat16 [768], P('dp'), may hold values from -1.5 to 1.5
- router_weight: bfloat16 [768, 8], P('dp'), may hold values from -0.15625 to 0.15625
- up_weight: bfloat16 [8, 768, 3072], P('dp', None, 'tensor'), may hold values from -0.21875 to 0.21875
- down_weight: bfloat16 [8, 768, 3072], P('dp', None, 'tensor'), may hold values from -0.625 to 0.625
Outputs:
- loss_value: float32 [], replicated
- output: bfloat16 [12608, 768], P(('dp', 'tensor'))
- grad_tokens: float32 [12608, 768], P(('dp', 'tensor'))
- grad_attn_gain: float32 [768], P('dp')
- grad_attn_shift: float32 [768], P('dp')
- grad_qkv_weight: float32 [768, 3, 768], P('dp', None, 'tensor')
- grad_proj_weight: float32 [768, 768], P('dp', 'tensor')
- grad_moe_gain: float32 [768], P('dp')
- grad_moe_shift: float32 [768], P('dp')
- grad_router_weight: float32 [768, 8], P('dp')
- grad_up_weight: float32 [8, 768, 3072], P('dp', None, 'tensor')
- grad_down_weight: float32 [8, 768, 3072], P('dp', None, 'tensor')
The draws below stay inside these ranges and needn't reach their ends.
Inputs may be any that keep to these rules, and one draw needn't show every extreme that they name: `valid_mask`: position 0 of every image is 1. `expert_ids`: each row names 2 different experts; among the 394 rows of one device (aligned blocks) no expert is named more than 123 times, a bound that some block reaches.
All inputs are finite; a program needn't handle non-finite values.
Results may differ from the reference program's by a relative error of at most 0.0085.
Values may be sent and summed in bfloat16 or wider, within the bound.
No kernel may reach another device: no remote copies, remote signals or barrier semaphores. Data moves between devices by JAX's collectives and lax.ppermute only.
A program may use at most 192 MiB of HBM per device.

```python
import math
import jax
import jax.numpy as jnp
import numpy as np
from jax import lax

D = 768
HEADS = 12
HD = 64
FF = 3072
SEQ = 197
TOP = 2
IMG_DEV = 8
IMAGES = 64
TOKENS = 12608
ROWS_DEV = 394
EXPERTS = 8
CAP = 123
N_DP = 8
N_TENSOR = 4


def draw_valid_mask(key, part):
    level = 300 + 650 * lax.iota(jnp.int32, IMAGES) // max(IMAGES - 1, 1)
    noise = jax.random.randint(key, (IMAGES, SEQ), 0, 1000)
    keep = (noise < level[:, None]).astype(jnp.int32)
    first = (lax.iota(jnp.int32, SEQ) == 0).astype(jnp.int32)
    return jnp.maximum(keep, first[None, :])


def steps_of(own_key, dims, cuts, least, top_value):
    loudness = 1.0
    for axis_at, parts in cuts:
        heights = jax.random.uniform(jax.random.fold_in(jax.random.fold_in(own_key, 6), axis_at), (parts,), jnp.float32, least / len(cuts), top_value / len(cuts))
        loudness = loudness * jnp.repeat(jnp.exp(heights), dims[axis_at] // parts).reshape((-1,) + (1,) * (len(dims) - 1 - axis_at))
    return loudness


def shared_out(rng, own, number, rows, count, top, limit, slope):
    order = jax.random.permutation(rng, count)
    crowded, usual = shares(count, rows * top, limit, slope, True), shares(count, rows * top, limit, slope, False)
    places = jnp.arange(count)

    def named(lengths, offset_by):
        used = int((lengths > 0).sum())
        fixed = max(1, used // 4)
        passed = fixed + (places - fixed + offset_by * (used - fixed)) % max(1, count - fixed)
        return jnp.zeros((count,), jnp.int32).at[order[jnp.where(places < fixed, places, passed)]].set(jnp.asarray(lengths, jnp.int32))

    lengths = jnp.where(number % 4 == 0, named(crowded, number // 4), named(usual, number - number // 4 - 1))
    mixed = jax.random.permutation(jax.random.fold_in(own, 3), count)
    giver, sink = mixed[0:count // 2 * 2:2], mixed[1:count // 2 * 2:2]
    room = jnp.minimum(lengths[giver] - 1, limit - lengths[sink]) // 2
    room = jnp.where((giver == order[0]) | (sink == order[0]) | (lengths[sink] == 0), 0, jnp.maximum(room, 0))
    passed = jax.random.randint(jax.random.fold_in(own, 4), (count // 2,), 0, 1 << 20) % (room + 1)
    lengths = lengths.at[giver].add(-passed).at[sink].add(passed)
    items = jnp.searchsorted(jnp.cumsum(lengths), jnp.arange(rows * top), side="right").astype(jnp.int32)
    table = items.reshape(top, rows).T
    table = table[jax.random.permutation(jax.random.fold_in(own, 1), rows)]
    offset_by = jax.random.randint(jax.random.fold_in(own, 2), (rows, 1), 0, top)
    return jnp.take_along_axis(table, (jnp.arange(top)[None, :] + offset_by) % top, axis=1)


def shares(count, total, bound, lean, full):
    loads = [(1 << 20) // math.isqrt(grade ** lean) + 1 for grade in range(1, count + 1)]
    largest = bound if full else min(bound, max(-(-total // count), total * loads[0] // sum(loads)))
    least = 1 if total - largest >= count - 1 else 0
    holding, surplus = [largest] + [least] * (count - 1), total - largest - least * (count - 1)
    while surplus > 0:
        movable = [i for i in range(1, count) if holding[i] < largest] or [i for i in range(1, count) if holding[i] < bound]
        mass, remaining = sum([loads[i] for i in movable]), surplus
        for i in movable:
            extra = min(bound - holding[i], max(1, remaining * loads[i] // mass), surplus)
            holding[i] = holding[i] + extra
            surplus = surplus - extra
    return np.array(holding)


def centred(key, shape, deviation, bound, pieces=(), held_as=jnp.bfloat16):
    gain = steps_of(key, shape, pieces, -0.22, 0.18) if pieces else 1.0
    array = jax.random.normal(key, shape, jnp.float32) * deviation * gain
    return jnp.minimum(jnp.maximum(array, -bound), bound).astype(held_as)


def setup_inputs(seed: int = 0) -> dict:
    streams_of = jax.random.split(jax.random.key(seed), 14)
    tokens = centred(streams_of[0], (TOKENS, D), 1.0, 6.0, ((0, 32),))
    teacher = centred(streams_of[1], (TOKENS, D), 1.0, 6.0, ((0, 32),))
    valid_mask = draw_valid_mask(jax.random.fold_in(streams_of[13], 71), 0)
    expert_ids_keys = jax.random.split(jax.random.fold_in(streams_of[3], 1), TOKENS // ROWS_DEV)
    expert_ids_turns = jax.random.permutation(jax.random.fold_in(streams_of[3], 3), TOKENS // ROWS_DEV)
    expert_ids = jax.vmap(lambda own, number: shared_out(jax.random.fold_in(streams_of[3], 2), own, number, ROWS_DEV, EXPERTS, TOP, CAP, 1))(expert_ids_keys, expert_ids_turns).reshape((TOKENS, TOP))
    attn_gain = jnp.clip(1.0 + 0.1 * jax.random.normal(streams_of[4], (D,), jnp.float32), 0.5, 1.5).astype(jnp.bfloat16)
    attn_shift = centred(streams_of[5], (D,), 0.3, 1.5, ((0, 8),))
    qkv_weight = centred(streams_of[6], (D, 3, D), D ** -0.5, 0.21875, ((0, 8), (2, 4)))
    proj_weight = centred(streams_of[7], (D, D), (max(1, D // 48)) ** -0.5, 1.5, ((0, 8), (1, 4)))
    moe_gain = jnp.clip(1.0 + 0.1 * jax.random.normal(streams_of[8], (D,), jnp.float32), 0.5, 1.5).astype(jnp.bfloat16)
    moe_shift = centred(streams_of[9], (D,), 0.3, 1.5, ((0, 8),))
    router_weight = centred(streams_of[10], (D, EXPERTS), (2 * D) ** -0.5, 0.15625, ((0, 8),))
    up_weight = centred(streams_of[11], (EXPERTS, D, FF), D ** -0.5, 0.21875, ((0, 8), (2, 4)))
    down_weight = centred(streams_of[12], (EXPERTS, D, FF), (max(1, 2 * FF // (EXPERTS * EXPERTS))) ** -0.5, 0.625, ((0, 8), (2, 4)))
    return {"tokens": tokens, "teacher": teacher, "valid_mask": valid_mask, "expert_ids": expert_ids, "attn_gain": attn_gain, "attn_shift": attn_shift, "qkv_weight": qkv_weight, "proj_weight": proj_weight, "moe_gain": moe_gain, "moe_shift": moe_shift, "router_weight": router_weight, "up_weight": up_weight, "down_weight": down_weight}


@jax.custom_vjp
def low(v):
    return lax.optimization_barrier(v.astype(jnp.bfloat16)).astype(jnp.float32)

@jax.custom_vjp
def low_back(v):
    return v

def low_keep(v):
    return (low(v), None)

def low_pass(kept, grad):
    return (grad,)

def back_keep(v):
    return (v, None)

def back_low(kept, grad):
    return (low(grad),)
low.defvjp(low_keep, low_pass)
low_back.defvjp(back_keep, back_low)
EPSILON = 1e-06
MASKED = -1000000000.0
HIGHEST = lax.Precision.HIGHEST

def layer_norm(values, norm_gain, norm_shift):
    center = values - lax.optimization_barrier(jnp.mean(values, axis=-1, keepdims=True))
    spread = lax.optimization_barrier(jnp.mean(center * center, axis=-1, keepdims=True))
    return center * lax.rsqrt(spread + EPSILON) * norm_gain + norm_shift

def group_loss(params, tokens, teacher, valid_mask, expert_ids):
    gain_one, shift_one, qkv_weight, proj_weight, gain_two, shift_two, router_weight, up_weight, down_weight = params
    group_len = IMG_DEV * SEQ
    normed = low(layer_norm(tokens, gain_one, shift_one))
    qkv_act = jnp.einsum('td,dcf->tcf', normed, qkv_weight, precision=HIGHEST)
    qkv_act = low(low_back(qkv_act))
    qkv_parts = qkv_act.reshape(IMG_DEV, SEQ, 3, HEADS, HD)
    queries = qkv_parts[:, :, 0]
    keys_all = qkv_parts[:, :, 1]
    values_all = qkv_parts[:, :, 2]
    scores = low_back(jnp.einsum('bqhe,bkhe->bhqk', queries, keys_all, precision=HIGHEST) * HD ** (-0.5))
    key_valid = (valid_mask > 0)[:, None, None, :]
    scores = jnp.where(key_valid, scores, MASKED)
    log_total = jax.nn.logsumexp(scores, axis=-1, keepdims=True)
    attn_probs = low(jnp.exp(scores - log_total))
    context = jnp.einsum('bhqk,bkhe->bqhe', attn_probs, values_all, precision=HIGHEST)
    context = low(low_back(context)).reshape(group_len, D)
    attn_out = low_back(jnp.dot(context, proj_weight.T, precision=HIGHEST))
    residual = tokens + attn_out
    hidden_in = low(layer_norm(residual, gain_two, shift_two))
    logits = low_back(jnp.dot(hidden_in, router_weight, precision=HIGHEST))
    router_probs = jax.nn.softmax(logits, axis=-1)
    gate_values = jnp.take_along_axis(router_probs, expert_ids, axis=1)
    flat_ids = expert_ids.reshape(N_TENSOR, -1)
    onehot = (flat_ids[:, :, None] == jnp.arange(EXPERTS, dtype=jnp.int32)[None, None, :]).astype(jnp.int32)
    earlier = jnp.cumsum(onehot, axis=1) - onehot
    slot_index = lax.optimization_barrier(jnp.sum(earlier * onehot, axis=2))
    device_of = jnp.arange(N_TENSOR, dtype=jnp.int32)[:, None]
    position = (flat_ids * (N_TENSOR * CAP) + device_of * CAP + slot_index).reshape(-1)
    token_of = jnp.repeat(jnp.arange(group_len, dtype=jnp.int32), TOP)
    table = jnp.full((EXPERTS * N_TENSOR * CAP,), group_len, dtype=jnp.int32).at[position].set(token_of)
    padded = jnp.concatenate([hidden_in, jnp.zeros((1, D), dtype=jnp.float32)], axis=0)
    expert_in = low_back(padded[table]).reshape(EXPERTS, N_TENSOR * CAP, D)
    up_values = low_back(jnp.einsum('ecd,edf->ecf', expert_in, up_weight, precision=HIGHEST))
    hidden_act = low(jax.nn.gelu(up_values, approximate=False))
    expert_out = jnp.einsum('ecf,edf->ecd', hidden_act, down_weight, precision=HIGHEST)
    expert_out = low(low_back(expert_out)).reshape(-1, D)
    picked = expert_out[position].reshape(group_len, TOP, D)
    moe_out = lax.optimization_barrier(jnp.sum(gate_values[:, :, None] * picked, axis=1))
    result = residual + moe_out
    errors = result - teacher
    mask_rows = valid_mask.reshape(-1).astype(jnp.float32)
    return (jnp.sum(mask_rows * lax.optimization_barrier(jnp.mean(errors * errors, axis=-1))), result)

def forward(params, tokens, teacher, valid_mask, expert_ids):
    group_len = IMG_DEV * SEQ
    group_fn = jax.checkpoint(group_loss)

    def scan_step(loss_sum, group_item):
        token_part, teacher_part, mask_part, ids_part = group_item
        part_sum, part_out = group_fn(params, token_part, teacher_part, mask_part, ids_part)
        return (loss_sum + part_sum, part_out)
    inputs = (tokens.reshape(N_DP, group_len, D), teacher.reshape(N_DP, group_len, D), valid_mask.reshape(N_DP, IMG_DEV, SEQ), expert_ids.reshape(N_DP, group_len, TOP))
    loss_sum, outputs = lax.scan(scan_step, jnp.zeros((), dtype=jnp.float32), inputs)
    valid_count = jnp.sum(valid_mask).astype(jnp.float32)
    return (loss_sum / valid_count, outputs.reshape(TOKENS, D))

def reference(tokens, teacher, valid_mask, expert_ids, attn_gain, attn_shift, qkv_weight, proj_weight, moe_gain, moe_shift, router_weight, up_weight, down_weight):
    params = (attn_gain.astype(jnp.float32), attn_shift.astype(jnp.float32), qkv_weight.astype(jnp.float32), proj_weight.astype(jnp.float32), moe_gain.astype(jnp.float32), moe_shift.astype(jnp.float32), router_weight.astype(jnp.float32), up_weight.astype(jnp.float32), down_weight.astype(jnp.float32))
    token_values = tokens.astype(jnp.float32)
    teacher_values = teacher.astype(jnp.float32)

    def objective(params_in, token_in):
        return forward(params_in, token_in, teacher_values, valid_mask, expert_ids)
    loss_value, pullback, output = jax.vjp(objective, params, token_values, has_aux=True)
    loss_scale = jnp.ones_like(loss_value) * (0.5 * D * TOKENS)
    param_grads, grad_tokens = pullback(loss_scale)
    return (loss_value, output.astype(jnp.bfloat16), grad_tokens, param_grads[0], param_grads[1], param_grads[2], param_grads[3], param_grads[4], param_grads[5], param_grads[6], param_grads[7], param_grads[8])
```

```python
import jax
import jax.numpy as jnp
from jax import lax
from jax.sharding import PartitionSpec as P

HD = 64
EPSILON = 1e-06
MASKED = -1000000000.0
BF = jnp.bfloat16
F32 = jnp.float32
TREE = 8


def dot(a, b, ca, cb):
    return lax.dot_general(a, b, (((ca,), (cb,)), ((), ())), preferred_element_type=F32)


def swap(value, axis, k):
    n = lax.axis_size(axis)
    return lax.ppermute(value, axis, [(i, i ^ k) for i in range(n)])


def bit(axis, k):
    return (lax.axis_index(axis) // k) % 2 == 1


def pair(low, high, flip, at):
    return jnp.where(flip, jnp.stack([high, low], at), jnp.stack([low, high], at))


def gather_z(v, at):
    r1, r2, r3 = swap(v, "dp", 2), swap(v, "dp", 4), swap(v, "dp", 6)
    odd, far = bit("dp", 2), bit("dp", 4)
    low, high = pair(v, r1, odd, at), pair(r2, r3, odd, at)
    return jnp.where(far, jnp.concatenate([high, low], at), jnp.concatenate([low, high], at))


def gather_x(v, at):
    return pair(v, swap(v, "dp", 1), bit("dp", 1), at)


def gather_t(v, k):
    return jnp.stack([v, swap(v, "tensor", k)], 0)


def gather_dense(v, order):
    dims = []
    for axis in order:
        if axis in "yc":
            v = gather_t(v, 2 if axis == "y" else 1)
            dims = [axis] + dims
        else:
            lead = sum(d in "yc" for d in dims)
            at = lead + (1 if axis == "x" and "z" in dims else 0)
            v = gather_z(v, at) if axis == "z" else gather_x(v, at)
            dims = dims[:at] + [axis] + dims[at:]
    if dims[0] == "c":
        v = jnp.swapaxes(v, 0, 1)
    return v.reshape(4, 768, v.shape[-1])


def take(v, index, at):
    return lax.dynamic_index_in_dim(v, index, at, keepdims=False)


def scatter_dense(v, order):
    rows = v.shape[1] // 8
    v = v.reshape(2, 2, 4, 2, rows, v.shape[-1])
    dims = ["y", "c", "z", "x"]
    me = lax.axis_index("dp")
    for axis in order:
        at = dims.index(axis)
        if axis in "yc":
            kept, sent = take(v, 0, at), take(v, 1, at)
            v = kept + swap(sent.astype(BF), "tensor", 2 if axis == "y" else 1).astype(F32)
        elif axis == "x":
            x = me % 2
            v = take(v, x, at) + swap(take(v, 1 - x, at).astype(BF), "dp", 1).astype(F32)
        else:
            z = me // 2
            total = take(v, z, at)
            for k in (1, 2, 3):
                total = total + swap(take(v, z ^ k, at).astype(BF), "dp", 2 * k).astype(F32)
            v = total
        dims.pop(at)
    return v


ORDERS = ("zxyc", "zyxc", "yzxc")


def dense_weights(shard):
    if lax.axis_size("dp") == TREE and lax.axis_size("tensor") == 4:
        c = shard.shape[1] // 3
        parts = [gather_dense(shard[:, i * c : (i + 1) * c], ORDERS[i]) for i in range(3)]
        return jnp.concatenate(parts, -1)
    v = lax.all_gather(shard, "dp", axis=0, tiled=True)
    return lax.all_gather(v, "tensor", axis=0)


def dense_sums(v):
    if lax.axis_size("dp") == TREE and lax.axis_size("tensor") == 4:
        c = v.shape[2] // 3
        parts = [scatter_dense(v[:, :, i * c : (i + 1) * c], ORDERS[i][::-1]) for i in range(3)]
        return jnp.concatenate(parts, -1)
    v = lax.psum_scatter(v, "tensor", scatter_dimension=0, tiled=False)
    return lax.psum_scatter(v, "dp", scatter_dimension=0, tiled=True)


def small_gather(v):
    if lax.axis_size("dp") == TREE:
        return gather_x(gather_z(v, 0), 1).reshape((-1,) + v.shape[1:])
    return lax.all_gather(v, "dp", axis=0, tiled=True)


def sum_over(v, axis):
    n = lax.axis_size(axis)
    if n > TREE:
        return lax.psum(v, axis)
    total = v
    for k in range(1, n):
        total = total + swap(v, axis, k)
    return total


def exchange(v):
    n = lax.axis_size("dp")
    if n > TREE:
        return lax.all_to_all(v, "dp", split_axis=0, concat_axis=0, tiled=True)
    return jnp.stack([v[0]] + [swap(v[k], "dp", k) for k in range(1, n)])


def relative(index):
    return index ^ lax.axis_index("dp") if lax.axis_size("dp") <= TREE else index


def gather_experts(v):
    if lax.axis_size("tensor") != 4:
        return lax.all_gather(v, "tensor", axis=0)
    two = jnp.stack([v, swap(v, "tensor", 2)])
    return jnp.concatenate([two, swap(two, "tensor", 1)])


def sum_experts(v):
    if lax.axis_size("tensor") != 4:
        return lax.psum_scatter(v, "tensor", scatter_dimension=0, tiled=False)
    two = v[:2] + swap(v[2:].astype(BF), "tensor", 1).astype(F32)
    return two[0] + swap(two[1].astype(BF), "tensor", 2).astype(F32)


def norm_parts(v):
    center = v - jnp.mean(v, axis=-1, keepdims=True)
    scale = lax.rsqrt(jnp.mean(center * center, axis=-1, keepdims=True) + EPSILON)
    return center * scale, scale


def norm_back(grad, n, scale, gain):
    gy = grad * gain
    back = scale * (
        gy - jnp.mean(gy, -1, keepdims=True) - n * jnp.mean(gy * n, -1, keepdims=True)
    )
    return back, jnp.sum(grad * n, 0), jnp.sum(grad, 0)


def local(
    tokens,
    teacher,
    valid_mask,
    expert_ids,
    attn_gain,
    attn_shift,
    qkv_weight,
    proj_weight,
    moe_gain,
    moe_shift,
    router_weight,
    up_weight,
    down_weight,
):
    rows, width = tokens.shape
    length = valid_mask.shape[1]
    images = rows // length
    experts = router_weight.shape[1]
    top = expert_ids.shape[1]
    capacity = max(2, (top * rows + experts - 1) // experts * 5 // 4)
    slots = -(-capacity // 16) * 16
    padded = -(-length // 16) * 16
    tensor_count = lax.axis_size("tensor")
    tensor_me = lax.axis_index("tensor")

    def pad(v, value=0):
        v = v.reshape((images, length) + v.shape[1:])
        v = jnp.pad(v, ((0, 0), (0, padded - length)) + ((0, 0),) * (v.ndim - 2), constant_values=value)
        return v.reshape((images * padded,) + v.shape[2:])

    def unpad(v):
        return v.reshape(images, padded, -1)[:, :length].reshape(rows, -1)

    heads_width = proj_weight.shape[1]
    shard = jnp.concatenate([qkv_weight.reshape(-1, 3 * heads_width), proj_weight], 1)
    dense = dense_weights(shard)
    small = jnp.concatenate(
        [attn_gain[:, None], attn_shift[:, None], moe_gain[:, None], moe_shift[:, None], router_weight], 1
    )
    small = small_gather(small)
    gain_one, shift_one, gain_two, shift_two = (small[:, i].astype(F32)[None] for i in range(4))
    router = small[:, 4:]
    up_all = gather_experts(up_weight[0])
    down_all = gather_experts(down_weight[0])
    count = sum_over(jnp.sum(valid_mask).astype(F32)[None], "dp")[0]
    own_mask = lax.dynamic_slice_in_dim(valid_mask, tensor_me * images, images)
    own_mask = jnp.pad(own_mask, ((0, 0), (0, padded - length)))
    row_mask = own_mask.reshape(-1, 1).astype(F32)

    ids = pad(expert_ids, -1)
    ids_rel = jnp.where(ids < 0, -1, relative(ids))
    each = lax.iota(jnp.int32, experts)
    names = jnp.any(ids_rel[:, :, None] == each, axis=1)
    padded_rows = images * padded
    row_at = lax.iota(jnp.int32, padded_rows)
    before = (row_at[:, None] > row_at[None, :]).astype(BF)
    slot = dot(before, names.astype(BF), 1, 0).astype(jnp.int32)
    slot = jnp.where(names, slot, -1)
    place = jnp.where(ids < 0, -1, ids_rel * slots + jnp.sum(jnp.where(ids_rel[:, :, None] == each, slot[:, None, :], 0), -1))
    slot_at = lax.iota(jnp.int32, slots)
    to_slots = (slot.T[:, None, :] == slot_at[None, :, None]).astype(BF).reshape(experts * slots, padded_rows)

    x = pad(tokens).astype(F32)
    n_one, scale_one = norm_parts(x)
    h1 = (n_one * gain_one + shift_one).astype(BF)
    heads = heads_width // HD
    qkv = jnp.einsum("rd,tdc->trc", h1, dense[:, :, : 3 * heads_width], preferred_element_type=F32).astype(BF)
    parts = qkv.reshape(tensor_count, images, padded, 3, heads, HD)
    q, k, v = parts[:, :, :, 0], parts[:, :, :, 1], parts[:, :, :, 2]
    scores = jnp.einsum("tbqhe,tbkhe->tbhqk", q, k, preferred_element_type=F32) * HD**-0.5
    scores = jnp.where((own_mask > 0)[None, :, None, None, :], scores, MASKED)
    log_total = jax.nn.logsumexp(scores, axis=-1, keepdims=True)
    probs_f = jnp.exp(scores - log_total)
    probs = probs_f.astype(BF)
    context = jnp.einsum("tbhqk,tbkhe->tbqhe", probs, v, preferred_element_type=F32).astype(BF)
    context = context.reshape(tensor_count, padded_rows, heads_width)
    proj = dense[:, :, 3 * heads_width :]
    attn = jnp.einsum("trc,tdc->rd", context, proj, preferred_element_type=F32)
    residual = x + attn
    n_two, scale_two = norm_parts(residual)
    h2 = (n_two * gain_two + shift_two).astype(BF)
    router_probs = jax.nn.softmax(dot(h2, router, 1, 0), axis=-1)
    choose = (ids[:, :, None] == each).astype(F32)
    gates = jnp.sum(choose * router_probs[:, None, :], -1)
    gates_rel = jnp.sum((ids_rel[:, :, None] == each).astype(F32) * gates[:, :, None], 1)

    sent = dot(to_slots, h2, 1, 0).astype(BF).reshape(experts, slots, width)
    arrived = exchange(sent).reshape(-1, width)
    up = [dot(arrived, up_all[t], 1, 0) for t in range(tensor_count)]
    hidden = [jax.nn.gelu(u, approximate=False).astype(BF) for u in up]
    out = sum(dot(hidden[t], down_all[t], 1, 1) for t in range(tensor_count))
    returned = exchange(out.astype(BF).reshape(experts, slots, width)).reshape(-1, width)
    all_at = lax.iota(jnp.int32, experts * slots)
    picked = [dot((place[:, j : j + 1] == all_at).astype(BF), returned, 1, 0) for j in range(top)]
    result = residual + sum(gates[:, j : j + 1] * picked[j] for j in range(top))
    errors = result - pad(teacher).astype(F32)
    loss_sum = jnp.sum(row_mask * jnp.mean(errors * errors, -1, keepdims=True))
    loss = sum_over(sum_over(loss_sum[None], "tensor"), "dp")[0] / count
    total_rows = rows * lax.axis_size("dp") * tensor_count
    g = row_mask * errors * (total_rows / count)
    grad_gates = jnp.stack([jnp.sum(g * picked[j], -1) for j in range(top)], 1)
    gated = (gates_rel.T[:, :, None] * g[None]).astype(BF)
    grad_sent = jnp.einsum(
        "esr,erd->esd", to_slots.reshape(experts, slots, padded_rows), gated, preferred_element_type=F32
    ).astype(BF)
    grad_out = exchange(grad_sent).reshape(-1, width)
    grad_up = []
    for t in range(tensor_count):
        gh = dot(grad_out, down_all[t], 1, 0)
        grad_up.append(jax.vjp(lambda u: jax.nn.gelu(u, approximate=False), up[t])[1](gh)[0].astype(BF))
    grad_arrived = sum(dot(grad_up[t], up_all[t], 1, 1) for t in range(tensor_count))
    grad_back = exchange(grad_arrived.astype(BF).reshape(experts, slots, width)).reshape(-1, width)
    grad_down_w = sum_experts(jnp.stack([dot(grad_out, hidden[t], 0, 0) for t in range(tensor_count)]))
    grad_up_w = sum_experts(jnp.stack([dot(arrived, grad_up[t], 0, 0) for t in range(tensor_count)]))

    either = jnp.any(place[:, :, None] == all_at, axis=1).astype(BF)
    grad_probs = jnp.sum(choose * grad_gates[:, :, None], 1)
    grad_logits = router_probs * (grad_probs - jnp.sum(router_probs * grad_probs, -1, keepdims=True))
    grad_logits = grad_logits.astype(BF)
    grad_h2 = dot(either, grad_back, 1, 0) + dot(grad_logits, router, 1, 1)
    grad_router = dot(h2, grad_logits, 0, 0)
    back, grad_gain_two, grad_shift_two = norm_back(grad_h2, n_two, scale_two, gain_two)
    grad_residual = g + back

    grad_attn = grad_residual.astype(BF)
    grad_context = jnp.einsum("rd,tdc->trc", grad_attn, proj, preferred_element_type=F32).astype(BF)
    grad_proj = jnp.einsum("rd,trc->tdc", grad_attn, context, preferred_element_type=F32)
    gc = grad_context.reshape(tensor_count, images, padded, heads, HD)
    grad_v = jnp.einsum("tbhqk,tbqhe->tbkhe", probs, gc, preferred_element_type=F32)
    grad_pr = jnp.einsum("tbqhe,tbkhe->tbhqk", gc, v, preferred_element_type=F32)
    delta = jnp.sum(probs_f * grad_pr, -1, keepdims=True)
    grad_scores = (probs_f * (grad_pr - delta)).astype(BF)
    grad_q = jnp.einsum("tbhqk,tbkhe->tbqhe", grad_scores, k, preferred_element_type=F32) * HD**-0.5
    grad_k = jnp.einsum("tbhqk,tbqhe->tbkhe", grad_scores, q, preferred_element_type=F32) * HD**-0.5
    grad_qkv = jnp.stack([grad_q, grad_k, grad_v], 3).astype(BF)
    grad_qkv = grad_qkv.reshape(tensor_count, padded_rows, 3 * heads_width)
    grad_qkv_w = jnp.einsum("rd,trc->tdc", h1, grad_qkv, preferred_element_type=F32)
    grad_h1 = jnp.einsum("trc,tdc->rd", grad_qkv, dense[:, :, : 3 * heads_width], preferred_element_type=F32)
    back, grad_gain_one, grad_shift_one = norm_back(grad_h1, n_one, scale_one, gain_one)
    grad_tokens = grad_residual + back

    summed = dense_sums(jnp.concatenate([grad_qkv_w, grad_proj], -1))
    vectors = jnp.concatenate(
        [jnp.stack([grad_gain_one, grad_shift_one, grad_gain_two, grad_shift_two]), grad_router.T]
    )
    n_dp = lax.axis_size("dp")
    vectors = vectors.reshape(4 + experts, n_dp, width // n_dp).swapaxes(0, 1)
    vectors = sum_over(vectors, "tensor")
    if n_dp > TREE:
        vectors = lax.psum_scatter(vectors, "dp", scatter_dimension=0, tiled=False)
    else:
        me = lax.axis_index("dp")
        own = take(vectors, me, 0)
        for k in range(1, n_dp):
            own = own + swap(take(vectors, me ^ k, 0), "dp", k)
        vectors = own
    return (
        loss,
        unpad(result).astype(BF),
        unpad(grad_tokens),
        vectors[0],
        vectors[1],
        summed[:, : 3 * heads_width].reshape(-1, 3, heads_width),
        summed[:, 3 * heads_width :],
        vectors[2],
        vectors[3],
        vectors[4:].T,
        grad_up_w[None],
        grad_down_w[None],
    )


def solution(mesh):
    rows = P(("dp", "tensor"), None)
    experts = P("dp", None, "tensor")
    in_specs = (
        rows,
        rows,
        P("dp", None),
        rows,
        P("dp"),
        P("dp"),
        experts,
        P("dp", "tensor"),
        P("dp"),
        P("dp"),
        P("dp", None),
        experts,
        experts,
    )
    out_specs = (
        P(),
        rows,
        rows,
        P("dp"),
        P("dp"),
        experts,
        P("dp", "tensor"),
        P("dp"),
        P("dp"),
        P("dp", None),
        experts,
        experts,
    )
    return jax.shard_map(local, mesh=mesh, in_specs=in_specs, out_specs=out_specs, check_vma=False)
```

```python
import functools
import jax
import jax.numpy as jnp
from jax import lax
from jax.experimental import pallas as pl
from jax.experimental.pallas import tpu as pltpu
from jax.sharding import PartitionSpec as P

HD = 64
EPSILON = 1e-06
MASKED = -1000000000.0
BF = jnp.bfloat16
F32 = jnp.float32
LOG2E = 1.4426950408889634
MIB = 1 << 20


def dot(a, b, ca, cb):
    return lax.dot_general(a, b, (((ca,), (cb,)), ((), ())), preferred_element_type=F32)


def swap(value, k):
    n = lax.axis_size("tensor")
    return lax.ppermute(value, "tensor", [(i, i ^ k) for i in range(n)])


def to_all(v):
    return lax.all_to_all(v, "dp", split_axis=0, concat_axis=0, tiled=True)


def norm_parts(v):
    center = v - jnp.mean(v, axis=-1, keepdims=True)
    scale = lax.rsqrt(jnp.mean(center * center, axis=-1, keepdims=True) + EPSILON)
    return center * scale, scale


def norm_back(grad, n, scale, gain):
    gy = grad * gain
    return scale * (
        gy - jnp.mean(gy, -1, keepdims=True) - n * jnp.mean(gy * n, -1, keepdims=True)
    )


def col_sum(v):
    return jnp.sum(v, axis=0, keepdims=True)


def scores_of(q, k, keep):
    s = dot(q, k, 1, 1) * HD**-0.5
    return jnp.where(keep, s, MASKED)


def one_image(x, keep, w, gain, shift, heads):
    n, _ = norm_parts(x.astype(F32))
    h1 = (n * gain + shift).astype(BF)
    c = heads * HD
    qkv = dot(h1, w[:, : 3 * c], 1, 0).astype(BF)
    contexts, totals = [], []
    for h in range(heads):
        q, k, v = (qkv[:, i * c + h * HD : i * c + (h + 1) * HD] for i in range(3))
        s = scores_of(q, k, keep)
        top = jnp.max(s, -1, keepdims=True)
        total = top + jnp.log(jnp.sum(jnp.exp(s - top), -1, keepdims=True))
        contexts.append(dot(jnp.exp(s - total).astype(BF), v, 1, 0).astype(BF))
        totals.append(total)
    context = jnp.concatenate(contexts, 1)
    return qkv, context, jnp.concatenate(totals, 1), dot(context, w[:, 3 * c :], 1, 1)


def attn_fwd_kernel(heads, xa, xb, ka, kb, w_ref, gains, pa, pb, qa, qb, ca, cb, la, lb):
    w = w_ref[...]
    gain, shift = gains[0:1], gains[1:2]
    for x, k, p, q, c, total in ((xa, ka, pa, qa, ca, la), (xb, kb, pb, qb, cb, lb)):
        qkv, context, lse, part = one_image(x[0], k[0] > 0, w, gain, shift, heads)
        q[0], c[0], total[0], p[0] = qkv, context, lse, part.astype(p.dtype)


def whole(shape):
    return pl.BlockSpec(shape, lambda *i: (0,) * len(shape))


def each(shape):
    return pl.BlockSpec((1,) + shape, lambda i: (i,) + (0,) * len(shape))


def params(vmem):
    return pltpu.CompilerParams(vmem_limit_bytes=vmem * MIB)


def attn_fwd(xa, xb, ka, kb, w, gains, heads):
    images, rows, width = xa.shape
    c = heads * HD
    one = lambda shape, dtype: jax.ShapeDtypeStruct((images,) + shape, dtype)
    kinds = [((rows, 3 * c), BF), ((rows, c), BF), ((rows, heads), F32)]
    outs = [((rows, width), BF), ((rows, width), F32)] + [k for k in kinds for _ in range(2)]
    return pl.pallas_call(
        functools.partial(attn_fwd_kernel, heads),
        grid=(images,),
        in_specs=[each((rows, width))] * 2 + [each((1, rows))] * 2 + [whole(w.shape), whole(gains.shape)],
        out_specs=[each(s) for s, _ in outs],
        out_shape=[one(s, d) for s, d in outs],
        compiler_params=params(32),
        cost_estimate=pl.CostEstimate(
            flops=4 * images * rows * width * width, bytes_accessed=8 * images * rows * width, transcendentals=0
        ),
    )(xa, xb, ka, kb, w, gains)


def one_image_back(x, ga, qkv, context, lse, keep, w, gain, shift, heads):
    n, _ = norm_parts(x.astype(F32))
    h1 = (n * gain + shift).astype(BF)
    c = heads * HD
    gc_all = dot(ga, w[:, 3 * c :], 1, 0).astype(BF)
    parts = [[], [], []]
    for h in range(heads):
        q, k, v = (qkv[:, i * c + h * HD : i * c + (h + 1) * HD] for i in range(3))
        gc = gc_all[:, h * HD : (h + 1) * HD]
        p = jnp.exp(scores_of(q, k, keep) - lse[:, h : h + 1])
        gv = dot(p.astype(BF), gc, 0, 0)
        gp = dot(gc, v, 1, 1)
        delta = jnp.sum(p * gp, -1, keepdims=True)
        gs = (p * (gp - delta)).astype(BF)
        parts[0].append((dot(gs, k, 1, 0) * HD**-0.5).astype(BF))
        parts[1].append((dot(gs, q, 0, 0) * HD**-0.5).astype(BF))
        parts[2].append(gv.astype(BF))
    gqkv = jnp.concatenate(parts[0] + parts[1] + parts[2], 1)
    gh1 = dot(gqkv, w[:, : 3 * c], 1, 1)
    dw = jnp.concatenate([dot(h1, gqkv, 0, 0), dot(ga, context, 0, 0)], 1)
    return gh1, dw, col_sum(gh1 * n), col_sum(gh1)


def attn_bwd_kernel(heads, xa, xb, ga, gb, qa, qb, ca, cb, la, lb, ka, kb, w_ref, gains, dw_in, vec_in, ha, hb, dw, vec):
    @pl.when(pl.program_id(0) == 0)
    def _():
        dw[...] = dw_in[...]
        vec[...] = vec_in[...]

    w = w_ref[...]
    gain, shift = gains[0:1], gains[1:2]
    for x, g, q, c, total, k, out in ((xa, ga, qa, ca, la, ka, ha), (xb, gb, qb, cb, lb, kb, hb)):
        gh1, part, gg, gs = one_image_back(x[0], g[0], q[0], c[0], total[0], k[0] > 0, w, gain, shift, heads)
        out[0] = gh1.astype(out.dtype)
        dw[...] += part
        vec[0:1] += gg
        vec[1:2] += gs


def attn_bwd(xa, xb, ga, gb, qa, qb, ca, cb, la, lb, ka, kb, w, gains, dw, vec, heads, out_types):
    images, rows, width = xa.shape
    c = heads * HD
    specs = [each((rows, k)) for k in (width, width, 3 * c, c, heads) for _ in range(2)] + [each((1, rows))] * 2
    return pl.pallas_call(
        functools.partial(attn_bwd_kernel, heads),
        grid=(images,),
        in_specs=specs + [whole(v.shape) for v in (w, gains, dw, vec)],
        out_specs=[each((rows, width))] * 2 + [whole(dw.shape), whole(vec.shape)],
        out_shape=[jax.ShapeDtypeStruct(xa.shape, t) for t in out_types]
        + [jax.ShapeDtypeStruct(v.shape, F32) for v in (dw, vec)],
        compiler_params=params(40),
        cost_estimate=pl.CostEstimate(
            flops=10 * images * rows * width * width, bytes_accessed=16 * images * rows * width, transcendentals=0
        ),
    )(xa, xb, ga, gb, qa, qb, ca, cb, la, lb, ka, kb, w, gains, dw, vec)


def chosen(slot_row, slots):
    at = lax.broadcasted_iota(jnp.int32, (slots, slot_row.shape[1]), 0)
    return jnp.where(slot_row == at, 1.0, 0.0).astype(BF)


def dispatch_kernel(slots, x, p0, r1, r2, gains, router, slot, residual, probs, sent):
    res = x[...].astype(F32) + p0[...] + r1[...].astype(F32) + r2[...].astype(F32)
    residual[...] = res
    n, _ = norm_parts(res)
    h2 = (n * gains[2:3] + gains[3:4]).astype(BF)
    logits = dot(h2, router[...], 1, 1)
    grown = jnp.exp(logits - jnp.max(logits, -1, keepdims=True))
    probs[...] = grown / jnp.sum(grown, -1, keepdims=True)
    for e in range(slot.shape[0]):
        sent[e * slots : (e + 1) * slots] = dot(chosen(slot[e : e + 1], slots), h2, 1, 0).astype(BF)


def picks(place, total):
    at = lax.broadcasted_iota(jnp.int32, (place.shape[0], total), 1)
    return jnp.where(place == at, 1.0, 0.0)


def combine_kernel(slots, back, place, ids, probs_in, residual, teacher, mask, factor, slot, out, g_out, gl_out, loss, sent):
    probs = probs_in[...]
    experts = probs.shape[1]
    at = lax.broadcasted_iota(jnp.int32, probs.shape, 1)
    choose = [jnp.where(ids[:, j : j + 1] == at, 1.0, 0.0) for j in range(ids.shape[1])]
    gates = [jnp.sum(c * probs, -1, keepdims=True) for c in choose]
    picked = [dot(picks(place[:, j : j + 1], back.shape[0]).astype(BF), back[...], 1, 0) for j in range(len(gates))]
    result = residual[...]
    result = result + sum(gate * p for gate, p in zip(gates, picked))
    out[...] = result.astype(BF)
    errors = result - teacher[...].astype(F32)
    m = mask[...]
    row_loss = jnp.mean(errors * errors, -1, keepdims=True) * m
    loss[...] = jnp.broadcast_to(col_sum(row_loss), loss.shape)
    g = m * errors * factor[0:1, 0:1]
    g_out[...] = g
    grad_probs = sum(c * jnp.sum(g * p, -1, keepdims=True) for c, p in zip(choose, picked))
    grad_logits = probs * (grad_probs - jnp.sum(probs * grad_probs, -1, keepdims=True))
    gl_out[...] = grad_logits.astype(BF)
    for e in range(experts):
        gated = (probs[:, e : e + 1] * g).astype(BF)
        sent[e * slots : (e + 1) * slots] = dot(chosen(slot[e : e + 1], slots), gated, 1, 0).astype(BF)


def back_kernel(back, place, residual, g, gl, gains, router, grad_residual, grad_attn, vec, grad_router):
    either = sum(picks(place[:, j : j + 1], back.shape[0]) for j in range(place.shape[1])).astype(BF)
    grad_h2 = dot(either, back[...], 1, 0) + dot(gl[...], router[...], 1, 0)
    n, scale = norm_parts(residual[...])
    gain = gains[2:3]
    h2 = (n * gain + gains[3:4]).astype(BF)
    vec[0:1] = col_sum(grad_h2 * n)
    vec[1:2] = col_sum(grad_h2)
    grad_router[...] = dot(gl[...], h2, 0, 0)
    total = g[...] + norm_back(grad_h2, n, scale, gain)
    grad_residual[...] = total
    grad_attn[...] = total.astype(BF)


def last_kernel(x, p0, r1, r2, gains, grad_residual, out):
    grad_h1 = p0[...] + r1[...].astype(F32) + r2[...].astype(F32)
    n, scale = norm_parts(x[...].astype(F32))
    out[...] = grad_residual[...] + norm_back(grad_h1, n, scale, gains[0:1])


def plain(kernel, outs, *args, vmem=32, flops=1 << 30):
    return pl.pallas_call(
        kernel,
        out_shape=[jax.ShapeDtypeStruct(s, d) for s, d in outs],
        compiler_params=params(vmem),
        cost_estimate=pl.CostEstimate(flops=flops, bytes_accessed=8 * MIB, transcendentals=0),
    )(*args)


TAIL_AT = 0.33 * 0.7071067811865476
TAIL = (
    -0.06767145544290543,
    0.23011283576488495,
    -0.17556501924991608,
    0.20424090325832367,
    0.02361520379781723,
    0.10061042755842209,
    0.09147822111845016,
    0.0931788831949234,
)


def gelu_parts(u):
    bell = jnp.exp2(u * u * (-0.5 * LOG2E))
    t = 1.0 / (1.0 + TAIL_AT * jnp.abs(u))
    poly = TAIL[0]
    for c in TAIL[1:]:
        poly = poly * t + c
    tail = t * poly * bell
    phi = jnp.where(u < 0, tail, 1.0 - tail)
    return u * phi, phi + u * bell * 0.3989422804014327


def expert_fwd_kernel(n, x, *refs):
    ups, downs, (out, hidden, slope) = refs[:n], refs[n : 2 * n], refs[2 * n :]
    total = None
    f = ups[0].shape[1]
    for t in range(n):
        value, der = gelu_parts(dot(x[...], ups[t][...], 1, 0))
        value = value.astype(BF)
        hidden[:, t * f : (t + 1) * f] = value
        slope[:, t * f : (t + 1) * f] = der.astype(BF)
        part = dot(value, downs[t][...], 1, 1)
        total = part if total is None else total + part
    out[...] = total.astype(BF)


def expert_bwd_kernel(n, go, slope, *refs):
    ups, downs, (grad_up, out) = refs[:n], refs[n : 2 * n], refs[2 * n :]
    total = None
    f = ups[0].shape[1]
    for t in range(n):
        at = slice(t * f, (t + 1) * f)
        gu = (dot(go[...], downs[t][...], 1, 0) * slope[:, at].astype(F32)).astype(BF)
        grad_up[:, at] = gu
        part = dot(gu, ups[t][...], 1, 1)
        total = part if total is None else total + part
    out[...] = total.astype(BF)


def over_rows(kernel, ins, weights, widths, step):
    rows = ins[0].shape[0]
    block = lambda k: pl.BlockSpec((step, k), lambda i: (i, 0))
    fixed = lambda s: pl.BlockSpec(s, lambda i: (0, 0), pipeline_mode=pl.Buffered(1))
    return pl.pallas_call(
        kernel,
        grid=(rows // step,),
        in_specs=[block(v.shape[1]) for v in ins] + [fixed(w.shape) for w in weights],
        out_specs=[block(k) for k in widths],
        out_shape=[jax.ShapeDtypeStruct((rows, k), BF) for k in widths],
        compiler_params=params(48),
        cost_estimate=pl.CostEstimate(
            flops=2 * rows * sum(w.size for w in weights), bytes_accessed=32 * MIB, transcendentals=0
        ),
    )(*ins, *weights)


def after(value, *others):
    return lax.optimization_barrier((value,) + others)[0]


def local(
    tokens,
    teacher,
    valid_mask,
    expert_ids,
    attn_gain,
    attn_shift,
    qkv_weight,
    proj_weight,
    moe_gain,
    moe_shift,
    router_weight,
    up_weight,
    down_weight,
):
    rows, width = tokens.shape
    length = valid_mask.shape[1]
    images = rows // length
    experts = router_weight.shape[1]
    top = expert_ids.shape[1]
    capacity = max(2, (top * rows + experts - 1) // experts * 5 // 4)
    slots = -(-capacity // 16) * 16
    padded = -(-length // 16) * 16
    own = images * padded
    n_dp = lax.axis_size("dp")
    n_tensor = lax.axis_size("tensor")
    tensor_me = lax.axis_index("tensor")
    heads_width = proj_weight.shape[1]
    heads = heads_width // HD

    def pad(v, value=0):
        v = v.reshape((images, length) + v.shape[1:])
        return jnp.pad(v, ((0, 0), (0, padded - length)) + ((0, 0),) * (v.ndim - 2), constant_values=value)

    def unpad(v):
        return v.reshape(images, padded, -1)[:, :length].reshape(rows, -1)

    x0 = pad(tokens)
    x1 = swap(x0, 1)
    x2 = swap(x0, 2)
    x3 = swap(x2, 1)
    x = (x0, x1, x2, x3)

    dense_rows = proj_weight.shape[0]
    valid_here = jnp.sum(valid_mask)
    count_parts = jnp.stack([valid_here // 128, valid_here % 128]).astype(BF)
    vectors = jnp.concatenate([attn_gain, attn_shift, moe_gain, moe_shift, count_parts])
    extra = jnp.concatenate([jnp.pad(vectors, (0, width - vectors.size)), router_weight.T.reshape(-1)])
    shard = jnp.concatenate(
        [jnp.concatenate([qkv_weight.reshape(-1, 3 * heads_width), proj_weight], 1), extra.reshape(-1, width)], 0
    )
    got = to_all(jnp.broadcast_to(shard[None], (n_dp,) + shard.shape))
    w = got[:, :dense_rows].reshape(width, width)
    extras = got[:, dense_rows]
    gains = extras[:, : 4 * dense_rows].reshape(n_dp, 4, dense_rows).swapaxes(0, 1).reshape(4, width).astype(F32)
    counts = jnp.sum(extras[:, 4 * dense_rows : 4 * dense_rows + 2].astype(F32), 0)
    count = counts[0] * 128 + counts[1]
    router = got[:, dense_rows + 1].reshape(n_dp, experts, dense_rows).swapaxes(0, 1).reshape(experts, width)

    up0, down0 = after((up_weight[0], down_weight[0]), x2)
    up2 = swap(up0, 2)
    down2 = swap(after(down0, up2), 2)
    ups = (up0, swap(up0, 1), up2, swap(up2, 1))
    downs = (down0, swap(down0, 1), down2, swap(down2, 1))

    mask = jnp.pad(valid_mask, ((0, 0), (0, padded - length))).reshape(n_tensor, images, 1, padded)
    masks = [lax.dynamic_index_in_dim(mask, tensor_me ^ k, 0, keepdims=False) for k in range(4)]
    row_mask = masks[0].reshape(own, 1).astype(F32)
    ids = pad(expert_ids, -1).reshape(own, top)
    each_expert = lax.iota(jnp.int32, experts)
    named = ids[:, :, None] == each_expert
    names = jnp.any(named, axis=1)
    row_at = lax.iota(jnp.int32, own)
    before = (row_at[:, None] > row_at[None, :]).astype(BF)
    slot = jnp.where(names, dot(before, names.astype(BF), 1, 0).astype(jnp.int32), -1)
    place = jnp.where(ids < 0, -1, ids * slots + jnp.sum(jnp.where(named, slot[:, None, :], 0), -1))
    slot = slot.T

    p3, p2, q3, q2, c3, c2, l3, l2 = attn_fwd(x3, x2, masks[3], masks[2], w, gains, heads)
    far = (p2 + swap(p3, 1).astype(F32)).astype(BF)
    r2 = swap(far, 2)
    p1, p0, q1, q0, c1, c0, l1, l0 = attn_fwd(x1, x0, masks[1], masks[0], w, gains, heads)
    r1 = swap(p1, 1)
    flat = lambda v: v.reshape(own, v.shape[-1])
    row_f32 = ((own, width), F32)
    row_bf = ((own, width), BF)
    all_slots = ((experts * slots, width), BF)
    residual, probs, sent = plain(
        functools.partial(dispatch_kernel, slots),
        [row_f32, ((own, experts), F32), all_slots],
        *(flat(x0), flat(p0), flat(r1), flat(r2), gains, router, slot),
    )

    exchange = lambda v: to_all(v.reshape(n_dp, slots, width)).reshape(n_dp * slots, width)
    arrived = exchange(sent)
    step = min(256, n_dp * slots)
    hidden_width = n_tensor * up0.shape[1]
    out, hidden, slope = over_rows(
        functools.partial(expert_fwd_kernel, n_tensor), (arrived,), ups + downs, (width, hidden_width, hidden_width), step
    )
    returned = exchange(out)
    factor = jnp.full((1, 128), rows * n_dp * n_tensor / count, F32)
    result, g, grad_logits, loss_part, grad_sent = plain(
        functools.partial(combine_kernel, slots),
        [row_bf, row_f32, ((own, experts), BF), ((1, 128), F32), all_slots],
        *(returned, place, ids, probs, residual, flat(pad(teacher)), row_mask, factor, slot),
    )
    grad_out = exchange(grad_sent)
    grad_up, grad_arrived = over_rows(
        functools.partial(expert_bwd_kernel, n_tensor), (grad_out, slope), ups + downs, (hidden_width, width), step
    )
    grad_back = exchange(grad_arrived)

    f = up0.shape[1]
    cut = lambda v, t: v[:, t * f : (t + 1) * f]

    def expert_sums(part):
        kept2 = part(2) + swap(part(3).astype(BF), 1).astype(F32)
        own_part = part(0) + swap(part(1).astype(BF), 1).astype(F32)
        return own_part, kept2.astype(BF)

    down_own, down_far = expert_sums(lambda t: dot(grad_out, cut(hidden, t), 0, 0))
    up_own, up_far = expert_sums(lambda t: dot(arrived, cut(grad_up, t), 0, 0))

    grad_residual, grad_attn, vec_two, grad_router = plain(
        back_kernel,
        [row_f32, row_bf, ((2, width), F32), ((experts, width), F32)],
        *(grad_back, place, residual, g, grad_logits, gains, router),
    )

    g0 = grad_attn.reshape(x0.shape)
    g1 = swap(g0, 1)
    g2 = swap(g0, 2)
    g3 = swap(g2, 1)
    grad_down_w = down_own + swap(down_far, 2).astype(F32)
    grad_up_w = up_own + swap(after(up_far, g2), 2).astype(F32)
    dw = jnp.zeros(w.shape, F32)
    vec_one = jnp.zeros((2, width), F32)
    h1, h0, dw, vec_one = attn_bwd(
        *(x1, x0, g1, g0, q1, q0, c1, c0, l1, l0, masks[1], masks[0], w, gains, dw, vec_one, heads, (BF, F32))
    )
    h3, h2, dw, vec_one = attn_bwd(
        *(x3, x2, g3, g2, q3, q2, c3, c2, l3, l2, masks[3], masks[2], w, gains, dw, vec_one, heads, (BF, F32))
    )
    t1 = swap(h1, 1)
    t2 = swap((h2 + swap(h3, 1).astype(F32)).astype(BF), 2)
    dense = to_all(dw.astype(BF).reshape(n_dp, dense_rows, width)).astype(F32).sum(0)
    [grad_tokens] = plain(
        last_kernel, [row_f32], *(flat(x0), flat(h0), flat(t1), flat(t2), gains, grad_residual)
    )

    small = jnp.concatenate([vec_one, vec_two, grad_router]).reshape(4 + experts, n_dp, dense_rows).swapaxes(0, 1)
    small = small.reshape(n_dp, -1)
    small = jnp.concatenate([small, jnp.broadcast_to(loss_part[:, :1], (n_dp, 1))], 1)
    size = small.shape[1]
    lanes = -(-size // 1024) * 1024
    small = jnp.pad(small, ((0, 0), (0, lanes - size))).reshape(n_dp, lanes // 128, 128)
    small = to_all(small).sum(0)
    small = small + swap(small, 1)
    small = (small + swap(small, 2)).reshape(-1)
    loss = small[size - 1] / count
    small = small[: size - 1].reshape(4 + experts, dense_rows)
    return (
        loss,
        unpad(result),
        unpad(grad_tokens),
        small[0],
        small[1],
        dense[:, : 3 * heads_width].reshape(-1, 3, heads_width),
        dense[:, 3 * heads_width :],
        small[2],
        small[3],
        small[4:].T,
        grad_up_w[None],
        grad_down_w[None],
    )


def solution(mesh):
    rows = P(("dp", "tensor"), None)
    experts = P("dp", None, "tensor")
    in_specs = (
        rows,
        rows,
        P("dp", None),
        rows,
        P("dp"),
        P("dp"),
        experts,
        P("dp", "tensor"),
        P("dp"),
        P("dp"),
        P("dp", None),
        experts,
        experts,
    )
    out_specs = (
        P(),
        rows,
        rows,
        P("dp"),
        P("dp"),
        experts,
        P("dp", "tensor"),
        P("dp"),
        P("dp"),
        P("dp", None),
        experts,
        experts,
    )
    return jax.shard_map(local, mesh=mesh, in_specs=in_specs, out_specs=out_specs, check_vma=False)
```

```python
import functools
import jax
import jax.numpy as jnp
from jax import lax
from jax.experimental import pallas as pl
from jax.experimental.pallas import tpu as pltpu
from jax.sharding import PartitionSpec as P

HD = 64
EPSILON = 1e-06
MASKED = -1000000000.0
BF = jnp.bfloat16
F32 = jnp.float32
LOG2E = 1.4426950408889634
MIB = 1 << 20
PLAIN = 10


def dot(a, b, ca, cb):
    return lax.dot_general(a, b, (((ca,), (cb,)), ((), ())), preferred_element_type=F32)


def swap(value, k):
    n = lax.axis_size("tensor")
    return lax.ppermute(value, "tensor", [(i, i ^ k) for i in range(n)])


def to_all(v):
    return lax.all_to_all(v, "dp", split_axis=0, concat_axis=0, tiled=True)


def norm_parts(v):
    center = v - jnp.mean(v, axis=-1, keepdims=True)
    scale = lax.rsqrt(jnp.mean(center * center, axis=-1, keepdims=True) + EPSILON)
    return center * scale, scale


def norm_back(grad, n, scale, gain):
    gy = grad * gain
    return scale * (
        gy - jnp.mean(gy, -1, keepdims=True) - n * jnp.mean(gy * n, -1, keepdims=True)
    )


def col_sum(v):
    return jnp.sum(v, axis=0, keepdims=True)


def scores_of(q, k, keep):
    s = dot(q, k, 1, 1) * HD**-0.5
    return jnp.where(keep, s, MASKED)


def one_image(x, keep, w, gain, shift, heads):
    n, _ = norm_parts(x.astype(F32))
    h1 = (n * gain + shift).astype(BF)
    c = heads * HD
    qkv = dot(h1, w[:, : 3 * c], 1, 0).astype(BF)
    contexts, totals = [], []
    for h in range(heads):
        q, k, v = (qkv[:, i * c + h * HD : i * c + (h + 1) * HD] for i in range(3))
        s = scores_of(q, k, keep)
        top = jnp.max(s, -1, keepdims=True)
        total = top + jnp.log(jnp.sum(jnp.exp(s - top), -1, keepdims=True))
        contexts.append(dot(jnp.exp(s - total).astype(BF), v, 1, 0).astype(BF))
        totals.append(total)
    context = jnp.concatenate(contexts, 1)
    return qkv, context, jnp.concatenate(totals, 1), dot(context, w[:, 3 * c :], 1, 1)


def attn_fwd_kernel(heads, n, *refs):
    xs, keeps, (w_ref, gains), outs = refs[:n], refs[n : 2 * n], refs[2 * n : 2 * n + 2], refs[2 * n + 2 :]
    w = w_ref[...]
    gain, shift = gains[0:1], gains[1:2]
    for i in range(n):
        values = one_image(xs[i][0], keeps[i][0] > 0, w, gain, shift, heads)
        for out, value in zip(outs[4 * i : 4 * i + 4], values):
            out[0] = value.astype(out.dtype)


CHEAP = pl.CostEstimate(flops=1 << 20, bytes_accessed=1 << 10, transcendentals=0)
NEAR = pl.CostEstimate(flops=1 << 28, bytes_accessed=8 * MIB, transcendentals=0)
ALL = 58


def whole(shape):
    return pl.BlockSpec(shape, lambda *i: (0,) * len(shape))


def each(shape):
    return pl.BlockSpec((1,) + shape, lambda i: (i,) + (0,) * len(shape))


def params(vmem):
    return pltpu.CompilerParams(vmem_limit_bytes=vmem * MIB)


def attn_fwd(xs, keeps, part_types, w, gains, heads):
    images, rows, width = xs[0].shape
    c = heads * HD
    outs = []
    for part_type in part_types:
        outs += [((rows, 3 * c), BF), ((rows, c), BF), ((rows, heads), F32), ((rows, width), part_type)]
    made = pl.pallas_call(
        functools.partial(attn_fwd_kernel, heads, len(xs)),
        grid=(images,),
        in_specs=[each((rows, width)) for _ in xs] + [each((1, rows)) for _ in xs] + [whole(w.shape), whole(gains.shape)],
        out_specs=[each(s) for s, _ in outs],
        out_shape=[jax.ShapeDtypeStruct((images,) + s, d) for s, d in outs],
        compiler_params=params(ALL),
        cost_estimate=CHEAP,
    )(*xs, *keeps, w, gains)
    return [made[4 * i : 4 * i + 4] for i in range(len(xs))]


def one_image_back(x, ga, qkv, context, lse, keep, w, gain, shift, heads):
    n, _ = norm_parts(x.astype(F32))
    h1 = (n * gain + shift).astype(BF)
    c = heads * HD
    gc_all = dot(ga, w[:, 3 * c :], 1, 0).astype(BF)
    parts = [[], [], []]
    for h in range(heads):
        q, k, v = (qkv[:, i * c + h * HD : i * c + (h + 1) * HD] for i in range(3))
        gc = gc_all[:, h * HD : (h + 1) * HD]
        p = jnp.exp(scores_of(q, k, keep) - lse[:, h : h + 1])
        gv = dot(p.astype(BF), gc, 0, 0)
        gp = dot(gc, v, 1, 1)
        delta = jnp.sum(p * gp, -1, keepdims=True)
        gs = (p * (gp - delta)).astype(BF)
        parts[0].append((dot(gs, k, 1, 0) * HD**-0.5).astype(BF))
        parts[1].append((dot(gs, q, 0, 0) * HD**-0.5).astype(BF))
        parts[2].append(gv.astype(BF))
    gqkv = jnp.concatenate(parts[0] + parts[1] + parts[2], 1)
    gh1 = dot(gqkv, w[:, : 3 * c], 1, 1)
    return gh1, h1, gqkv, col_sum(gh1 * n), col_sum(gh1)


def split_float(v):
    high = v.astype(BF)
    return high, (v - high.astype(F32)).astype(BF)


def attn_bwd_kernel(heads, xa, xb, ga, gb, qa, qb, ca, cb, la, lb, ka, kb, w_ref, gains, *refs):
    others, (ha, hb, dw_out, vec, h_all, q_all, g_all, c_all) = refs[:-8], refs[-8:]

    @pl.when(pl.program_id(0) == 0)
    def _():
        vec[...] = others[1][...] if others else jnp.zeros_like(vec)

    w = w_ref[...]
    gain, shift = gains[0:1], gains[1:2]
    length = xa.shape[1]
    groups = ((xa, ga, qa, ca, la, ka, ha), (xb, gb, qb, cb, lb, kb, hb))
    for i, (x, g, q, c, total, k, out) in enumerate(groups):
        gh1, h1, gqkv, gg, gs = one_image_back(x[0], g[0], q[0], c[0], total[0], k[0] > 0, w, gain, shift, heads)
        out[0] = gh1.astype(out.dtype)
        at = pl.ds(pl.multiple_of((2 * pl.program_id(0) + i) * length, length), length)
        h_all[at], q_all[at], g_all[at], c_all[at] = h1, gqkv, g[0], c[0]
        vec[0:1] += gg
        vec[1:2] += gs

    @pl.when(pl.program_id(0) == pl.num_programs(0) - 1)
    def _():
        dw = jnp.concatenate([dot(h_all[...], q_all[...], 0, 0), dot(g_all[...], c_all[...], 0, 0)], 1)
        if others:
            dw = dw + others[0][...]
        if not others:
            dw_out[...] = dw
        else:
            rows = dw.shape[0] // dw_out.shape[0]
            vec_two, router, loss = others[2:]
            experts, width = router.shape
            rest = jnp.zeros((experts - 5, width), F32)
            named = jnp.concatenate([vec[...], vec_two[...], loss[...], rest], 0)
            pieces = [p.astype(F32) for v in (router[...], named) for p in split_float(v)]
            for k in range(dw_out.shape[0]):
                at = slice(k * rows, (k + 1) * rows)
                last = jnp.concatenate([p[:, at] for p in pieces] + [jnp.zeros((experts, width - 4 * rows), F32)], 1)
                dw_out[k] = jnp.concatenate([dw[at], last], 0).astype(BF)


def attn_bwd(xa, xb, ga, gb, qa, qb, ca, cb, la, lb, ka, kb, w, gains, others, heads, pack):
    images, rows, width = xa.shape
    c = heads * HD
    vec_shape = (2, width)
    specs = [each((rows, k)) for k in (width, width, 3 * c, c, heads) for _ in range(2)] + [each((1, rows))] * 2
    return pl.pallas_call(
        functools.partial(attn_bwd_kernel, heads),
        grid=(images,),
        in_specs=specs + [whole(v.shape) for v in (w, gains) + others],
        out_specs=[each((rows, width))] * 2 + [whole(pack[0] if pack else w.shape), whole(vec_shape)],
        out_shape=[jax.ShapeDtypeStruct(xa.shape, t) for t in (BF, F32)]
        + [jax.ShapeDtypeStruct(*(pack or (w.shape, F32))), jax.ShapeDtypeStruct(vec_shape, F32)],
        scratch_shapes=[pltpu.VMEM((2 * images * rows, k), BF) for k in (width, 3 * c, width, c)],
        compiler_params=params(ALL),
        cost_estimate=NEAR,
    )(xa, xb, ga, gb, qa, qb, ca, cb, la, lb, ka, kb, w, gains, *others)


def chosen(slot_row, slots):
    at = lax.broadcasted_iota(jnp.int32, (slots, slot_row.shape[1]), 0)
    return jnp.where(slot_row == at, 1.0, 0.0).astype(BF)


def dispatch_kernel(slots, x, p0, r1, r2, gains, router, slot, residual, probs, sent):
    res = x[...].astype(F32) + p0[...] + r1[...].astype(F32) + r2[...].astype(F32)
    residual[...] = res
    n, _ = norm_parts(res)
    h2 = (n * gains[2:3] + gains[3:4]).astype(BF)
    logits = dot(h2, router[...], 1, 1)
    grown = jnp.exp(logits - jnp.max(logits, -1, keepdims=True))
    probs[...] = grown / jnp.sum(grown, -1, keepdims=True)
    for e in range(slot.shape[0]):
        at = slice(e * slots, (e + 1) * slots)
        sent[at] = dot(chosen(slot[e : e + 1], slots), h2, 1, 0).astype(BF)


def picks(place, total):
    at = lax.broadcasted_iota(jnp.int32, (place.shape[0], total), 1)
    return jnp.where(place == at, 1.0, 0.0)


def combine_kernel(slots, back, place, ids, probs_in, residual, teacher, mask, factor, slot, out, g_out, gl_out, loss, sent):
    probs = probs_in[...]
    experts = probs.shape[1]
    at = lax.broadcasted_iota(jnp.int32, probs.shape, 1)
    choose = [jnp.where(ids[:, j : j + 1] == at, 1.0, 0.0) for j in range(ids.shape[1])]
    gates = [jnp.sum(c * probs, -1, keepdims=True) for c in choose]
    picked = [dot(picks(place[:, j : j + 1], back.shape[0]).astype(BF), back[...], 1, 0) for j in range(len(gates))]
    result = residual[...]
    result = result + sum(gate * p for gate, p in zip(gates, picked))
    out[...] = result.astype(BF)
    errors = result - teacher[...].astype(F32)
    m = mask[...]
    row_loss = jnp.mean(errors * errors, -1, keepdims=True) * m
    loss[...] = jnp.broadcast_to(col_sum(row_loss), loss.shape)
    g = m * errors * factor[0:1, 0:1]
    g_out[...] = g
    grad_probs = sum(c * jnp.sum(g * p, -1, keepdims=True) for c, p in zip(choose, picked))
    grad_logits = probs * (grad_probs - jnp.sum(probs * grad_probs, -1, keepdims=True))
    gl_out[...] = grad_logits.astype(BF)
    for e in range(experts):
        at = slice(e * slots, (e + 1) * slots)
        gated = (probs[:, e : e + 1] * g).astype(BF)
        sent[at] = dot(chosen(slot[e : e + 1], slots), gated, 1, 0).astype(BF)


def back_kernel(back, place, residual, g, gl, gains, router, grad_residual, grad_attn, vec, grad_router):
    either = sum(picks(place[:, j : j + 1], back.shape[0]) for j in range(place.shape[1])).astype(BF)
    grad_h2 = dot(either, back[...], 1, 0) + dot(gl[...], router[...], 1, 0)
    n, scale = norm_parts(residual[...])
    gain = gains[2:3]
    h2 = (n * gain + gains[3:4]).astype(BF)
    vec[0:1] = col_sum(grad_h2 * n)
    vec[1:2] = col_sum(grad_h2)
    grad_router[...] = dot(gl[...], h2, 0, 0)
    total = g[...] + norm_back(grad_h2, n, scale, gain)
    grad_residual[...] = total
    grad_attn[...] = total.astype(BF)


def last_kernel(images, x, p0, r1, r2, gains, grad_residual, out):
    grad_h1 = p0[...] + r1[...].astype(F32) + r2[...].astype(F32)
    n, scale = norm_parts(x[...].astype(F32))
    total = grad_residual[...] + norm_back(grad_h1, n, scale, gains[0:1])
    padded, length = x.shape[0] // images, out.shape[0] // images
    for i in range(images):
        out[i * length : (i + 1) * length] = total[i * padded : i * padded + length]


def plain(kernel, outs, *args):
    return pl.pallas_call(
        kernel,
        grid=(1,),
        in_specs=[whole(v.shape) for v in args],
        out_specs=[whole(s) for s, _ in outs],
        out_shape=[jax.ShapeDtypeStruct(s, d) for s, d in outs],
        compiler_params=params(ALL),
        cost_estimate=CHEAP,
    )(*args)


class Copies:
    def __init__(self, sems):
        self.sems, self.made = sems, []

    def start(self, source, target):
        copy = pltpu.make_async_copy(source, target, self.sems.at[len(self.made)])
        copy.start()
        self.made.append(copy)
        return copy


def dense_kernel(parts, qkv, proj, small):
    total = parts[0].astype(F32)
    for k in range(1, parts.shape[0]):
        total = total + parts[k].astype(F32)
    rows, c = proj.shape
    for i in range(3):
        qkv[:, i, :] = total[:rows, i * c : (i + 1) * c]
    proj[...] = total[:rows, 3 * c :]
    last = total[rows:]
    piece = lambda i: last[:, i * rows : (i + 1) * rows]
    small[...] = jnp.concatenate([piece(0) + piece(1), piece(2) + piece(3)], 0)


def shard_kernel(qkv, proj, g1, s1, g2, s2, router, mask, out, block, sems):
    weights = jnp.concatenate([qkv[:, i, :] for i in range(3)] + [proj[...]], 1)
    rows, width = weights.shape
    count = jnp.sum(jnp.sum(mask[...].astype(F32), 1, keepdims=True), 0, keepdims=True)
    high = jnp.floor(count / 128)
    vectors = [v[...].astype(F32) for v in (g1, s1, g2, s2)] + [high, count - 128 * high]
    vectors.append(jnp.zeros((1, width - 4 * rows - 2), F32))
    at = [lax.broadcasted_iota(jnp.int32, (rows, rows), i) for i in (0, 1)]
    turned = dot(router[...], jnp.where(at[0] == at[1], 1.0, 0.0).astype(BF), 0, 0)
    last = jnp.concatenate([turned[e : e + 1] for e in range(turned.shape[0])], 1)
    extra = jnp.concatenate([jnp.concatenate(vectors, 1), last], 0)
    block[...] = jnp.concatenate([weights, extra.astype(BF)], 0)
    copies = Copies(sems)
    for k in range(out.shape[0]):
        copies.start(block, out.at[k])
    for copy in copies.made:
        copy.wait()


def gelu_parts(u):
    phi = 0.5 * lax.erf(u * 0.7071067811865476) + 0.5
    bell = jnp.exp2(u * u * (-0.5 * LOG2E))
    return u * phi, phi + u * bell * 0.3989422804014327


def side_by_side(refs):
    return jnp.concatenate([r[...] for r in refs], 1)


def over_chunks(rows, step, body):
    def one(i, carry):
        body(pl.ds(pl.multiple_of(i * step, step), step))
        return carry

    lax.fori_loop(0, rows // step, one, 0)


def expert_fwd_kernel(n, step, x, *refs):
    ups, downs, (out, hidden, slope) = refs[:n], refs[n : 2 * n], refs[2 * n : 2 * n + 3]
    wu, wd, hs, ss, os, sems = refs[2 * n + 3 :]
    copies = Copies(sems)
    f = wu.shape[2]
    up_in = [copies.start(ups[t], wu.at[t]) for t in range(n)]
    down_in = []
    outgoing = []
    for row in range(0, x.shape[0], step):
        at = slice(row, row + step)
        for t in range(n):
            cols = slice(t * f, (t + 1) * f)
            if row == 0:
                up_in[t].wait()
                if t == 0:
                    down_in = [copies.start(downs[i], wd.at[i]) for i in range(n)]
            value, der = gelu_parts(dot(x[at], wu[t], 1, 0))
            hs[at, cols] = value.astype(BF)
            ss[at, cols] = der.astype(BF)
        outgoing.append(copies.start(hs.at[at], hidden.at[at]))
        outgoing.append(copies.start(ss.at[at], slope.at[at]))
        if row == 0:
            for copy in down_in:
                copy.wait()
        os[at] = dot(hs[at], jnp.concatenate([wd[t] for t in range(n)], 1), 1, 1).astype(BF)
        outgoing.append(copies.start(os.at[at], out.at[at]))
    for copy in outgoing:
        copy.wait()


def expert_bwd_kernel(n, step, go, slope, *refs):
    ups, downs, (grad_up, out) = refs[:n], refs[n : 2 * n], refs[2 * n : 2 * n + 2]
    wu, wd, gs, ss, os, sems = refs[2 * n + 2 :]
    copies = Copies(sems)
    f = wu.shape[2]
    rows = go.shape[0]
    chunks = [slice(row, row + step) for row in range(0, rows, step)]
    down_in = [copies.start(downs[0], wd.at[0])]
    slope_in = [copies.start(slope.at[chunks[0]], ss.at[chunks[0]])]
    up_in = []
    outgoing = []
    for i, at in enumerate(chunks):
        for t in range(n):
            cols = slice(t * f, (t + 1) * f)
            if i == 0:
                down_in[t].wait()
            if t == 0:
                slope_in[i].wait()
                if i == 0:
                    down_in += [copies.start(downs[j], wd.at[j]) for j in range(1, n)]
                    up_in = [copies.start(ups[j], wu.at[j]) for j in range(n)]
                    slope_in += [copies.start(slope.at[later], ss.at[later]) for later in chunks[1:]]
            grad_hidden = dot(go[at], wd[t], 1, 0)
            gs[at, cols] = (grad_hidden * ss[at, cols].astype(F32)).astype(BF)
        outgoing.append(copies.start(gs.at[at], grad_up.at[at]))
        if i == 0:
            for copy in up_in:
                copy.wait()
        os[at] = dot(gs[at], jnp.concatenate([wu[t] for t in range(n)], 1), 1, 1).astype(BF)
        outgoing.append(copies.start(os.at[at], out.at[at]))
    for copy in outgoing:
        copy.wait()


def expert_weights_kernel(n, rows, cols, *refs):
    outs, (rs, cs, os, sems) = refs[:n], refs[n:]
    copies = Copies(sems)
    f = os.shape[2]
    rows_in = copies.start(rows, rs)
    cols_in = [copies.start(cols.at[:, slice(t * f, (t + 1) * f)], cs.at[t]) for t in range(n)]
    rows_in.wait()
    outgoing = []
    for t in range(n):
        cols_in[t].wait()
        os[t] = dot(rs[...], cs[t], 0, 0).astype(BF)
        outgoing.append(copies.start(os.at[t], outs[t]))
    for copy in outgoing:
        copy.wait()


IN_HBM = pl.BlockSpec(memory_space=pltpu.HBM)
IN_VMEM = pl.BlockSpec(memory_space=pltpu.VMEM)


def copying(kernel, ins, in_hbm, outs, out_hbm, scratch, copies, vmem=PLAIN):
    spec = lambda far: IN_HBM if far else IN_VMEM
    return pl.pallas_call(
        kernel,
        in_specs=[spec(far) for far in in_hbm],
        out_specs=[spec(far) for far in out_hbm],
        out_shape=[jax.ShapeDtypeStruct(s, d) for s, d in outs],
        scratch_shapes=[pltpu.VMEM(s, d) for s, d in scratch] + [pltpu.SemaphoreType.DMA((copies,))],
        compiler_params=params(vmem),
        cost_estimate=CHEAP if vmem == ALL else NEAR,
    )(*ins)


def after(value, *others):
    return lax.optimization_barrier((value,) + others)[0]


def local(
    tokens,
    teacher,
    valid_mask,
    expert_ids,
    attn_gain,
    attn_shift,
    qkv_weight,
    proj_weight,
    moe_gain,
    moe_shift,
    router_weight,
    up_weight,
    down_weight,
):
    rows, width = tokens.shape
    length = valid_mask.shape[1]
    images = rows // length
    experts = router_weight.shape[1]
    top = expert_ids.shape[1]
    capacity = max(2, (top * rows + experts - 1) // experts * 5 // 4)
    slots = -(-capacity // 16) * 16
    padded = -(-length // 16) * 16
    own = images * padded
    n_dp = lax.axis_size("dp")
    n_tensor = lax.axis_size("tensor")
    tensor_me = lax.axis_index("tensor")
    heads_width = proj_weight.shape[1]
    heads = heads_width // HD

    def pad(v, value=0):
        v = v.reshape((images, length) + v.shape[1:])
        return jnp.pad(v, ((0, 0), (0, padded - length)) + ((0, 0),) * (v.ndim - 2), constant_values=value)

    def unpad(v):
        return v.reshape(images, padded, -1)[:, :length].reshape(rows, -1)

    x0 = pad(tokens)
    x1 = swap(x0, 1)
    x2 = swap(x0, 2)
    x3 = swap(x2, 1)
    x = (x0, x1, x2, x3)

    dense_rows = proj_weight.shape[0]
    row = lambda v: v.reshape(1, dense_rows)
    block = (dense_rows + 2, width)
    [shards] = copying(
        shard_kernel,
        (qkv_weight, proj_weight)
        + tuple(row(v) for v in (attn_gain, attn_shift, moe_gain, moe_shift))
        + (router_weight, valid_mask),
        (0,) * 8,
        [((n_dp,) + block, BF)],
        (1,),
        [(block, BF)],
        n_dp,
        PLAIN,
    )
    got = to_all(shards)
    w = got[:, :dense_rows].reshape(width, width)
    extras = got[:, dense_rows]
    gains = extras[:, : 4 * dense_rows].reshape(n_dp, 4, dense_rows).swapaxes(0, 1).reshape(4, width).astype(F32)
    counts = jnp.sum(extras[:, 4 * dense_rows : 4 * dense_rows + 2].astype(F32), 0)
    count = counts[0] * 128 + counts[1]
    router = got[:, dense_rows + 1].reshape(n_dp, experts, dense_rows).swapaxes(0, 1).reshape(experts, width)

    up0, down0 = up_weight[0], down_weight[0]
    part = lambda eighths: width * eighths // 8
    up2 = [swap(up0[: part(4)], 2)]

    mask = jnp.pad(valid_mask, ((0, 0), (0, padded - length))).reshape(n_tensor, images, 1, padded)
    masks = [lax.dynamic_index_in_dim(mask, tensor_me ^ k, 0, keepdims=False) for k in range(4)]
    row_mask = masks[0].reshape(own, 1).astype(F32)
    ids = pad(expert_ids, -1).reshape(own, top)
    each_expert = lax.iota(jnp.int32, experts)
    named = ids[:, :, None] == each_expert
    names = jnp.any(named, axis=1)
    row_at = lax.iota(jnp.int32, own)
    before = (row_at[:, None] > row_at[None, :]).astype(BF)
    slot = jnp.where(names, dot(before, names.astype(BF), 1, 0).astype(jnp.int32), -1)
    place = jnp.where(ids < 0, -1, ids * slots + jnp.sum(jnp.where(named, slot[:, None, :], 0), -1))
    slot = slot.T

    w, up2[0] = lax.optimization_barrier((w, up2[0]))
    (q3, c3, l3, p3), (q2, c2, l2, p2), (q1, c1, l1, p1) = attn_fwd(
        (x3, x2, x1), (masks[3], masks[2], masks[1]), (BF, F32, BF), w, gains, heads
    )
    far = (p2 + swap(p3, 1).astype(F32)).astype(BF)
    r2 = swap(far, 2)
    [(q0, c0, l0, p0)] = attn_fwd((x0,), (masks[0],), (F32,), w, gains, heads)
    r1 = swap(p1, 1)
    up2.append(swap(after(up0[part(4) :], r2), 2))
    up2 = jnp.concatenate(up2)
    ups = (up0, swap(up0, 1), up2, swap(up2, 1))
    down2 = swap(after(down0, r2), 2)
    downs = (down0, swap(down0, 1), down2, swap(down2, 1))
    flat = lambda v: v.reshape(own, v.shape[-1])
    row_f32 = ((own, width), F32)
    row_bf = ((own, width), BF)
    all_slots = ((experts * slots, width), BF)
    residual, probs, sent = plain(
        functools.partial(dispatch_kernel, slots),
        [row_f32, ((own, experts), F32), all_slots],
        *(flat(x0), flat(p0), flat(r1), flat(r2), gains, router, slot),
    )

    exchange = lambda v: to_all(v.reshape(n_dp, slots, width)).reshape(n_dp * slots, width)
    arrived = exchange(sent)
    total = n_dp * slots
    step = min(256, total)
    f = up0.shape[1]
    wide = ((total, n_tensor * f), BF)
    weights_in = [((n_tensor, width, f), BF)] * 2
    chunks = total // step
    out, hidden, slope = copying(
        functools.partial(expert_fwd_kernel, n_tensor, step),
        (arrived, *ups, *downs),
        (0,) + (1,) * (2 * n_tensor),
        [all_slots, wide, wide],
        (1, 1, 1),
        weights_in + [wide, wide, all_slots],
        2 * n_tensor + 3 * chunks,
        ALL,
    )
    returned = exchange(out)
    factor = jnp.full((1, 128), rows * n_dp * n_tensor / count, F32)
    result, g, grad_logits, loss_part, grad_sent = plain(
        functools.partial(combine_kernel, slots),
        [row_bf, row_f32, ((own, experts), BF), ((1, width), F32), all_slots],
        *(returned, place, ids, probs, residual, flat(pad(teacher)), row_mask, factor, slot),
    )
    grad_out = exchange(grad_sent)
    grad_up, grad_arrived = copying(
        functools.partial(expert_bwd_kernel, n_tensor, step),
        (grad_out, slope, *ups, *downs),
        (0, 1) + (1,) * (2 * n_tensor),
        [wide, all_slots],
        (1, 1),
        weights_in + [wide, wide, all_slots],
        2 * n_tensor + 3 * chunks,
        ALL,
    )
    grad_back = exchange(grad_arrived)

    def weight_parts(rows_in, cols_in):
        return copying(
            functools.partial(expert_weights_kernel, n_tensor),
            (rows_in, cols_in),
            (1, 1),
            [((width, f), BF)] * n_tensor,
            (1,) * n_tensor,
            [all_slots, ((n_tensor, total, f), BF), ((n_tensor, width, f), BF)],
            2 * n_tensor + 1,
            ALL,
        )

    widened = lambda v: v.astype(F32)
    downs_part = weight_parts(grad_out, hidden)
    down_near = swap(downs_part[1], 1)
    down_far = (widened(downs_part[2]) + widened(swap(downs_part[3], 1))).astype(BF)
    down_got = [swap(down_far[: part(7)], 2)]
    ups_part = weight_parts(arrived, after(grad_up, down_far))
    grad_back, down_got[0], ups_part = lax.optimization_barrier((grad_back, down_got[0], ups_part))
    down_got.append(swap(down_far[part(7) :], 2))
    up_near = swap(ups_part[1], 1)
    up_far = (widened(ups_part[2]) + widened(swap(ups_part[3], 1))).astype(BF)

    grad_residual, grad_attn, vec_two, grad_router = plain(
        back_kernel,
        [row_f32, row_bf, ((2, width), F32), ((experts, width), F32)],
        *(grad_back, place, residual, g, grad_logits, gains, router),
    )

    g0 = grad_attn.reshape(x0.shape)
    g1 = swap(g0, 1)
    g2 = swap(g0, 2)
    packed = ((n_dp, dense_rows + experts, width), BF)
    others = (vec_two, grad_router, loss_part)
    h1, h0, dw, vec_one = attn_bwd(
        *(x1, x0, g1, g0, q1, q0, c1, c0, l1, l0, masks[1], masks[0], w, gains, (), heads, None)
    )
    g2, dw, up_far, down_got[1] = lax.optimization_barrier((g2, dw, up_far, down_got[1]))
    down_got = jnp.concatenate(down_got)
    up_got = [swap(up_far[: part(5)], 2)]
    g3 = swap(g2, 1)
    h3, h2, sums, _ = attn_bwd(
        *(x3, x2, g3, g2, q3, q2, c3, c2, l3, l2, masks[3], masks[2], w, gains, (dw, vec_one) + others, heads, packed)
    )
    sums, up_got[0] = lax.optimization_barrier((sums, up_got[0]))
    t1 = swap(h1, 1)
    t2 = swap((h2 + swap(h3, 1).astype(F32)).astype(BF), 2)
    up_got.append(swap(after(up_far[part(5) :], t2), 2))
    up_got = jnp.concatenate(up_got)
    grad_down_w = widened(downs_part[0]) + widened(down_near) + widened(down_got)
    grad_up_w = widened(ups_part[0]) + widened(up_near) + widened(up_got)
    [grad_tokens] = plain(
        functools.partial(last_kernel, images), [((rows, width), F32)], *(flat(x0), flat(h0), flat(t1), flat(t2), gains, grad_residual)
    )
    gathered, grad_tokens, grad_down_w, grad_up_w = lax.optimization_barrier(
        (to_all(sums), grad_tokens, grad_down_w, grad_up_w)
    )
    grad_qkv_w, grad_proj_w, small = plain(
        dense_kernel,
        [(qkv_weight.shape, F32), (proj_weight.shape, F32), ((2 * experts, dense_rows), F32)],
        gathered,
    )
    small = small + swap(small, 1) + swap(small, 2) + swap(small, 3)
    vectors = small[experts:]
    loss = vectors[4, 0] / count
    return (
        loss,
        unpad(result),
        grad_tokens,
        vectors[0],
        vectors[1],
        grad_qkv_w,
        grad_proj_w,
        vectors[2],
        vectors[3],
        small[:experts].T,
        grad_up_w[None],
        grad_down_w[None],
    )


def solution(mesh):
    rows = P(("dp", "tensor"), None)
    experts = P("dp", None, "tensor")
    in_specs = (
        rows,
        rows,
        P("dp", None),
        rows,
        P("dp"),
        P("dp"),
        experts,
        P("dp", "tensor"),
        P("dp"),
        P("dp"),
        P("dp", None),
        experts,
        experts,
    )
    out_specs = (
        P(),
        rows,
        rows,
        P("dp"),
        P("dp"),
        experts,
        P("dp", "tensor"),
        P("dp"),
        P("dp"),
        P("dp", None),
        experts,
        experts,
    )
    return jax.shard_map(local, mesh=mesh, in_specs=in_specs, out_specs=out_specs, check_vma=False)
```

```python
import functools
import jax
import jax.numpy as jnp
from jax import lax
from jax.experimental import pallas as pl
from jax.experimental.pallas import tpu as pltpu
from jax.sharding import PartitionSpec as P

HD = 64
EPSILON = 1e-06
MASKED = -1000000000.0
BF = jnp.bfloat16
F32 = jnp.float32
LOG2E = 1.4426950408889634
MIB = 1 << 20
PLAIN = 10


def dot(a, b, ca, cb):
    return lax.dot_general(a, b, (((ca,), (cb,)), ((), ())), preferred_element_type=F32)


def swap(value, k):
    n = lax.axis_size("tensor")
    return lax.ppermute(value, "tensor", [(i, i ^ k) for i in range(n)])


def to_all(v):
    return lax.all_to_all(v, "dp", split_axis=0, concat_axis=0, tiled=True)


def norm_parts(v):
    center = v - jnp.mean(v, axis=-1, keepdims=True)
    scale = lax.rsqrt(jnp.mean(center * center, axis=-1, keepdims=True) + EPSILON)
    return center * scale, scale


def norm_back(grad, n, scale, gain):
    gy = grad * gain
    return scale * (
        gy - jnp.mean(gy, -1, keepdims=True) - n * jnp.mean(gy * n, -1, keepdims=True)
    )


def col_sum(v):
    return jnp.sum(v, axis=0, keepdims=True)


def scores_of(q, k, keep):
    s = dot(q, k, 1, 1) * HD**-0.5
    return jnp.where(keep, s, MASKED)


def one_image(x, keep, w, gain, shift, heads):
    n, _ = norm_parts(x.astype(F32))
    h1 = (n * gain + shift).astype(BF)
    c = heads * HD
    qkv = dot(h1, w[:, : 3 * c], 1, 0).astype(BF)
    contexts, totals = [], []
    for h in range(heads):
        q, k, v = (qkv[:, i * c + h * HD : i * c + (h + 1) * HD] for i in range(3))
        s = scores_of(q, k, keep)
        top = jnp.max(s, -1, keepdims=True)
        total = top + jnp.log(jnp.sum(jnp.exp(s - top), -1, keepdims=True))
        contexts.append(dot(jnp.exp(s - total).astype(BF), v, 1, 0).astype(BF))
        totals.append(total)
    context = jnp.concatenate(contexts, 1)
    return qkv, context, jnp.concatenate(totals, 1), dot(context, w[:, 3 * c :], 1, 1)


def attn_fwd_kernel(heads, n, *refs):
    xs, keeps, (w_ref, gains), outs = refs[:n], refs[n : 2 * n], refs[2 * n : 2 * n + 2], refs[2 * n + 2 :]
    if len(w_ref.shape) == 3:
        unpacked = outs[-1]

        @pl.when(pl.program_id(0) == 0)
        def _():
            rows = unpacked.shape[0] // w_ref.shape[0]
            for k in range(w_ref.shape[0]):
                unpacked[k * rows : (k + 1) * rows] = w_ref[k, :rows]

        w_ref = unpacked
    w = w_ref[...]
    gain, shift = gains[0:1], gains[1:2]
    for i in range(n):
        values = one_image(xs[i][0], keeps[i][0] > 0, w, gain, shift, heads)
        for out, value in zip(outs[4 * i : 4 * i + 4], values):
            out[0] = value.astype(out.dtype)


CHEAP = pl.CostEstimate(flops=1 << 20, bytes_accessed=1 << 10, transcendentals=0)
NEAR = pl.CostEstimate(flops=1 << 28, bytes_accessed=8 * MIB, transcendentals=0)
ALL = 58


def whole(shape):
    return pl.BlockSpec(shape, lambda *i: (0,) * len(shape))


def each(shape):
    return pl.BlockSpec((1,) + shape, lambda i: (i,) + (0,) * len(shape))


def params(vmem):
    return pltpu.CompilerParams(vmem_limit_bytes=vmem * MIB)


def attn_fwd(xs, keeps, part_types, w, gains, heads):
    images, rows, width = xs[0].shape
    c = heads * HD
    outs = []
    for part_type in part_types:
        outs += [((rows, 3 * c), BF), ((rows, c), BF), ((rows, heads), F32), ((rows, width), part_type)]
    made = pl.pallas_call(
        functools.partial(attn_fwd_kernel, heads, len(xs)),
        grid=(images,),
        in_specs=[each((rows, width)) for _ in xs] + [each((1, rows)) for _ in xs] + [whole(w.shape), whole(gains.shape)],
        out_specs=[each(s) for s, _ in outs] + [whole((width, width))] * (w.ndim - 2),
        out_shape=[jax.ShapeDtypeStruct((images,) + s, d) for s, d in outs]
        + [jax.ShapeDtypeStruct((width, width), BF)] * (w.ndim - 2),
        compiler_params=params(ALL),
        cost_estimate=CHEAP,
    )(*xs, *keeps, w, gains)
    return [made[4 * i : 4 * i + 4] for i in range(len(xs))] + list(made[4 * len(xs) :])


def one_image_back(x, ga, qkv, context, lse, keep, w, gain, shift, heads):
    n, _ = norm_parts(x.astype(F32))
    h1 = (n * gain + shift).astype(BF)
    c = heads * HD
    gc_all = dot(ga, w[:, 3 * c :], 1, 0).astype(BF)
    parts = [[], [], []]
    for h in range(heads):
        q, k, v = (qkv[:, i * c + h * HD : i * c + (h + 1) * HD] for i in range(3))
        gc = gc_all[:, h * HD : (h + 1) * HD]
        p = jnp.exp(scores_of(q, k, keep) - lse[:, h : h + 1])
        gv = dot(p.astype(BF), gc, 0, 0)
        gp = dot(gc, v, 1, 1)
        delta = jnp.sum(p * gp, -1, keepdims=True)
        gs = (p * (gp - delta)).astype(BF)
        parts[0].append((dot(gs, k, 1, 0) * HD**-0.5).astype(BF))
        parts[1].append((dot(gs, q, 0, 0) * HD**-0.5).astype(BF))
        parts[2].append(gv.astype(BF))
    gqkv = jnp.concatenate(parts[0] + parts[1] + parts[2], 1)
    gh1 = dot(gqkv, w[:, : 3 * c], 1, 1)
    return gh1, h1, gqkv, col_sum(gh1 * n), col_sum(gh1)


def split_float(v):
    high = v.astype(BF)
    return high, (v - high.astype(F32)).astype(BF)


def attn_bwd_kernel(heads, xa, xb, ga, gb, qa, qb, ca, cb, la, lb, ka, kb, w_ref, gains, *refs):
    others, (ha, hb, dw_out, vec, h_all, q_all, g_all, c_all) = refs[:-8], refs[-8:]

    @pl.when(pl.program_id(0) == 0)
    def _():
        vec[...] = others[1][...] if others else jnp.zeros_like(vec)

    w = w_ref[...]
    gain, shift = gains[0:1], gains[1:2]
    length = xa.shape[1]
    groups = ((xa, ga, qa, ca, la, ka, ha), (xb, gb, qb, cb, lb, kb, hb))
    for i, (x, g, q, c, total, k, out) in enumerate(groups):
        gh1, h1, gqkv, gg, gs = one_image_back(x[0], g[0], q[0], c[0], total[0], k[0] > 0, w, gain, shift, heads)
        out[0] = gh1.astype(out.dtype)
        at = pl.ds(pl.multiple_of((2 * pl.program_id(0) + i) * length, length), length)
        h_all[at], q_all[at], g_all[at], c_all[at] = h1, gqkv, g[0], c[0]
        vec[0:1] += gg
        vec[1:2] += gs

    @pl.when(pl.program_id(0) == pl.num_programs(0) - 1)
    def _():
        dw = jnp.concatenate([dot(h_all[...], q_all[...], 0, 0), dot(g_all[...], c_all[...], 0, 0)], 1)
        if others:
            dw = dw + others[0][...]
        if not others:
            dw_out[...] = dw
        else:
            rows = dw.shape[0] // dw_out.shape[0]
            vec_two, router, loss = others[2:]
            experts, width = router.shape
            rest = jnp.zeros((experts - 5, width), F32)
            named = jnp.concatenate([vec[...], vec_two[...], loss[...], rest], 0)
            pieces = [p.astype(F32) for v in (router[...], named) for p in split_float(v)]
            for k in range(dw_out.shape[0]):
                at = slice(k * rows, (k + 1) * rows)
                last = jnp.concatenate([p[:, at] for p in pieces] + [jnp.zeros((experts, width - 4 * rows), F32)], 1)
                dw_out[k] = jnp.concatenate([dw[at], last], 0).astype(BF)


def attn_bwd(xa, xb, ga, gb, qa, qb, ca, cb, la, lb, ka, kb, w, gains, others, heads, pack):
    images, rows, width = xa.shape
    c = heads * HD
    vec_shape = (2, width)
    specs = [each((rows, k)) for k in (width, width, 3 * c, c, heads) for _ in range(2)] + [each((1, rows))] * 2
    return pl.pallas_call(
        functools.partial(attn_bwd_kernel, heads),
        grid=(images,),
        in_specs=specs + [whole(v.shape) for v in (w, gains) + others],
        out_specs=[each((rows, width))] * 2 + [whole(pack[0] if pack else w.shape), whole(vec_shape)],
        out_shape=[jax.ShapeDtypeStruct(xa.shape, t) for t in (BF, F32)]
        + [jax.ShapeDtypeStruct(*(pack or (w.shape, F32))), jax.ShapeDtypeStruct(vec_shape, F32)],
        scratch_shapes=[pltpu.VMEM((2 * images * rows, k), BF) for k in (width, 3 * c, width, c)],
        compiler_params=params(ALL),
        cost_estimate=NEAR,
    )(xa, xb, ga, gb, qa, qb, ca, cb, la, lb, ka, kb, w, gains, *others)


def chosen(slot_row, slots):
    at = lax.broadcasted_iota(jnp.int32, (slots, slot_row.shape[1]), 0)
    return jnp.where(slot_row == at, 1.0, 0.0).astype(BF)


def dispatch_kernel(slots, x, p0, r1, r2, gains, router, slot, residual, probs, sent):
    res = x[...].astype(F32) + p0[...] + r1[...].astype(F32) + r2[...].astype(F32)
    residual[...] = res
    n, _ = norm_parts(res)
    h2 = (n * gains[2:3] + gains[3:4]).astype(BF)
    logits = dot(h2, router[...], 1, 1)
    grown = jnp.exp(logits - jnp.max(logits, -1, keepdims=True))
    probs[...] = grown / jnp.sum(grown, -1, keepdims=True)
    for e in range(slot.shape[0]):
        at = slice(e * slots, (e + 1) * slots)
        sent[at] = dot(chosen(slot[e : e + 1], slots), h2, 1, 0).astype(BF)


def picks(place, total):
    at = lax.broadcasted_iota(jnp.int32, (place.shape[0], total), 1)
    return jnp.where(place == at, 1.0, 0.0)


def combine_kernel(slots, back, place, ids, probs_in, residual, teacher, mask, factor, slot, out, g_out, gl_out, loss, sent):
    probs = probs_in[...]
    experts = probs.shape[1]
    at = lax.broadcasted_iota(jnp.int32, probs.shape, 1)
    choose = [jnp.where(ids[:, j : j + 1] == at, 1.0, 0.0) for j in range(ids.shape[1])]
    gates = [jnp.sum(c * probs, -1, keepdims=True) for c in choose]
    picked = [dot(picks(place[:, j : j + 1], back.shape[0]).astype(BF), back[...], 1, 0) for j in range(len(gates))]
    result = residual[...]
    result = result + sum(gate * p for gate, p in zip(gates, picked))
    out[...] = result.astype(BF)
    errors = result - teacher[...].astype(F32)
    m = mask[...]
    row_loss = jnp.mean(errors * errors, -1, keepdims=True) * m
    loss[...] = jnp.broadcast_to(col_sum(row_loss), loss.shape)
    g = m * errors * factor[0:1, 0:1]
    g_out[...] = g
    grad_probs = sum(c * jnp.sum(g * p, -1, keepdims=True) for c, p in zip(choose, picked))
    grad_logits = probs * (grad_probs - jnp.sum(probs * grad_probs, -1, keepdims=True))
    gl_out[...] = grad_logits.astype(BF)
    for e in range(experts):
        at = slice(e * slots, (e + 1) * slots)
        gated = (probs[:, e : e + 1] * g).astype(BF)
        sent[at] = dot(chosen(slot[e : e + 1], slots), gated, 1, 0).astype(BF)


def back_kernel(back, place, residual, g, gl, gains, router, grad_residual, grad_attn, vec, grad_router):
    either = sum(picks(place[:, j : j + 1], back.shape[0]) for j in range(place.shape[1])).astype(BF)
    grad_h2 = dot(either, back[...], 1, 0) + dot(gl[...], router[...], 1, 0)
    n, scale = norm_parts(residual[...])
    gain = gains[2:3]
    h2 = (n * gain + gains[3:4]).astype(BF)
    vec[0:1] = col_sum(grad_h2 * n)
    vec[1:2] = col_sum(grad_h2)
    grad_router[...] = dot(gl[...], h2, 0, 0)
    total = g[...] + norm_back(grad_h2, n, scale, gain)
    grad_residual[...] = total
    grad_attn[...] = total.astype(BF)


def last_kernel(images, x, p0, r1, r2, gains, grad_residual, out):
    grad_h1 = p0[...] + r1[...].astype(F32) + r2[...].astype(F32)
    n, scale = norm_parts(x[...].astype(F32))
    total = grad_residual[...] + norm_back(grad_h1, n, scale, gains[0:1])
    padded, length = x.shape[0] // images, out.shape[0] // images
    for i in range(images):
        out[i * length : (i + 1) * length] = total[i * padded : i * padded + length]


def plain(kernel, outs, *args):
    return pl.pallas_call(
        kernel,
        grid=(1,),
        in_specs=[whole(v.shape) for v in args],
        out_specs=[whole(s) for s, _ in outs],
        out_shape=[jax.ShapeDtypeStruct(s, d) for s, d in outs],
        compiler_params=params(ALL),
        cost_estimate=CHEAP,
    )(*args)


class Copies:
    def __init__(self, sems):
        self.sems, self.made = sems, []

    def start(self, source, target):
        copy = pltpu.make_async_copy(source, target, self.sems.at[len(self.made)])
        copy.start()
        self.made.append(copy)
        return copy


def dense_kernel(parts, qkv, proj):
    rows, c = proj.shape
    total = parts[0, :rows].astype(F32)
    for k in range(1, parts.shape[0]):
        total = total + parts[k, :rows].astype(F32)
    for i in range(3):
        qkv[:, i, :] = total[:, i * c : (i + 1) * c]
    proj[...] = total[:, 3 * c :]


def shard_kernel(qkv, proj, g1, s1, g2, s2, router, mask, out):
    weights = jnp.concatenate([qkv[:, i, :] for i in range(3)] + [proj[...]], 1)
    rows, width = weights.shape
    count = jnp.sum(jnp.sum(mask[...].astype(F32), 1, keepdims=True), 0, keepdims=True)
    high = jnp.floor(count / 128)
    vectors = [v[...].astype(F32) for v in (g1, s1, g2, s2)] + [high, count - 128 * high]
    vectors.append(jnp.zeros((1, width - 4 * rows - 2), F32))
    turned = router[...].astype(F32)
    last = jnp.concatenate([turned[e : e + 1] for e in range(turned.shape[0])], 1)
    extra = jnp.concatenate([jnp.concatenate(vectors, 1), last], 0)
    block = jnp.concatenate([weights, extra.astype(BF)], 0)
    for k in range(out.shape[0]):
        out[k] = block


def gelu_parts(u):
    phi = 0.5 * lax.erf(u * 0.7071067811865476) + 0.5
    bell = jnp.exp2(u * u * (-0.5 * LOG2E))
    return u * phi, phi + u * bell * 0.3989422804014327


class Pieces:
    def __init__(self, lists):
        self.arrays = [v for pieces in lists for v in pieces]
        self.plan = []
        for pieces in lists:
            ends = [sum(v.shape[0] for v in pieces[: i + 1]) for i in range(len(pieces))]
            self.plan.append([(end - v.shape[0], v.shape[0]) for end, v in zip(ends, pieces)])

    def starter(self, copies, refs, target):
        refs, made = iter(refs), []
        for t, pieces in enumerate(self.plan):
            made.append([(next(refs), target.at[t, slice(at, at + size)]) for at, size in pieces])
        return lambda t: [copies.start(*pair) for pair in made[t]]


def wait_all(copies):
    for copy in copies:
        copy.wait()


def expert_fwd_kernel(ups, downs, step, x, *refs):
    count = len(ups.arrays), len(downs.arrays)
    (out, hidden, slope), (wu, wd, hs, ss, os, sems) = refs[-9:-6], refs[-6:]
    copies = Copies(sems)
    start_up = ups.starter(copies, refs[: count[0]], wu)
    start_down = downs.starter(copies, refs[count[0] : sum(count)], wd)
    n, f = wu.shape[0], wu.shape[2]
    chunks = [slice(row, row + step) for row in range(0, x.shape[0], step)]
    ready, down_in, outgoing = [start_up(t) for t in range(min(2, n))], [], []
    for i, at in enumerate(chunks):
        for t in range(n):
            cols = slice(t * f, (t + 1) * f)
            if i == 0:
                wait_all(ready[t])
                if t + 2 < n:
                    ready.append(start_up(t + 2))
            value, der = gelu_parts(dot(x[at], wu[t], 1, 0))
            hs[at, cols] = value.astype(BF)
            ss[at, cols] = der.astype(BF)
        for t in range(i * n // len(chunks), (i + 1) * n // len(chunks)):
            down_in += start_down(t)
        outgoing.append(copies.start(hs.at[at], hidden.at[at]))
        outgoing.append(copies.start(ss.at[at], slope.at[at]))
    wait_all(down_in)
    for at in chunks:
        os[at] = dot(hs[at], jnp.concatenate([wd[t] for t in range(n)], 1), 1, 1).astype(BF)
        outgoing.append(copies.start(os.at[at], out.at[at]))
    wait_all(outgoing)


def expert_bwd_kernel(ups, downs, step, go, slope, *refs):
    count = len(ups.arrays), len(downs.arrays)
    (grad_up, out), (wu, wd, gs, ss, os, sems) = refs[-8:-6], refs[-6:]
    copies = Copies(sems)
    start_up = ups.starter(copies, refs[: count[0]], wu)
    start_down = downs.starter(copies, refs[count[0] : sum(count)], wd)
    n, f = wu.shape[0], wu.shape[2]
    chunks = [slice(row, row + step) for row in range(0, go.shape[0], step)]
    def start_first(t):
        cols = slice(t * f, (t + 1) * f)
        return start_down(t) + [copies.start(slope.at[chunks[0], cols], ss.at[chunks[0], cols])]

    ready, slope_in = [start_first(t) for t in range(min(2, n))], [None]
    up_in, outgoing = [], []
    for i, at in enumerate(chunks):
        if i > 0:
            slope_in[i].wait()
        if 0 < i and i + 1 < len(chunks):
            slope_in.append(copies.start(slope.at[chunks[i + 1]], ss.at[chunks[i + 1]]))
        for t in range(n):
            cols = slice(t * f, (t + 1) * f)
            if i == 0:
                wait_all(ready[t])
                if t + 2 < n:
                    ready.append(start_first(t + 2))
                elif t + 2 == n and len(chunks) > 1:
                    slope_in.append(copies.start(slope.at[chunks[1]], ss.at[chunks[1]]))
            grad_hidden = dot(go[at], wd[t], 1, 0)
            gs[at, cols] = (grad_hidden * ss[at, cols].astype(F32)).astype(BF)
        for t in range(i * n // len(chunks), (i + 1) * n // len(chunks)):
            up_in += start_up(t)
        outgoing.append(copies.start(gs.at[at], grad_up.at[at]))
    wait_all(up_in)
    for at in chunks:
        os[at] = dot(gs[at], jnp.concatenate([wu[t] for t in range(n)], 1), 1, 1).astype(BF)
        outgoing.append(copies.start(os.at[at], out.at[at]))
    wait_all(outgoing)


def expert_weights_kernel(parts, rows, cols, *refs):
    n = len(parts)
    outs, (rs, cs, os, sems) = refs[:n], refs[n:]
    copies = Copies(sems)
    f = os.shape[2]
    rows_in = copies.start(rows, rs)
    cols_in = [copies.start(cols.at[:, slice(t * f, (t + 1) * f)], cs.at[i]) for i, t in enumerate(parts)]
    rows_in.wait()
    outgoing = []
    for t in range(n):
        cols_in[t].wait()
        os[t] = dot(rs[...], cs[t], 0, 0).astype(BF)
        outgoing.append(copies.start(os.at[t], outs[t]))
    for copy in outgoing:
        copy.wait()


IN_HBM = pl.BlockSpec(memory_space=pltpu.HBM)
IN_VMEM = pl.BlockSpec(memory_space=pltpu.VMEM)


def copying(kernel, ins, in_hbm, outs, out_hbm, scratch, copies, vmem=PLAIN):
    spec = lambda far: IN_HBM if far else IN_VMEM
    return pl.pallas_call(
        kernel,
        in_specs=[spec(far) for far in in_hbm],
        out_specs=[spec(far) for far in out_hbm],
        out_shape=[jax.ShapeDtypeStruct(s, d) for s, d in outs],
        scratch_shapes=[pltpu.VMEM(s, d) for s, d in scratch] + [pltpu.SemaphoreType.DMA((copies,))],
        compiler_params=params(vmem),
        cost_estimate=CHEAP if vmem == ALL else NEAR,
    )(*ins)


def after(value, *others):
    return lax.optimization_barrier((value,) + others)[0]


def local(
    tokens,
    teacher,
    valid_mask,
    expert_ids,
    attn_gain,
    attn_shift,
    qkv_weight,
    proj_weight,
    moe_gain,
    moe_shift,
    router_weight,
    up_weight,
    down_weight,
):
    rows, width = tokens.shape
    length = valid_mask.shape[1]
    images = rows // length
    experts = router_weight.shape[1]
    top = expert_ids.shape[1]
    capacity = max(2, (top * rows + experts - 1) // experts * 5 // 4)
    slots = -(-capacity // 16) * 16
    padded = -(-length // 16) * 16
    own = images * padded
    n_dp = lax.axis_size("dp")
    n_tensor = lax.axis_size("tensor")
    tensor_me = lax.axis_index("tensor")
    heads_width = proj_weight.shape[1]
    heads = heads_width // HD

    def pad(v, value=0):
        v = v.reshape((images, length) + v.shape[1:])
        return jnp.pad(v, ((0, 0), (0, padded - length)) + ((0, 0),) * (v.ndim - 2), constant_values=value)

    def unpad(v):
        return v.reshape(images, padded, -1)[:, :length].reshape(rows, -1)

    x0 = pad(tokens)
    x1 = swap(x0, 1)
    x2 = swap(x0, 2)
    x3 = swap(x2, 1)
    x = (x0, x1, x2, x3)

    dense_rows = proj_weight.shape[0]
    row = lambda v: v.reshape(1, dense_rows)
    [shards] = plain(
        shard_kernel,
        [((n_dp, dense_rows + 2, width), BF)],
        *(qkv_weight, proj_weight, row(attn_gain), row(attn_shift), row(moe_gain), row(moe_shift)),
        *(router_weight.T, valid_mask),
    )
    got = to_all(shards)
    extras = got[:, dense_rows]
    gains = extras[:, : 4 * dense_rows].reshape(n_dp, 4, dense_rows).swapaxes(0, 1).reshape(4, width).astype(F32)
    counts = jnp.sum(extras[:, 4 * dense_rows : 4 * dense_rows + 2].astype(F32), 0)
    count = counts[0] * 128 + counts[1]
    router = got[:, dense_rows + 1].reshape(n_dp, experts, dense_rows).swapaxes(0, 1).reshape(experts, width)

    up0, down0 = up_weight[0], down_weight[0]
    part = lambda sixteenths: width * sixteenths // 16
    up2 = [swap(up0[: part(9)], 2)]

    mask = jnp.pad(valid_mask, ((0, 0), (0, padded - length))).reshape(n_tensor, images, 1, padded)
    masks = [lax.dynamic_index_in_dim(mask, tensor_me ^ k, 0, keepdims=False) for k in range(4)]
    row_mask = masks[0].reshape(own, 1).astype(F32)
    ids = pad(expert_ids, -1).reshape(own, top)
    each_expert = lax.iota(jnp.int32, experts)
    named = ids[:, :, None] == each_expert
    names = jnp.any(named, axis=1)
    row_at = lax.iota(jnp.int32, own)
    before = (row_at[:, None] > row_at[None, :]).astype(BF)
    slot = jnp.where(names, dot(before, names.astype(BF), 1, 0).astype(jnp.int32), -1)
    place = jnp.where(ids < 0, -1, ids * slots + jnp.sum(jnp.where(named, slot[:, None, :], 0), -1))
    slot = slot.T

    got, up2[0] = lax.optimization_barrier((got, up2[0]))
    w = got if dense_rows % 16 == 0 else got[:, :dense_rows].reshape(width, width)
    (q3, c3, l3, p3), (q2, c2, l2, p2), (q1, c1, l1, p1), *unpacked = attn_fwd(
        (x3, x2, x1), (masks[3], masks[2], masks[1]), (BF, F32, BF), w, gains, heads
    )
    w = unpacked[0] if unpacked else w
    far = (p2 + swap(p3, 1).astype(F32)).astype(BF)
    r2 = swap(far, 2)
    [(q0, c0, l0, p0)] = attn_fwd((x0,), (masks[0],), (F32,), w, gains, heads)
    r1 = swap(p1, 1)
    flat = lambda v: v.reshape(own, v.shape[-1])
    row_f32 = ((own, width), F32)
    row_bf = ((own, width), BF)
    all_slots = ((experts * slots, width), BF)
    residual, probs, sent = plain(
        functools.partial(dispatch_kernel, slots),
        [row_f32, ((own, experts), F32), all_slots],
        *(flat(x0), flat(p0), flat(r1), flat(r2), gains, router, slot),
    )
    up2.append(swap(after(up0[part(9) :], r2), 2))
    down2 = [swap(after(down0[: part(12)], r2), 2)]
    down2.append(swap(after(down0[part(12) :], down2[0]), 2))
    beside = lambda v: [swap(piece, 1) for piece in v]
    ups = [[up0], beside([up0]), up2, beside(up2)]
    downs = [[down0], beside([down0]), down2, beside(down2)]

    exchange = lambda v: to_all(v.reshape(n_dp, slots, width)).reshape(n_dp * slots, width)
    arrived = exchange(sent)
    total = n_dp * slots
    step = min(256, total)
    f = up0.shape[1]
    wide = ((total, n_tensor * f), BF)
    weights_in = [((n_tensor, width, f), BF)] * 2
    chunks = total // step
    pieces = Pieces(ups), Pieces(downs)
    weights = pieces[0].arrays + pieces[1].arrays
    out, hidden, slope = copying(
        functools.partial(expert_fwd_kernel, *pieces, step),
        (arrived, *weights),
        (0,) + (1,) * len(weights),
        [all_slots, wide, wide],
        (1, 1, 1),
        weights_in + [wide, wide, all_slots],
        len(weights) + 3 * chunks,
        ALL,
    )
    returned = exchange(out)
    factor = jnp.full((1, 128), rows * n_dp * n_tensor / count, F32)
    result, g, grad_logits, loss_part, grad_sent = plain(
        functools.partial(combine_kernel, slots),
        [row_bf, row_f32, ((own, experts), BF), ((1, width), F32), all_slots],
        *(returned, place, ids, probs, residual, flat(pad(teacher)), row_mask, factor, slot),
    )
    grad_out = exchange(grad_sent)
    grad_up, grad_arrived = copying(
        functools.partial(expert_bwd_kernel, *pieces, step),
        (grad_out, slope, *weights),
        (0, 1) + (1,) * len(weights),
        [wide, all_slots],
        (1, 1),
        weights_in + [wide, wide, all_slots],
        len(weights) + n_tensor + 3 * chunks,
        ALL,
    )
    grad_back = exchange(grad_arrived)

    def weight_parts(rows_in, cols_in, parts):
        n = len(parts)
        return copying(
            functools.partial(expert_weights_kernel, parts),
            (rows_in, cols_in),
            (1, 1),
            [((width, f), BF)] * n,
            (1,) * n,
            [all_slots, ((n, total, f), BF), ((n, width, f), BF)],
            2 * n + 1,
            ALL,
        )

    widened = lambda v: v.astype(F32)
    near, far = (0, 1), (2, 3)
    downs_far = weight_parts(grad_out, hidden, far)
    down_far = (widened(downs_far[0]) + widened(swap(downs_far[1], 1))).astype(BF)
    down_got = swap(down_far, 2)
    grad_out, grad_up = lax.optimization_barrier((grad_out, grad_up, downs_far))[:2]
    downs_part = weight_parts(grad_out, hidden, near)
    ups_part = weight_parts(arrived, grad_up, near + far)
    grad_back, down_got, downs_part, ups_part = lax.optimization_barrier((grad_back, down_got, downs_part, ups_part))
    down_near = swap(downs_part[1], 1)
    up_near = swap(ups_part[1], 1)
    up_far = (widened(ups_part[2]) + widened(swap(ups_part[3], 1))).astype(BF)

    grad_residual, grad_attn, vec_two, grad_router = plain(
        back_kernel,
        [row_f32, row_bf, ((2, width), F32), ((experts, width), F32)],
        *(grad_back, place, residual, g, grad_logits, gains, router),
    )

    g0 = grad_attn.reshape(x0.shape)
    g1 = swap(g0, 1)
    g2 = swap(g0, 2)
    packed = ((n_dp, dense_rows + experts, width), BF)
    others = (vec_two, grad_router, loss_part)
    h1, h0, dw, vec_one = attn_bwd(
        *(x1, x0, g1, g0, q1, q0, c1, c0, l1, l0, masks[1], masks[0], w, gains, (), heads, None)
    )
    g2, dw, up_far = lax.optimization_barrier((g2, dw, up_far))
    up_got = [swap(up_far[: part(10)], 2)]
    g3 = swap(g2, 1)
    h3, h2, sums, _ = attn_bwd(
        *(x3, x2, g3, g2, q3, q2, c3, c2, l3, l2, masks[3], masks[2], w, gains, (dw, vec_one) + others, heads, packed)
    )
    sums, up_got[0] = lax.optimization_barrier((sums, up_got[0]))
    t1 = swap(h1, 1)
    t2 = swap((h2 + swap(h3, 1).astype(F32)).astype(BF), 2)
    up_got.append(swap(after(up_far[part(10) :], t2), 2))
    up_got = jnp.concatenate(up_got)
    grad_down_w = widened(downs_part[0]) + widened(down_near) + widened(down_got)
    grad_up_w = widened(ups_part[0]) + widened(up_near) + widened(up_got)
    [grad_tokens] = plain(
        functools.partial(last_kernel, images), [((rows, width), F32)], *(flat(x0), flat(h0), flat(t1), flat(t2), gains, grad_residual)
    )
    gathered, grad_tokens, grad_down_w, grad_up_w, result = lax.optimization_barrier(
        (to_all(sums), grad_tokens, grad_down_w, grad_up_w, unpad(result))
    )
    grad_qkv_w, grad_proj_w = plain(
        dense_kernel,
        [(qkv_weight.shape, F32), (proj_weight.shape, F32)],
        gathered if dense_rows % 16 == 0 else gathered[:, :dense_rows],
    )
    last = jnp.sum(gathered[:, dense_rows:, : 4 * dense_rows].astype(F32), 0)
    piece = lambda i: last[:, i * dense_rows : (i + 1) * dense_rows]
    small = jnp.concatenate([piece(0) + piece(1), piece(2) + piece(3)])
    small = small + swap(small, 1) + swap(small, 2) + swap(small, 3)
    vectors = small[experts:]
    loss = vectors[4, 0] / count
    return (
        loss,
        result,
        grad_tokens,
        vectors[0],
        vectors[1],
        grad_qkv_w,
        grad_proj_w,
        vectors[2],
        vectors[3],
        small[:experts].T,
        grad_up_w[None],
        grad_down_w[None],
    )


def solution(mesh):
    rows = P(("dp", "tensor"), None)
    experts = P("dp", None, "tensor")
    in_specs = (
        rows,
        rows,
        P("dp", None),
        rows,
        P("dp"),
        P("dp"),
        experts,
        P("dp", "tensor"),
        P("dp"),
        P("dp"),
        P("dp", None),
        experts,
        experts,
    )
    out_specs = (
        P(),
        rows,
        rows,
        P("dp"),
        P("dp"),
        experts,
        P("dp", "tensor"),
        P("dp"),
        P("dp"),
        P("dp", None),
        experts,
        experts,
    )
    return jax.shard_map(local, mesh=mesh, in_specs=in_specs, out_specs=out_specs, check_vma=False)
```

```python
import functools
import jax
import jax.numpy as jnp
from jax import lax
from jax.experimental import pallas as pl
from jax.experimental.pallas import tpu as pltpu
from jax.sharding import PartitionSpec as P

HD = 64
EPSILON = 1e-06
MASKED = -1000000000.0
BF = jnp.bfloat16
F32 = jnp.float32
LOG2E = 1.4426950408889634
MIB = 1 << 20
PLAIN = 10


def dot(a, b, ca, cb):
    return lax.dot_general(a, b, (((ca,), (cb,)), ((), ())), preferred_element_type=F32)


def swap(value, k):
    n = lax.axis_size("tensor")
    return lax.ppermute(value, "tensor", [(i, i ^ k) for i in range(n)])


def to_all(v):
    return lax.all_to_all(v, "dp", split_axis=0, concat_axis=0, tiled=True)


def norm_parts(v):
    center = v - jnp.mean(v, axis=-1, keepdims=True)
    scale = lax.rsqrt(jnp.mean(center * center, axis=-1, keepdims=True) + EPSILON)
    return center * scale, scale


def norm_back(grad, n, scale, gain):
    gy = grad * gain
    return scale * (
        gy - jnp.mean(gy, -1, keepdims=True) - n * jnp.mean(gy * n, -1, keepdims=True)
    )


def col_sum(v):
    return jnp.sum(v, axis=0, keepdims=True)


def one_image(x, keep, w, gain, shift, heads):
    n, _ = norm_parts(x.astype(F32))
    h1 = (n * gain + shift).astype(BF)
    c = heads * HD
    qkv = dot(h1, w[:, : 3 * c], 1, 0).astype(BF)
    contexts = []
    for h in range(heads):
        q, k, v = (qkv[:, i * c + h * HD : i * c + (h + 1) * HD] for i in range(3))
        s = jnp.where(keep, dot(q, k, 1, 1) * HD**-0.5, MASKED)
        grown = jnp.exp(s - jnp.max(s, -1, keepdims=True))
        probs = grown * (1.0 / jnp.sum(grown, -1, keepdims=True))
        contexts.append(dot(probs.astype(BF), v, 1, 0).astype(BF))
    context = jnp.concatenate(contexts, 1)
    return qkv, context, dot(context, w[:, 3 * c :], 1, 1)


def attn_fwd_kernel(heads, n, *refs):
    xs, keeps, (w_ref, gains), outs = refs[:n], refs[n : 2 * n], refs[2 * n : 2 * n + 2], refs[2 * n + 2 :]
    if len(w_ref.shape) == 3:
        unpacked = outs[-1]

        @pl.when(pl.program_id(0) == 0)
        def _():
            rows = unpacked.shape[0] // w_ref.shape[0]
            for k in range(w_ref.shape[0]):
                unpacked[k * rows : (k + 1) * rows] = w_ref[k, :rows]

        w_ref = unpacked
    w = w_ref[...]
    gain, shift = gains[0:1], gains[1:2]
    for i in range(n):
        for m in range(xs[i].shape[0]):
            values = one_image(xs[i][m], keeps[i][m] > 0, w, gain, shift, heads)
            for out, value in zip(outs[3 * i : 3 * i + 3], values):
                out[m] = value.astype(out.dtype)


CHEAP = pl.CostEstimate(flops=1 << 20, bytes_accessed=1 << 10, transcendentals=0)
NEAR = pl.CostEstimate(flops=1 << 28, bytes_accessed=8 * MIB, transcendentals=0)
ALL = 61


def whole(shape):
    return pl.BlockSpec(shape, lambda *i: (0,) * len(shape))


def params(vmem):
    return pltpu.CompilerParams(vmem_limit_bytes=vmem * MIB)


def attn_fwd(xs, keeps, part_types, w, gains, heads):
    images, rows, width = xs[0].shape
    c = heads * HD
    outs = []
    for part_type in part_types:
        outs += [((rows, 3 * c), BF), ((rows, c), BF), ((rows, width), part_type)]
    made = pl.pallas_call(
        functools.partial(attn_fwd_kernel, heads, len(xs)),
        grid=(1,),
        in_specs=[whole((images, rows, width)) for _ in xs] + [whole((images, 1, rows)) for _ in xs] + [whole(w.shape), whole(gains.shape)],
        out_specs=[whole((images,) + s) for s, _ in outs] + [whole((width, width))] * (w.ndim - 2),
        out_shape=[jax.ShapeDtypeStruct((images,) + s, d) for s, d in outs]
        + [jax.ShapeDtypeStruct((width, width), BF)] * (w.ndim - 2),
        compiler_params=params(ALL),
        cost_estimate=CHEAP,
    )(*xs, *keeps, w, gains)
    return [made[3 * i : 3 * i + 3] for i in range(len(xs))] + list(made[3 * len(xs) :])


def one_image_back(x, ga, qkv, context, keep, w, gain, shift, heads):
    n, _ = norm_parts(x.astype(F32))
    h1 = (n * gain + shift).astype(BF)
    c = heads * HD
    gc_all = dot(ga, w[:, 3 * c :], 1, 0).astype(BF)
    length = x.shape[0]
    at = [lax.broadcasted_iota(jnp.int32, (length, length), i) for i in (0, 1)]
    keep = jnp.sum(jnp.where(at[0] == at[1], jnp.where(keep, 1.0, 0.0), 0.0), -1, keepdims=True) > 0
    parts = [[], [], []]
    for h in range(heads):
        q, k, v = (qkv[:, i * c + h * HD : i * c + (h + 1) * HD] for i in range(3))
        gc = gc_all[:, h * HD : (h + 1) * HD]
        s = jnp.where(keep, dot(k, q, 1, 1) * HD**-0.5, MASKED)
        grown = jnp.exp(s - jnp.max(s, 0, keepdims=True))
        p = grown * (1.0 / jnp.sum(grown, 0, keepdims=True))
        gp = dot(v, gc, 1, 1)
        delta = jnp.sum(p * gp, 0, keepdims=True)
        gs = (p * (gp - delta)).astype(BF)
        parts[0].append((dot(gs, k, 0, 0) * HD**-0.5).astype(BF))
        parts[1].append((dot(gs, q, 1, 0) * HD**-0.5).astype(BF))
        parts[2].append(dot(p.astype(BF), gc, 1, 0).astype(BF))
    gqkv = jnp.concatenate(parts[0] + parts[1] + parts[2], 1)
    gh1 = dot(gqkv, w[:, : 3 * c], 1, 1)
    return gh1, h1, gqkv, col_sum(gh1 * n), col_sum(gh1)


def split_float(v):
    high = v.astype(BF)
    return high, (v - high.astype(F32)).astype(BF)


def attn_bwd_kernel(heads, xa, xb, ga, gb, qa, qb, ca, cb, ka, kb, w_ref, gains, *refs):
    others, (ha, hb, dw_out, vec, h_all, q_all, g_all, c_all) = refs[:-8], refs[-8:]

    vec[...] = others[1][...] if others else jnp.zeros_like(vec)
    w = w_ref[...]
    gain, shift = gains[0:1], gains[1:2]
    length = xa.shape[1]
    groups = ((xa, ga, qa, ca, ka, ha), (xb, gb, qb, cb, kb, hb))
    for i, (x, g, q, c, k, out) in enumerate(groups):
        for m in range(x.shape[0]):
            gh1, h1, gqkv, gg, gs = one_image_back(x[m], g[m], q[m], c[m], k[m] > 0, w, gain, shift, heads)
            out[m] = gh1.astype(out.dtype)
            at = slice((2 * m + i) * length, (2 * m + i + 1) * length)
            h_all[at], q_all[at], g_all[at], c_all[at] = h1, gqkv, g[m], c[m]
            vec[0:1] += gg
            vec[1:2] += gs

    dw = jnp.concatenate([dot(h_all[...], q_all[...], 0, 0), dot(g_all[...], c_all[...], 0, 0)], 1)
    if others:
        dw = dw + others[0][...].astype(F32)
    if not others:
        dw_out[...] = dw.astype(BF)
    else:
        rows = dw.shape[0] // dw_out.shape[0]
        vec_two, router, loss = others[2:]
        experts, width = router.shape
        rest = jnp.zeros((experts - 5, width), F32)
        named = jnp.concatenate([vec[...], vec_two[...], loss[...], rest], 0)
        pieces = [p.astype(F32) for v in (router[...], named) for p in split_float(v)]
        for k in range(dw_out.shape[0]):
            at = slice(k * rows, (k + 1) * rows)
            last = jnp.concatenate([p[:, at] for p in pieces] + [jnp.zeros((experts, width - 4 * rows), F32)], 1)
            dw_out[k] = jnp.concatenate([dw[at], last], 0).astype(BF)


def attn_bwd(xa, xb, ga, gb, qa, qb, ca, cb, ka, kb, w, gains, others, heads, pack):
    images, rows, width = xa.shape
    c = heads * HD
    vec_shape = (2, width)
    specs = [whole((images, rows, k)) for k in (width, width, 3 * c, c) for _ in range(2)] + [whole((images, 1, rows))] * 2
    return pl.pallas_call(
        functools.partial(attn_bwd_kernel, heads),
        grid=(1,),
        in_specs=specs + [whole(v.shape) for v in (w, gains) + others],
        out_specs=[whole((images, rows, width))] * 2 + [whole(pack[0] if pack else w.shape), whole(vec_shape)],
        out_shape=[jax.ShapeDtypeStruct(xa.shape, t) for t in (BF, F32)]
        + [jax.ShapeDtypeStruct(*(pack or (w.shape, BF))), jax.ShapeDtypeStruct(vec_shape, F32)],
        scratch_shapes=[pltpu.VMEM((2 * images * rows, k), BF) for k in (width, 3 * c, width, c)],
        compiler_params=params(ALL),
        cost_estimate=CHEAP,
    )(xa, xb, ga, gb, qa, qb, ca, cb, ka, kb, w, gains, *others)


def chosen(slot_row, slots):
    at = lax.broadcasted_iota(jnp.int32, (slots, slot_row.shape[1]), 0)
    return jnp.where(slot_row == at, 1.0, 0.0).astype(BF)


def dispatch_kernel(slots, x, p0, r1, r2, gains, router, slot, residual, probs, sent):
    res = x[...].astype(F32) + p0[...] + r1[...].astype(F32) + r2[...].astype(F32)
    residual[...] = res
    n, _ = norm_parts(res)
    h2 = (n * gains[2:3] + gains[3:4]).astype(BF)
    logits = dot(h2, router[...], 1, 1)
    grown = jnp.exp(logits - jnp.max(logits, -1, keepdims=True))
    probs[...] = grown / jnp.sum(grown, -1, keepdims=True)
    for e in range(slot.shape[0]):
        at = slice(e * slots, (e + 1) * slots)
        sent[at] = dot(chosen(slot[e : e + 1], slots), h2, 1, 0).astype(BF)


def picks(place, total):
    at = lax.broadcasted_iota(jnp.int32, (place.shape[0], total), 1)
    return jnp.where(place == at, 1.0, 0.0)


def combine_kernel(slots, back, place, ids, probs_in, residual, teacher, mask, factor, slot, out, g_out, gl_out, loss, sent):
    probs = probs_in[...]
    experts = probs.shape[1]
    at = lax.broadcasted_iota(jnp.int32, probs.shape, 1)
    choose = [jnp.where(ids[:, j : j + 1] == at, 1.0, 0.0) for j in range(ids.shape[1])]
    gates = [jnp.sum(c * probs, -1, keepdims=True) for c in choose]
    picked = [dot(picks(place[:, j : j + 1], back.shape[0]).astype(BF), back[...], 1, 0) for j in range(len(gates))]
    result = residual[...]
    result = result + sum(gate * p for gate, p in zip(gates, picked))
    out[...] = result.astype(BF)
    errors = result - teacher[...].astype(F32)
    m = mask[...]
    row_loss = jnp.mean(errors * errors, -1, keepdims=True) * m
    loss[...] = jnp.broadcast_to(col_sum(row_loss), loss.shape)
    g = m * errors * factor[0:1, 0:1]
    g_out[...] = g
    grad_probs = sum(c * jnp.sum(g * p, -1, keepdims=True) for c, p in zip(choose, picked))
    grad_logits = probs * (grad_probs - jnp.sum(probs * grad_probs, -1, keepdims=True))
    gl_out[...] = grad_logits.astype(BF)
    for e in range(experts):
        at = slice(e * slots, (e + 1) * slots)
        gated = (probs[:, e : e + 1] * g).astype(BF)
        sent[at] = dot(chosen(slot[e : e + 1], slots), gated, 1, 0).astype(BF)


def back_kernel(back, place, residual, g, gl, gains, router, grad_residual, grad_attn, vec, grad_router):
    either = sum(picks(place[:, j : j + 1], back.shape[0]) for j in range(place.shape[1])).astype(BF)
    grad_h2 = dot(either, back[...], 1, 0) + dot(gl[...], router[...], 1, 0)
    n, scale = norm_parts(residual[...])
    gain = gains[2:3]
    h2 = (n * gain + gains[3:4]).astype(BF)
    vec[0:1] = col_sum(grad_h2 * n)
    vec[1:2] = col_sum(grad_h2)
    grad_router[...] = dot(gl[...], h2, 0, 0)
    total = g[...] + norm_back(grad_h2, n, scale, gain)
    grad_residual[...] = total
    grad_attn[...] = total.astype(BF)


def last_kernel(images, x, p0, r1, r2, gains, grad_residual, out):
    grad_h1 = p0[...] + r1[...].astype(F32) + r2[...].astype(F32)
    n, scale = norm_parts(x[...].astype(F32))
    total = grad_residual[...] + norm_back(grad_h1, n, scale, gains[0:1])
    padded, length = x.shape[0] // images, out.shape[0] // images
    for i in range(images):
        out[i * length : (i + 1) * length] = total[i * padded : i * padded + length]


def plain(kernel, outs, *args):
    return pl.pallas_call(
        kernel,
        grid=(1,),
        in_specs=[whole(v.shape) for v in args],
        out_specs=[whole(s) for s, _ in outs],
        out_shape=[jax.ShapeDtypeStruct(s, d) for s, d in outs],
        compiler_params=params(ALL),
        cost_estimate=CHEAP,
    )(*args)


class Copies:
    def __init__(self, sems):
        self.sems, self.made = sems, []

    def start(self, source, target):
        copy = pltpu.make_async_copy(source, target, self.sems.at[len(self.made)])
        copy.start()
        self.made.append(copy)
        return copy


def dense_kernel(parts, qkv, proj):
    rows, c = proj.shape
    total = parts[0, :rows].astype(F32)
    for k in range(1, parts.shape[0]):
        total = total + parts[k, :rows].astype(F32)
    qkv[...] = total[:, : 3 * c]
    proj[...] = total[:, 3 * c :]


def shard_kernel(qkv, proj, g1, s1, g2, s2, router, mask, out):
    weights = jnp.concatenate([qkv[:, i, :] for i in range(3)] + [proj[...]], 1)
    rows, width = weights.shape
    count = jnp.sum(jnp.sum(mask[...].astype(F32), 1, keepdims=True), 0, keepdims=True)
    high = jnp.floor(count / 128)
    vectors = [v[...].astype(F32) for v in (g1, s1, g2, s2)] + [high, count - 128 * high]
    vectors.append(jnp.zeros((1, width - 4 * rows - 2), F32))
    turned = router[...].astype(F32)
    last = jnp.concatenate([turned[e : e + 1] for e in range(turned.shape[0])], 1)
    extra = jnp.concatenate([jnp.concatenate(vectors, 1), last], 0)
    block = jnp.concatenate([weights, extra.astype(BF)], 0)
    for k in range(out.shape[0]):
        out[k] = block


def gelu_parts(u):
    phi = 0.5 * lax.erf(u * 0.7071067811865476) + 0.5
    bell = jnp.exp2(u * u * (-0.5 * LOG2E))
    return u * phi, phi + u * bell * 0.3989422804014327


class Pieces:
    def __init__(self, lists):
        self.arrays = [v for pieces in lists for v in pieces]
        self.plan = []
        for pieces in lists:
            ends = [sum(v.shape[0] for v in pieces[: i + 1]) for i in range(len(pieces))]
            self.plan.append([(end - v.shape[0], v.shape[0]) for end, v in zip(ends, pieces)])

    def starter(self, copies, refs, target):
        refs, made = iter(refs), []
        for t, pieces in enumerate(self.plan):
            made.append([(next(refs), target.at[t, slice(at, at + size)]) for at, size in pieces])
        return lambda t: [copies.start(*pair) for pair in made[t]]


def wait_all(copies):
    for copy in copies:
        copy.wait()


def expert_fwd_kernel(ups, downs, step, x, *refs):
    count = len(ups.arrays), len(downs.arrays)
    (out, hidden, slope), (wu, wd, hs, ss, os, sems) = refs[-9:-6], refs[-6:]
    copies = Copies(sems)
    start_up = ups.starter(copies, refs[: count[0]], wu)
    start_down = downs.starter(copies, refs[count[0] : sum(count)], wd)
    n, f = wu.shape[0], wu.shape[2]
    chunks = [slice(row, row + step) for row in range(0, x.shape[0], step)]
    ready, down_in, outgoing = [start_up(t) for t in range(min(2, n))], [], []
    for i, at in enumerate(chunks):
        for t in range(n):
            cols = slice(t * f, (t + 1) * f)
            if i == 0:
                wait_all(ready[t])
                if t + 2 < n:
                    ready.append(start_up(t + 2))
            value, der = gelu_parts(dot(x[at], wu[t], 1, 0))
            hs[at, cols] = value.astype(BF)
            ss[at, cols] = der.astype(BF)
        for t in range(i * n // len(chunks), (i + 1) * n // len(chunks)):
            down_in += start_down(t)
        outgoing.append(copies.start(hs.at[at], hidden.at[at]))
        outgoing.append(copies.start(ss.at[at], slope.at[at]))
    wait_all(down_in)
    for at in chunks:
        os[at] = dot(hs[at], jnp.concatenate([wd[t] for t in range(n)], 1), 1, 1).astype(BF)
        outgoing.append(copies.start(os.at[at], out.at[at]))
    wait_all(outgoing)


def expert_bwd_kernel(ups, downs, step, go, slope, *refs):
    count = len(ups.arrays), len(downs.arrays)
    (grad_up, out), (wu, wd, gs, ss, os, sems) = refs[-8:-6], refs[-6:]
    copies = Copies(sems)
    start_up = ups.starter(copies, refs[: count[0]], wu)
    start_down = downs.starter(copies, refs[count[0] : sum(count)], wd)
    n, f = wu.shape[0], wu.shape[2]
    chunks = [slice(row, row + step) for row in range(0, go.shape[0], step)]
    def start_first(t):
        cols = slice(t * f, (t + 1) * f)
        return start_down(t) + [copies.start(slope.at[chunks[0], cols], ss.at[chunks[0], cols])]

    ready, slope_in = [start_first(t) for t in range(min(2, n))], [None]
    up_in, outgoing = [], []
    for i, at in enumerate(chunks):
        if i > 0:
            slope_in[i].wait()
        if 0 < i and i + 1 < len(chunks):
            slope_in.append(copies.start(slope.at[chunks[i + 1]], ss.at[chunks[i + 1]]))
        for t in range(n):
            cols = slice(t * f, (t + 1) * f)
            if i == 0:
                wait_all(ready[t])
                if t + 2 < n:
                    ready.append(start_first(t + 2))
                elif t + 2 == n and len(chunks) > 1:
                    slope_in.append(copies.start(slope.at[chunks[1]], ss.at[chunks[1]]))
            grad_hidden = dot(go[at], wd[t], 1, 0)
            gs[at, cols] = (grad_hidden * ss[at, cols].astype(F32)).astype(BF)
        for t in range(i * n // len(chunks), (i + 1) * n // len(chunks)):
            up_in += start_up(t)
        outgoing.append(copies.start(gs.at[at], grad_up.at[at]))
    wait_all(up_in)
    for at in chunks:
        os[at] = dot(gs[at], jnp.concatenate([wu[t] for t in range(n)], 1), 1, 1).astype(BF)
        outgoing.append(copies.start(os.at[at], out.at[at]))
    wait_all(outgoing)


def expert_weights_kernel(parts, rows, cols, *refs):
    n = len(parts)
    outs, (rs, cs, os, sems) = refs[:n], refs[n:]
    copies = Copies(sems)
    f = os.shape[2]
    rows_in = copies.start(rows, rs)
    cols_in = [copies.start(cols.at[:, slice(t * f, (t + 1) * f)], cs.at[i]) for i, t in enumerate(parts)]
    rows_in.wait()
    outgoing = []
    for t in range(n):
        cols_in[t].wait()
        os[t] = dot(rs[...], cs[t], 0, 0).astype(BF)
        outgoing.append(copies.start(os.at[t], outs[t]))
    for copy in outgoing:
        copy.wait()


IN_HBM = pl.BlockSpec(memory_space=pltpu.HBM)
IN_VMEM = pl.BlockSpec(memory_space=pltpu.VMEM)


def copying(kernel, ins, in_hbm, outs, out_hbm, scratch, copies, vmem=PLAIN):
    spec = lambda far: IN_HBM if far else IN_VMEM
    return pl.pallas_call(
        kernel,
        in_specs=[spec(far) for far in in_hbm],
        out_specs=[spec(far) for far in out_hbm],
        out_shape=[jax.ShapeDtypeStruct(s, d) for s, d in outs],
        scratch_shapes=[pltpu.VMEM(s, d) for s, d in scratch] + [pltpu.SemaphoreType.DMA((copies,))],
        compiler_params=params(vmem),
        cost_estimate=CHEAP if vmem == ALL else NEAR,
    )(*ins)


def after(value, *others):
    return lax.optimization_barrier((value,) + others)[0]


def local(
    tokens,
    teacher,
    valid_mask,
    expert_ids,
    attn_gain,
    attn_shift,
    qkv_weight,
    proj_weight,
    moe_gain,
    moe_shift,
    router_weight,
    up_weight,
    down_weight,
):
    rows, width = tokens.shape
    length = valid_mask.shape[1]
    images = rows // length
    experts = router_weight.shape[1]
    top = expert_ids.shape[1]
    capacity = max(2, (top * rows + experts - 1) // experts * 5 // 4)
    slots = -(-capacity // 16) * 16
    padded = -(-length // 16) * 16
    own = images * padded
    n_dp = lax.axis_size("dp")
    n_tensor = lax.axis_size("tensor")
    tensor_me = lax.axis_index("tensor")
    heads_width = proj_weight.shape[1]
    heads = heads_width // HD

    def pad(v, value=0):
        v = v.reshape((images, length) + v.shape[1:])
        return jnp.pad(v, ((0, 0), (0, padded - length)) + ((0, 0),) * (v.ndim - 2), constant_values=value)

    def unpad(v):
        return v.reshape(images, padded, -1)[:, :length].reshape(rows, -1)

    x0 = pad(tokens)
    x1 = swap(x0, 1)
    x2 = swap(x0, 2)
    x3 = swap(x2, 1)
    x = (x0, x1, x2, x3)

    dense_rows = proj_weight.shape[0]
    row = lambda v: v.reshape(1, dense_rows)
    [shards] = plain(
        shard_kernel,
        [((n_dp, dense_rows + 2, width), BF)],
        *(qkv_weight, proj_weight, row(attn_gain), row(attn_shift), row(moe_gain), row(moe_shift)),
        *(router_weight.T, valid_mask),
    )
    got = to_all(shards)
    extras = got[:, dense_rows]
    gains = extras[:, : 4 * dense_rows].reshape(n_dp, 4, dense_rows).swapaxes(0, 1).reshape(4, width).astype(F32)
    counts = jnp.sum(extras[:, 4 * dense_rows : 4 * dense_rows + 2].astype(F32), 0)
    count = counts[0] * 128 + counts[1]
    router = got[:, dense_rows + 1].reshape(n_dp, experts, dense_rows).swapaxes(0, 1).reshape(experts, width)

    up0, down0 = up_weight[0], down_weight[0]
    part = lambda sixteenths: width * sixteenths // 16
    up2 = [swap(up0[: part(9)], 2)]

    mask = jnp.pad(valid_mask, ((0, 0), (0, padded - length))).reshape(n_tensor, images, 1, padded)
    masks = [lax.dynamic_index_in_dim(mask, tensor_me ^ k, 0, keepdims=False) for k in range(4)]
    row_mask = masks[0].reshape(own, 1).astype(F32)
    ids = pad(expert_ids, -1).reshape(own, top)
    each_expert = lax.iota(jnp.int32, experts)
    named = ids[:, :, None] == each_expert
    names = jnp.any(named, axis=1)
    row_at = lax.iota(jnp.int32, own)
    before = (row_at[:, None] > row_at[None, :]).astype(BF)
    slot = jnp.where(names, dot(before, names.astype(BF), 1, 0).astype(jnp.int32), -1)
    place = jnp.where(ids < 0, -1, ids * slots + jnp.sum(jnp.where(named, slot[:, None, :], 0), -1))
    slot = slot.T

    got, up2[0] = lax.optimization_barrier((got, up2[0]))
    w = got if dense_rows % 16 == 0 else got[:, :dense_rows].reshape(width, width)
    (q3, c3, p3), (q2, c2, p2), (q1, c1, p1), *unpacked = attn_fwd(
        (x3, x2, x1), (masks[3], masks[2], masks[1]), (BF, F32, BF), w, gains, heads
    )
    w = unpacked[0] if unpacked else w
    far = (p2 + swap(p3, 1).astype(F32)).astype(BF)
    r2 = swap(far, 2)
    [(q0, c0, p0)] = attn_fwd((x0,), (masks[0],), (F32,), w, gains, heads)
    r1 = swap(p1, 1)
    flat = lambda v: v.reshape(own, v.shape[-1])
    row_f32 = ((own, width), F32)
    row_bf = ((own, width), BF)
    all_slots = ((experts * slots, width), BF)
    residual, probs, sent = plain(
        functools.partial(dispatch_kernel, slots),
        [row_f32, ((own, experts), F32), all_slots],
        *(flat(x0), flat(p0), flat(r1), flat(r2), gains, router, slot),
    )
    up2.append(swap(after(up0[part(9) :], r2), 2))
    down2 = [swap(after(down0[: part(12)], r2), 2)]
    down2.append(swap(after(down0[part(12) :], down2[0]), 2))
    beside = lambda v: [swap(piece, 1) for piece in v]
    ups = [[up0], beside([up0]), up2, beside(up2)]
    downs = [[down0], beside([down0]), down2, beside(down2)]

    exchange = lambda v: to_all(v.reshape(n_dp, slots, width)).reshape(n_dp * slots, width)
    arrived = exchange(sent)
    total = n_dp * slots
    step = min(256, total)
    f = up0.shape[1]
    wide = ((total, n_tensor * f), BF)
    weights_in = [((n_tensor, width, f), BF)] * 2
    chunks = total // step
    pieces = Pieces(ups), Pieces(downs)
    weights = pieces[0].arrays + pieces[1].arrays
    out, hidden, slope = copying(
        functools.partial(expert_fwd_kernel, *pieces, step),
        (arrived, *weights),
        (0,) + (1,) * len(weights),
        [all_slots, wide, wide],
        (1, 1, 1),
        weights_in + [wide, wide, all_slots],
        len(weights) + 3 * chunks,
        ALL,
    )
    returned = exchange(out)
    factor = jnp.full((1, 128), rows * n_dp * n_tensor / count, F32)
    result, g, grad_logits, loss_part, grad_sent = plain(
        functools.partial(combine_kernel, slots),
        [row_bf, row_f32, ((own, experts), BF), ((1, width), F32), all_slots],
        *(returned, place, ids, probs, residual, flat(pad(teacher)), row_mask, factor, slot),
    )
    grad_out = exchange(grad_sent)
    grad_up, grad_arrived = copying(
        functools.partial(expert_bwd_kernel, *pieces, step),
        (grad_out, slope, *weights),
        (0, 1) + (1,) * len(weights),
        [wide, all_slots],
        (1, 1),
        weights_in + [wide, wide, all_slots],
        len(weights) + n_tensor + 3 * chunks,
        ALL,
    )
    grad_back = exchange(grad_arrived)

    def weight_parts(rows_in, cols_in, parts):
        n = len(parts)
        return copying(
            functools.partial(expert_weights_kernel, parts),
            (rows_in, cols_in),
            (1, 1),
            [((width, f), BF)] * n,
            (1,) * n,
            [all_slots, ((n, total, f), BF), ((n, width, f), BF)],
            2 * n + 1,
            ALL,
        )

    widened = lambda v: v.astype(F32)
    near, far = (0, 1), (2, 3)
    downs_far = weight_parts(grad_out, hidden, far)
    down_far = (widened(downs_far[0]) + widened(swap(downs_far[1], 1))).astype(BF)
    down_got = swap(down_far, 2)
    grad_out, grad_up = lax.optimization_barrier((grad_out, grad_up, downs_far))[:2]
    downs_part = weight_parts(grad_out, hidden, near)
    ups_part = weight_parts(arrived, grad_up, near + far)
    grad_back, down_got, downs_part, ups_part = lax.optimization_barrier((grad_back, down_got, downs_part, ups_part))
    down_near = swap(downs_part[1], 1)
    up_near = swap(ups_part[1], 1)
    up_far = (widened(ups_part[2]) + widened(swap(ups_part[3], 1))).astype(BF)

    grad_residual, grad_attn, vec_two, grad_router = plain(
        back_kernel,
        [row_f32, row_bf, ((2, width), F32), ((experts, width), F32)],
        *(grad_back, place, residual, g, grad_logits, gains, router),
    )

    g0 = grad_attn.reshape(x0.shape)
    g1 = swap(g0, 1)
    g2 = swap(g0, 2)
    packed = ((n_dp, dense_rows + experts, width), BF)
    others = (vec_two, grad_router, loss_part)
    h1, h0, dw, vec_one = attn_bwd(
        *(x1, x0, g1, g0, q1, q0, c1, c0, masks[1], masks[0], w, gains, (), heads, None)
    )
    g2, dw, up_far = lax.optimization_barrier((g2, dw, up_far))
    up_got = [swap(up_far[: part(9)], 2)]
    g3 = swap(g2, 1)
    h3, h2, sums, _ = attn_bwd(
        *(x3, x2, g3, g2, q3, q2, c3, c2, masks[3], masks[2], w, gains, (dw, vec_one) + others, heads, packed)
    )
    sums, up_got[0] = lax.optimization_barrier((sums, up_got[0]))
    t1 = swap(h1, 1)
    t2 = swap((h2 + swap(h3, 1).astype(F32)).astype(BF), 2)
    up_got.append(swap(after(up_far[part(9) :], t2), 2))
    up_got = jnp.concatenate(up_got)
    grad_down_w = widened(downs_part[0]) + widened(down_near) + widened(down_got)
    grad_up_w = widened(ups_part[0]) + widened(up_near) + widened(up_got)
    [grad_tokens] = plain(
        functools.partial(last_kernel, images), [((rows, width), F32)], *(flat(x0), flat(h0), flat(t1), flat(t2), gains, grad_residual)
    )
    gathered, grad_tokens, grad_down_w, grad_up_w, result = lax.optimization_barrier(
        (to_all(sums), grad_tokens, grad_down_w, grad_up_w, unpad(result))
    )
    grad_qkv_w, grad_proj_w = plain(
        dense_kernel,
        [((dense_rows, 3 * heads_width), F32), (proj_weight.shape, F32)],
        gathered if dense_rows % 16 == 0 else gathered[:, :dense_rows],
    )
    last = jnp.sum(gathered[:, dense_rows:, : 4 * dense_rows].astype(F32), 0)
    piece = lambda i: last[:, i * dense_rows : (i + 1) * dense_rows]
    small = jnp.concatenate([piece(0) + piece(1), piece(2) + piece(3)])
    small = small + swap(small, 1) + swap(small, 2) + swap(small, 3)
    vectors = small[experts:]
    loss = vectors[4, 0] / count
    return (
        loss,
        result,
        grad_tokens,
        vectors[0],
        vectors[1],
        grad_qkv_w.reshape(qkv_weight.shape),
        grad_proj_w,
        vectors[2],
        vectors[3],
        small[:experts].T,
        grad_up_w[None],
        grad_down_w[None],
    )


def solution(mesh):
    rows = P(("dp", "tensor"), None)
    experts = P("dp", None, "tensor")
    in_specs = (
        rows,
        rows,
        P("dp", None),
        rows,
        P("dp"),
        P("dp"),
        experts,
        P("dp", "tensor"),
        P("dp"),
        P("dp"),
        P("dp", None),
        experts,
        experts,
    )
    out_specs = (
        P(),
        rows,
        rows,
        P("dp"),
        P("dp"),
        experts,
        P("dp", "tensor"),
        P("dp"),
        P("dp"),
        P("dp", None),
        experts,
        experts,
    )
    return jax.shard_map(local, mesh=mesh, in_specs=in_specs, out_specs=out_specs, check_vma=False)
```

```python
import functools
import jax
import jax.numpy as jnp
from jax import lax
from jax.experimental import pallas as pl
from jax.experimental.pallas import tpu as pltpu
from jax.sharding import PartitionSpec as P

HD = 64
EPSILON = 1e-06
MASKED = -1000000000.0
BF = jnp.bfloat16
F32 = jnp.float32
LOG2E = 1.4426950408889634
MIB = 1 << 20
PLAIN = 10


def dot(a, b, ca, cb):
    return lax.dot_general(a, b, (((ca,), (cb,)), ((), ())), preferred_element_type=F32)


def swap(value, k):
    n = lax.axis_size("tensor")
    return lax.ppermute(value, "tensor", [(i, i ^ k) for i in range(n)])


def to_all(v):
    return lax.all_to_all(v, "dp", split_axis=0, concat_axis=0, tiled=True)


def norm_parts(v):
    center = v - jnp.mean(v, axis=-1, keepdims=True)
    scale = lax.rsqrt(jnp.mean(center * center, axis=-1, keepdims=True) + EPSILON)
    return center * scale, scale


def norm_back(grad, n, scale, gain):
    gy = grad * gain
    return scale * (
        gy - jnp.mean(gy, -1, keepdims=True) - n * jnp.mean(gy * n, -1, keepdims=True)
    )


def col_sum(v):
    return jnp.sum(v, axis=0, keepdims=True)


def one_image(x, keep, w, gain, shift, heads):
    n, _ = norm_parts(x.astype(F32))
    h1 = (n * gain + shift).astype(BF)
    c = heads * HD
    qkv = dot(h1, w[:, : 3 * c], 1, 0).astype(BF)
    contexts = []
    for h in range(heads):
        q, k, v = (qkv[:, i * c + h * HD : i * c + (h + 1) * HD] for i in range(3))
        s = jnp.where(keep, dot(q, k, 1, 1) * HD**-0.5, MASKED)
        grown = jnp.exp(s - jnp.max(s, -1, keepdims=True))
        probs = grown * (1.0 / jnp.sum(grown, -1, keepdims=True))
        contexts.append(dot(probs.astype(BF), v, 1, 0).astype(BF))
    context = jnp.concatenate(contexts, 1)
    return qkv, context, dot(context, w[:, 3 * c :], 1, 1)


def unpack(got, w, vectors, router, count):
    every = range(got.shape[0])
    rows = w.shape[0] // len(every)
    extras = []
    for k in every:
        block = got[k]
        w[k * rows : (k + 1) * rows] = block[:rows]
        extras.append(block[rows:].astype(F32))
    piece = lambda k, row, j: extras[k][row : row + 1, j * rows : (j + 1) * rows]
    line = lambda row, j: jnp.concatenate([piece(k, row, j) for k in every], 1)
    for j in range(vectors.shape[0]):
        vectors[j : j + 1] = line(0, j)
    router[...] = jnp.concatenate([line(1, j) for j in range(router.shape[0])], 0).astype(BF)
    at = 4 * rows
    total = sum(128 * e[0:1, at : at + 1] + e[0:1, at + 1 : at + 2] for e in extras)
    count[...] = jnp.broadcast_to(total, count.shape)


def attn_fwd_kernel(heads, n, *refs):
    xs, keeps, outs = refs[:n], refs[n : 2 * n], refs[2 * n :]
    if len(outs[0].shape) == 3:
        unpack(outs[0], *outs[-4:])
        w_ref, gains, outs = outs[-4], outs[-3], outs[1:-4]
    else:
        w_ref, gains, outs = outs[0], outs[1], outs[2:]
    w = w_ref[...]
    gain, shift = gains[0:1], gains[1:2]
    for i in range(n):
        for m in range(xs[i].shape[0]):
            values = one_image(xs[i][m], keeps[i][m] > 0, w, gain, shift, heads)
            for out, value in zip(outs[3 * i : 3 * i + 3], values):
                out[m] = value.astype(out.dtype)


CHEAP = pl.CostEstimate(flops=1 << 20, bytes_accessed=1 << 10, transcendentals=0)
NEAR = pl.CostEstimate(flops=1 << 28, bytes_accessed=8 * MIB, transcendentals=0)
ALL = 61


def whole(shape):
    return pl.BlockSpec(shape, lambda *i: (0,) * len(shape))


def params(vmem):
    return pltpu.CompilerParams(vmem_limit_bytes=vmem * MIB)


def attn_fwd(xs, keeps, part_types, weights, unpacked, heads):
    images, rows, width = xs[0].shape
    c = heads * HD
    outs = []
    for part_type in part_types:
        outs += [((rows, 3 * c), BF), ((rows, c), BF), ((rows, width), part_type)]
    outs = [((images,) + s, d) for s, d in outs] + unpacked
    made = pl.pallas_call(
        functools.partial(attn_fwd_kernel, heads, len(xs)),
        grid=(1,),
        in_specs=[whole(v.shape) for v in (*xs, *keeps, *weights)],
        out_specs=[whole(s) for s, _ in outs],
        out_shape=[jax.ShapeDtypeStruct(s, d) for s, d in outs],
        compiler_params=params(ALL),
        cost_estimate=CHEAP,
    )(*xs, *keeps, *weights)
    return [made[3 * i : 3 * i + 3] for i in range(len(xs))] + list(made[3 * len(xs) :])


def one_image_back(x, ga, qkv, context, keep, w, gain, shift, heads):
    n, _ = norm_parts(x.astype(F32))
    h1 = (n * gain + shift).astype(BF)
    c = heads * HD
    gc_all = dot(ga, w[:, 3 * c :], 1, 0).astype(BF)
    length = x.shape[0]
    at = [lax.broadcasted_iota(jnp.int32, (length, length), i) for i in (0, 1)]
    keep = jnp.sum(jnp.where(at[0] == at[1], jnp.where(keep, 1.0, 0.0), 0.0), -1, keepdims=True) > 0
    parts = [[], [], []]
    for h in range(heads):
        q, k, v = (qkv[:, i * c + h * HD : i * c + (h + 1) * HD] for i in range(3))
        gc = gc_all[:, h * HD : (h + 1) * HD]
        s = jnp.where(keep, dot(k, q, 1, 1) * HD**-0.5, MASKED)
        grown = jnp.exp(s - jnp.max(s, 0, keepdims=True))
        p = grown * (1.0 / jnp.sum(grown, 0, keepdims=True))
        gp = dot(v, gc, 1, 1)
        delta = jnp.sum(p * gp, 0, keepdims=True)
        gs = (p * (gp - delta)).astype(BF)
        parts[0].append((dot(gs, k, 0, 0) * HD**-0.5).astype(BF))
        parts[1].append((dot(gs, q, 1, 0) * HD**-0.5).astype(BF))
        parts[2].append(dot(p.astype(BF), gc, 1, 0).astype(BF))
    gqkv = jnp.concatenate(parts[0] + parts[1] + parts[2], 1)
    gh1 = dot(gqkv, w[:, : 3 * c], 1, 1)
    return gh1, h1, gqkv, col_sum(gh1 * n), col_sum(gh1)


def split_float(v):
    high = v.astype(BF)
    return high, (v - high.astype(F32)).astype(BF)


def attn_bwd_kernel(heads, xa, xb, ga, gb, qa, qb, ca, cb, ka, kb, w_ref, gains, *refs):
    others, (ha, hb, dw_out, vec, h_all, q_all, g_all, c_all) = refs[:-8], refs[-8:]

    vec[...] = others[1][...] if others else jnp.zeros_like(vec)
    w = w_ref[...]
    gain, shift = gains[0:1], gains[1:2]
    length = xa.shape[1]
    groups = ((xa, ga, qa, ca, ka, ha), (xb, gb, qb, cb, kb, hb))
    for i, (x, g, q, c, k, out) in enumerate(groups):
        for m in range(x.shape[0]):
            gh1, h1, gqkv, gg, gs = one_image_back(x[m], g[m], q[m], c[m], k[m] > 0, w, gain, shift, heads)
            out[m] = gh1.astype(out.dtype)
            at = slice((2 * m + i) * length, (2 * m + i + 1) * length)
            h_all[at], q_all[at], g_all[at], c_all[at] = h1, gqkv, g[m], c[m]
            vec[0:1] += gg
            vec[1:2] += gs

    dw = jnp.concatenate([dot(h_all[...], q_all[...], 0, 0), dot(g_all[...], c_all[...], 0, 0)], 1)
    if others:
        dw = dw + others[0][...].astype(F32)
    if not others:
        dw_out[...] = dw.astype(BF)
    else:
        rows = dw.shape[0] // dw_out.shape[0]
        vec_two, router, loss = others[2:]
        experts, width = router.shape
        rest = jnp.zeros((experts - 5, width), F32)
        named = jnp.concatenate([vec[...], vec_two[...], loss[...], rest], 0)
        pieces = [p.astype(F32) for v in (router[...], named) for p in split_float(v)]
        for k in range(dw_out.shape[0]):
            at = slice(k * rows, (k + 1) * rows)
            last = jnp.concatenate([p[:, at] for p in pieces] + [jnp.zeros((experts, width - 4 * rows), F32)], 1)
            dw_out[k] = jnp.concatenate([dw[at], last], 0).astype(BF)


def attn_bwd(xa, xb, ga, gb, qa, qb, ca, cb, ka, kb, w, gains, others, heads, pack):
    images, rows, width = xa.shape
    c = heads * HD
    vec_shape = (2, width)
    specs = [whole((images, rows, k)) for k in (width, width, 3 * c, c) for _ in range(2)] + [whole((images, 1, rows))] * 2
    return pl.pallas_call(
        functools.partial(attn_bwd_kernel, heads),
        grid=(1,),
        in_specs=specs + [whole(v.shape) for v in (w, gains) + others],
        out_specs=[whole((images, rows, width))] * 2 + [whole(pack[0] if pack else w.shape), whole(vec_shape)],
        out_shape=[jax.ShapeDtypeStruct(xa.shape, t) for t in (BF, F32)]
        + [jax.ShapeDtypeStruct(*(pack or (w.shape, BF))), jax.ShapeDtypeStruct(vec_shape, F32)],
        scratch_shapes=[pltpu.VMEM((2 * images * rows, k), BF) for k in (width, 3 * c, width, c)],
        compiler_params=params(ALL),
        cost_estimate=CHEAP,
    )(xa, xb, ga, gb, qa, qb, ca, cb, ka, kb, w, gains, *others)


def chosen(slot_row, slots):
    at = lax.broadcasted_iota(jnp.int32, (slots, slot_row.shape[1]), 0)
    return jnp.where(slot_row == at, 1.0, 0.0).astype(BF)


def dispatch_kernel(slots, x, p0, r1, r2, gains, router, slot, residual, probs, sent):
    res = x[...].astype(F32) + p0[...] + r1[...].astype(F32) + r2[...].astype(F32)
    residual[...] = res
    n, _ = norm_parts(res)
    h2 = (n * gains[2:3] + gains[3:4]).astype(BF)
    logits = dot(h2, router[...], 1, 1)
    grown = jnp.exp(logits - jnp.max(logits, -1, keepdims=True))
    probs[...] = grown / jnp.sum(grown, -1, keepdims=True)
    for e in range(slot.shape[0]):
        at = slice(e * slots, (e + 1) * slots)
        sent[at] = dot(chosen(slot[e : e + 1], slots), h2, 1, 0).astype(BF)


def picks(place, total):
    at = lax.broadcasted_iota(jnp.int32, (place.shape[0], total), 1)
    return jnp.where(place == at, 1.0, 0.0)


def combine_kernel(slots, back, place, ids, probs_in, residual, teacher, mask, factor, slot, out, g_out, gl_out, loss, sent):
    probs = probs_in[...]
    experts = probs.shape[1]
    at = lax.broadcasted_iota(jnp.int32, probs.shape, 1)
    choose = [jnp.where(ids[:, j : j + 1] == at, 1.0, 0.0) for j in range(ids.shape[1])]
    gates = [jnp.sum(c * probs, -1, keepdims=True) for c in choose]
    picked = [dot(picks(place[:, j : j + 1], back.shape[0]).astype(BF), back[...], 1, 0) for j in range(len(gates))]
    result = residual[...]
    result = result + sum(gate * p for gate, p in zip(gates, picked))
    out[...] = result.astype(BF)
    errors = result - teacher[...].astype(F32)
    m = mask[...]
    row_loss = jnp.mean(errors * errors, -1, keepdims=True) * m
    loss[...] = jnp.broadcast_to(col_sum(row_loss), loss.shape)
    g = m * errors * factor[0:1, 0:1]
    g_out[...] = g
    grad_probs = sum(c * jnp.sum(g * p, -1, keepdims=True) for c, p in zip(choose, picked))
    grad_logits = probs * (grad_probs - jnp.sum(probs * grad_probs, -1, keepdims=True))
    gl_out[...] = grad_logits.astype(BF)
    for e in range(experts):
        at = slice(e * slots, (e + 1) * slots)
        gated = (probs[:, e : e + 1] * g).astype(BF)
        sent[at] = dot(chosen(slot[e : e + 1], slots), gated, 1, 0).astype(BF)


def back_kernel(back, place, residual, g, gl, gains, router, grad_residual, grad_attn, vec, grad_router):
    either = sum(picks(place[:, j : j + 1], back.shape[0]) for j in range(place.shape[1])).astype(BF)
    grad_h2 = dot(either, back[...], 1, 0) + dot(gl[...], router[...], 1, 0)
    n, scale = norm_parts(residual[...])
    gain = gains[2:3]
    h2 = (n * gain + gains[3:4]).astype(BF)
    vec[0:1] = col_sum(grad_h2 * n)
    vec[1:2] = col_sum(grad_h2)
    grad_router[...] = dot(gl[...], h2, 0, 0)
    total = g[...] + norm_back(grad_h2, n, scale, gain)
    grad_residual[...] = total
    grad_attn[...] = total.astype(BF)


def last_kernel(images, x, p0, r1, r2, gains, grad_residual, out):
    grad_h1 = p0[...] + r1[...].astype(F32) + r2[...].astype(F32)
    n, scale = norm_parts(x[...].astype(F32))
    total = grad_residual[...] + norm_back(grad_h1, n, scale, gains[0:1])
    padded, length = x.shape[0] // images, out.shape[0] // images
    for i in range(images):
        out[i * length : (i + 1) * length] = total[i * padded : i * padded + length]


def plain(kernel, outs, *args):
    return pl.pallas_call(
        kernel,
        grid=(1,),
        in_specs=[whole(v.shape) for v in args],
        out_specs=[whole(s) for s, _ in outs],
        out_shape=[jax.ShapeDtypeStruct(s, d) for s, d in outs],
        compiler_params=params(ALL),
        cost_estimate=CHEAP,
    )(*args)


class Copies:
    def __init__(self, sems):
        self.sems, self.made = sems, []

    def start(self, source, target):
        copy = pltpu.make_async_copy(source, target, self.sems.at[len(self.made)])
        copy.start()
        self.made.append(copy)
        return copy


def dense_kernel(parts, qkv, proj):
    rows, c = proj.shape
    total = parts[0, :rows].astype(F32)
    for k in range(1, parts.shape[0]):
        total = total + parts[k, :rows].astype(F32)
    qkv[...] = total[:, : 3 * c]
    proj[...] = total[:, 3 * c :]


def shard_kernel(qkv, proj, g1, s1, g2, s2, router, mask, out):
    weights = jnp.concatenate([qkv[:, i, :] for i in range(3)] + [proj[...]], 1)
    rows, width = weights.shape
    count = jnp.sum(jnp.sum(mask[...].astype(F32), 1, keepdims=True), 0, keepdims=True)
    high = jnp.floor(count / 128)
    vectors = [v[...].astype(F32) for v in (g1, s1, g2, s2)] + [high, count - 128 * high]
    vectors.append(jnp.zeros((1, width - 4 * rows - 2), F32))
    turned = router[...].astype(F32)
    last = jnp.concatenate([turned[e : e + 1] for e in range(turned.shape[0])], 1)
    extra = jnp.concatenate([jnp.concatenate(vectors, 1), last], 0)
    block = jnp.concatenate([weights, extra.astype(BF)], 0)
    for k in range(out.shape[0]):
        out[k] = block


def gelu_parts(u):
    phi = 0.5 * lax.erf(u * 0.7071067811865476) + 0.5
    bell = jnp.exp2(u * u * (-0.5 * LOG2E))
    return u * phi, phi + u * bell * 0.3989422804014327


class Pieces:
    def __init__(self, lists):
        self.arrays = [v for pieces in lists for v in pieces]
        self.plan = []
        for pieces in lists:
            ends = [sum(v.shape[0] for v in pieces[: i + 1]) for i in range(len(pieces))]
            self.plan.append([(end - v.shape[0], v.shape[0]) for end, v in zip(ends, pieces)])

    def starter(self, copies, refs, target):
        refs, made = iter(refs), []
        for t, pieces in enumerate(self.plan):
            made.append([(next(refs), target.at[t, slice(at, at + size)]) for at, size in pieces])
        return lambda t: [copies.start(*pair) for pair in made[t]]


def wait_all(copies):
    for copy in copies:
        copy.wait()


def expert_fwd_kernel(ups, downs, step, x, *refs):
    count = len(ups.arrays), len(downs.arrays)
    (out, hidden, slope), (wu, wd, hs, ss, os, sems) = refs[-9:-6], refs[-6:]
    copies = Copies(sems)
    start_up = ups.starter(copies, refs[: count[0]], wu)
    start_down = downs.starter(copies, refs[count[0] : sum(count)], wd)
    n, f = wu.shape[0], wu.shape[2]
    chunks = [slice(row, row + step) for row in range(0, x.shape[0], step)]
    ready, down_in, outgoing = [start_up(t) for t in range(min(2, n))], [], []
    for i, at in enumerate(chunks):
        for t in range(n):
            cols = slice(t * f, (t + 1) * f)
            if i == 0:
                wait_all(ready[t])
                if t + 2 < n:
                    ready.append(start_up(t + 2))
            value, der = gelu_parts(dot(x[at], wu[t], 1, 0))
            hs[at, cols] = value.astype(BF)
            ss[at, cols] = der.astype(BF)
        for t in range(i * n // len(chunks), (i + 1) * n // len(chunks)):
            down_in += start_down(t)
        outgoing.append(copies.start(hs.at[at], hidden.at[at]))
        outgoing.append(copies.start(ss.at[at], slope.at[at]))
    wait_all(down_in)
    for at in chunks:
        os[at] = dot(hs[at], jnp.concatenate([wd[t] for t in range(n)], 1), 1, 1).astype(BF)
        outgoing.append(copies.start(os.at[at], out.at[at]))
    wait_all(outgoing)


def expert_bwd_kernel(ups, downs, step, go, slope, *refs):
    count = len(ups.arrays), len(downs.arrays)
    (grad_up, out), (wu, wd, gs, ss, os, sems) = refs[-8:-6], refs[-6:]
    copies = Copies(sems)
    start_up = ups.starter(copies, refs[: count[0]], wu)
    start_down = downs.starter(copies, refs[count[0] : sum(count)], wd)
    n, f = wu.shape[0], wu.shape[2]
    chunks = [slice(row, row + step) for row in range(0, go.shape[0], step)]
    def start_first(t):
        cols = slice(t * f, (t + 1) * f)
        return start_down(t) + [copies.start(slope.at[chunks[0], cols], ss.at[chunks[0], cols])]

    ready, slope_in = [start_first(t) for t in range(min(2, n))], [None]
    up_in, outgoing = [], []
    for i, at in enumerate(chunks):
        if i > 0:
            slope_in[i].wait()
        if 0 < i and i + 1 < len(chunks):
            slope_in.append(copies.start(slope.at[chunks[i + 1]], ss.at[chunks[i + 1]]))
        for t in range(n):
            cols = slice(t * f, (t + 1) * f)
            if i == 0:
                wait_all(ready[t])
                if t + 2 < n:
                    ready.append(start_first(t + 2))
                elif t + 2 == n and len(chunks) > 1:
                    slope_in.append(copies.start(slope.at[chunks[1]], ss.at[chunks[1]]))
            grad_hidden = dot(go[at], wd[t], 1, 0)
            gs[at, cols] = (grad_hidden * ss[at, cols].astype(F32)).astype(BF)
        for t in range(i * n // len(chunks), (i + 1) * n // len(chunks)):
            up_in += start_up(t)
        outgoing.append(copies.start(gs.at[at], grad_up.at[at]))
    wait_all(up_in)
    for at in chunks:
        os[at] = dot(gs[at], jnp.concatenate([wu[t] for t in range(n)], 1), 1, 1).astype(BF)
        outgoing.append(copies.start(os.at[at], out.at[at]))
    wait_all(outgoing)


def expert_weights_kernel(parts, rows, cols, *refs):
    n = len(parts)
    outs, (rs, cs, os, sems) = refs[:n], refs[n:]
    copies = Copies(sems)
    f = os.shape[2]
    rows_in = copies.start(rows, rs)
    cols_in = [copies.start(cols.at[:, slice(t * f, (t + 1) * f)], cs.at[i]) for i, t in enumerate(parts)]
    rows_in.wait()
    outgoing = []
    for t in range(n):
        cols_in[t].wait()
        os[t] = dot(rs[...], cs[t], 0, 0).astype(BF)
        outgoing.append(copies.start(os.at[t], outs[t]))
    for copy in outgoing:
        copy.wait()


IN_HBM = pl.BlockSpec(memory_space=pltpu.HBM)
IN_VMEM = pl.BlockSpec(memory_space=pltpu.VMEM)


def copying(kernel, ins, in_hbm, outs, out_hbm, scratch, copies, vmem=PLAIN):
    spec = lambda far: IN_HBM if far else IN_VMEM
    return pl.pallas_call(
        kernel,
        in_specs=[spec(far) for far in in_hbm],
        out_specs=[spec(far) for far in out_hbm],
        out_shape=[jax.ShapeDtypeStruct(s, d) for s, d in outs],
        scratch_shapes=[pltpu.VMEM(s, d) for s, d in scratch] + [pltpu.SemaphoreType.DMA((copies,))],
        compiler_params=params(vmem),
        cost_estimate=CHEAP if vmem == ALL else NEAR,
    )(*ins)


def after(value, *others):
    return lax.optimization_barrier((value,) + others)[0]


def local(
    tokens,
    teacher,
    valid_mask,
    expert_ids,
    attn_gain,
    attn_shift,
    qkv_weight,
    proj_weight,
    moe_gain,
    moe_shift,
    router_weight,
    up_weight,
    down_weight,
):
    rows, width = tokens.shape
    length = valid_mask.shape[1]
    images = rows // length
    experts = router_weight.shape[1]
    top = expert_ids.shape[1]
    capacity = max(2, (top * rows + experts - 1) // experts * 5 // 4)
    slots = -(-capacity // 16) * 16
    padded = -(-length // 16) * 16
    own = images * padded
    n_dp = lax.axis_size("dp")
    n_tensor = lax.axis_size("tensor")
    tensor_me = lax.axis_index("tensor")
    heads_width = proj_weight.shape[1]
    heads = heads_width // HD

    def pad(v, value=0):
        v = v.reshape((images, length) + v.shape[1:])
        return jnp.pad(v, ((0, 0), (0, padded - length)) + ((0, 0),) * (v.ndim - 2), constant_values=value)

    def unpad(v):
        return v.reshape(images, padded, -1)[:, :length].reshape(rows, -1)

    x0 = pad(tokens)
    x1 = swap(x0, 1)
    x2 = swap(x0, 2)
    x3 = swap(x2, 1)
    x = (x0, x1, x2, x3)

    dense_rows = proj_weight.shape[0]
    row = lambda v: v.reshape(1, dense_rows)
    [shards] = plain(
        shard_kernel,
        [((n_dp, dense_rows + 2, width), BF)],
        *(qkv_weight, proj_weight, row(attn_gain), row(attn_shift), row(moe_gain), row(moe_shift)),
        *(router_weight.T, valid_mask),
    )
    got = to_all(shards)
    up0, down0 = up_weight[0], down_weight[0]
    part = lambda sixteenths: width * sixteenths // 16
    up2 = [swap(up0[: part(9)], 2)]

    mask = jnp.pad(valid_mask, ((0, 0), (0, padded - length))).reshape(n_tensor, images, 1, padded)
    masks = [lax.dynamic_index_in_dim(mask, tensor_me ^ k, 0, keepdims=False) for k in range(4)]
    row_mask = masks[0].reshape(own, 1).astype(F32)
    ids = pad(expert_ids, -1).reshape(own, top)
    each_expert = lax.iota(jnp.int32, experts)
    named = ids[:, :, None] == each_expert
    names = jnp.any(named, axis=1)
    row_at = lax.iota(jnp.int32, own)
    before = (row_at[:, None] > row_at[None, :]).astype(BF)
    slot = jnp.where(names, dot(before, names.astype(BF), 1, 0).astype(jnp.int32), -1)
    place = jnp.where(ids < 0, -1, ids * slots + jnp.sum(jnp.where(named, slot[:, None, :], 0), -1))
    slot = slot.T

    got, up2[0] = lax.optimization_barrier((got, up2[0]))
    groups = (x3, x2, x1), (masks[3], masks[2], masks[1]), (BF, F32, BF)
    if dense_rows % 16 == 0:
        unpacked = [((width, width), BF), ((4, width), F32), ((experts, width), BF), ((1, 128), F32)]
        third, second, first, w, gains, router, count = attn_fwd(*groups, (got,), unpacked, heads)
        count = count[0, 0]
    else:
        extras = got[:, dense_rows]
        gains = extras[:, : 4 * dense_rows].reshape(n_dp, 4, dense_rows).swapaxes(0, 1).reshape(4, width).astype(F32)
        counts = jnp.sum(extras[:, 4 * dense_rows : 4 * dense_rows + 2].astype(F32), 0)
        count = counts[0] * 128 + counts[1]
        router = got[:, dense_rows + 1].reshape(n_dp, experts, dense_rows).swapaxes(0, 1).reshape(experts, width)
        w = got[:, :dense_rows].reshape(width, width)
        third, second, first = attn_fwd(*groups, (w, gains), [], heads)
    (q3, c3, p3), (q2, c2, p2), (q1, c1, p1) = third, second, first
    far = (p2 + swap(p3, 1).astype(F32)).astype(BF)
    r2 = swap(far, 2)
    [(q0, c0, p0)] = attn_fwd((x0,), (masks[0],), (F32,), (w, gains), [], heads)
    r1 = swap(p1, 1)
    flat = lambda v: v.reshape(own, v.shape[-1])
    row_f32 = ((own, width), F32)
    row_bf = ((own, width), BF)
    all_slots = ((experts * slots, width), BF)
    residual, probs, sent = plain(
        functools.partial(dispatch_kernel, slots),
        [row_f32, ((own, experts), F32), all_slots],
        *(flat(x0), flat(p0), flat(r1), flat(r2), gains, router, slot),
    )
    up2.append(swap(after(up0[part(9) :], r2), 2))
    down2 = [swap(after(down0[: part(12)], r2), 2)]
    down2.append(swap(after(down0[part(12) :], down2[0]), 2))
    beside = lambda v: [swap(piece, 1) for piece in v]
    ups = [[up0], beside([up0]), up2, beside(up2)]
    downs = [[down0], beside([down0]), down2, beside(down2)]

    exchange = lambda v: to_all(v.reshape(n_dp, slots, width)).reshape(n_dp * slots, width)
    arrived = exchange(sent)
    total = n_dp * slots
    step = min(256, total)
    f = up0.shape[1]
    wide = ((total, n_tensor * f), BF)
    weights_in = [((n_tensor, width, f), BF)] * 2
    chunks = total // step
    pieces = Pieces(ups), Pieces(downs)
    weights = pieces[0].arrays + pieces[1].arrays
    out, hidden, slope = copying(
        functools.partial(expert_fwd_kernel, *pieces, step),
        (arrived, *weights),
        (0,) + (1,) * len(weights),
        [all_slots, wide, wide],
        (1, 1, 1),
        weights_in + [wide, wide, all_slots],
        len(weights) + 3 * chunks,
        ALL,
    )
    returned = exchange(out)
    factor = jnp.full((1, 128), rows * n_dp * n_tensor / count, F32)
    result, g, grad_logits, loss_part, grad_sent = plain(
        functools.partial(combine_kernel, slots),
        [row_bf, row_f32, ((own, experts), BF), ((1, width), F32), all_slots],
        *(returned, place, ids, probs, residual, flat(pad(teacher)), row_mask, factor, slot),
    )
    grad_out = exchange(grad_sent)
    grad_up, grad_arrived = copying(
        functools.partial(expert_bwd_kernel, *pieces, min(512, total)),
        (grad_out, slope, *weights),
        (0, 1) + (1,) * len(weights),
        [wide, all_slots],
        (1, 1),
        weights_in + [wide, wide, all_slots],
        len(weights) + n_tensor + 3 * chunks,
        ALL,
    )
    grad_back = exchange(grad_arrived)

    def weight_parts(rows_in, cols_in, parts):
        n = len(parts)
        return copying(
            functools.partial(expert_weights_kernel, parts),
            (rows_in, cols_in),
            (1, 1),
            [((width, f), BF)] * n,
            (1,) * n,
            [all_slots, ((n, total, f), BF), ((n, width, f), BF)],
            2 * n + 1,
            ALL,
        )

    widened = lambda v: v.astype(F32)
    near, far = (0, 1), (2, 3)
    downs_far = weight_parts(grad_out, hidden, far)
    down_far = (widened(downs_far[0]) + widened(swap(downs_far[1], 1))).astype(BF)
    down_got = swap(down_far, 2)
    grad_out, grad_up = lax.optimization_barrier((grad_out, grad_up, downs_far))[:2]
    downs_part = weight_parts(grad_out, hidden, near)
    ups_part = weight_parts(arrived, grad_up, near + far)
    grad_back, down_got, downs_part, ups_part = lax.optimization_barrier((grad_back, down_got, downs_part, ups_part))
    down_near = swap(downs_part[1], 1)
    up_near = swap(ups_part[1], 1)
    up_far = (widened(ups_part[2]) + widened(swap(ups_part[3], 1))).astype(BF)

    grad_residual, grad_attn, vec_two, grad_router = plain(
        back_kernel,
        [row_f32, row_bf, ((2, width), F32), ((experts, width), F32)],
        *(grad_back, place, residual, g, grad_logits, gains, router),
    )

    g0 = grad_attn.reshape(x0.shape)
    g1 = swap(g0, 1)
    g2 = swap(g0, 2)
    packed = ((n_dp, dense_rows + experts, width), BF)
    others = (vec_two, grad_router, loss_part)
    h1, h0, dw, vec_one = attn_bwd(
        *(x1, x0, g1, g0, q1, q0, c1, c0, masks[1], masks[0], w, gains, (), heads, None)
    )
    g2, dw, up_far = lax.optimization_barrier((g2, dw, up_far))
    up_got = [swap(up_far[: part(9)], 2)]
    g3 = swap(g2, 1)
    h3, h2, sums, _ = attn_bwd(
        *(x3, x2, g3, g2, q3, q2, c3, c2, masks[3], masks[2], w, gains, (dw, vec_one) + others, heads, packed)
    )
    sums, up_got[0] = lax.optimization_barrier((sums, up_got[0]))
    t1 = swap(h1, 1)
    t2 = swap((h2 + swap(h3, 1).astype(F32)).astype(BF), 2)
    up_got.append(swap(up_far[part(9) :], 2))
    up_got = jnp.concatenate(up_got)
    grad_down_w = widened(downs_part[0]) + widened(down_near) + widened(down_got)
    grad_up_w = widened(ups_part[0]) + widened(up_near) + widened(up_got)
    [grad_tokens] = plain(
        functools.partial(last_kernel, images), [((rows, width), F32)], *(flat(x0), flat(h0), flat(t1), flat(t2), gains, grad_residual)
    )
    gathered, grad_tokens, grad_down_w, grad_up_w, result = lax.optimization_barrier(
        (to_all(sums), grad_tokens, grad_down_w, grad_up_w, unpad(result))
    )
    grad_qkv_w, grad_proj_w = plain(
        dense_kernel,
        [((dense_rows, 3 * heads_width), F32), (proj_weight.shape, F32)],
        gathered if dense_rows % 16 == 0 else gathered[:, :dense_rows],
    )
    last = jnp.sum(gathered[:, dense_rows:, : 4 * dense_rows].astype(F32), 0)
    piece = lambda i: last[:, i * dense_rows : (i + 1) * dense_rows]
    small = jnp.concatenate([piece(0) + piece(1), piece(2) + piece(3)])
    small = small + swap(small, 1) + swap(small, 2) + swap(small, 3)
    vectors = small[experts:]
    loss = vectors[4, 0] / count
    return (
        loss,
        result,
        grad_tokens,
        vectors[0],
        vectors[1],
        grad_qkv_w.reshape(qkv_weight.shape),
        grad_proj_w,
        vectors[2],
        vectors[3],
        small[:experts].T,
        grad_up_w[None],
        grad_down_w[None],
    )


def solution(mesh):
    rows = P(("dp", "tensor"), None)
    experts = P("dp", None, "tensor")
    in_specs = (
        rows,
        rows,
        P("dp", None),
        rows,
        P("dp"),
        P("dp"),
        experts,
        P("dp", "tensor"),
        P("dp"),
        P("dp"),
        P("dp", None),
        experts,
        experts,
    )
    out_specs = (
        P(),
        rows,
        rows,
        P("dp"),
        P("dp"),
        experts,
        P("dp", "tensor"),
        P("dp"),
        P("dp"),
        P("dp", None),
        experts,
        experts,
    )
    return jax.shard_map(local, mesh=mesh, in_specs=in_specs, out_specs=out_specs, check_vma=False)
```

```python
import functools
import jax
import jax.numpy as jnp
from jax import lax
from jax.experimental import pallas as pl
from jax.experimental.pallas import tpu as pltpu
from jax.sharding import PartitionSpec as P

HD = 64
EPSILON = 1e-06
MASKED = -1000000000.0
BF = jnp.bfloat16
F32 = jnp.float32
LOG2E = 1.4426950408889634
MIB = 1 << 20
PLAIN = 10


def dot(a, b, ca, cb):
    return lax.dot_general(a, b, (((ca,), (cb,)), ((), ())), preferred_element_type=F32)


def swap(value, k):
    n = lax.axis_size("tensor")
    return lax.ppermute(value, "tensor", [(i, i ^ k) for i in range(n)])


def to_all(v):
    return lax.all_to_all(v, "dp", split_axis=0, concat_axis=0, tiled=True)


def norm_parts(v):
    center = v - jnp.mean(v, axis=-1, keepdims=True)
    scale = lax.rsqrt(jnp.mean(center * center, axis=-1, keepdims=True) + EPSILON)
    return center * scale, scale


def norm_back(grad, n, scale, gain):
    gy = grad * gain
    return scale * (
        gy - jnp.mean(gy, -1, keepdims=True) - n * jnp.mean(gy * n, -1, keepdims=True)
    )


def col_sum(v):
    return jnp.sum(v, axis=0, keepdims=True)


def one_image(x, keep, w, gain, shift, heads):
    n, _ = norm_parts(x.astype(F32))
    h1 = (n * gain + shift).astype(BF)
    c = heads * HD
    qkv = dot(h1, w[:, : 3 * c], 1, 0).astype(BF)
    contexts = []
    for h in range(heads):
        q, k, v = (qkv[:, i * c + h * HD : i * c + (h + 1) * HD] for i in range(3))
        s = jnp.where(keep, dot(q, k, 1, 1) * HD**-0.5, MASKED)
        grown = jnp.exp(s - jnp.max(s, -1, keepdims=True))
        probs = grown * (1.0 / jnp.sum(grown, -1, keepdims=True))
        contexts.append(dot(probs.astype(BF), v, 1, 0).astype(BF))
    context = jnp.concatenate(contexts, 1)
    return qkv, context, dot(context, w[:, 3 * c :], 1, 1)


def unpack(got, w, vectors, router, count):
    every = range(got.shape[0])
    rows = w.shape[0] // len(every)
    extras = []
    for k in every:
        block = got[k]
        w[k * rows : (k + 1) * rows] = block[:rows]
        extras.append(block[rows:].astype(F32))
    piece = lambda k, row, j: extras[k][row : row + 1, j * rows : (j + 1) * rows]
    line = lambda row, j: jnp.concatenate([piece(k, row, j) for k in every], 1)
    for j in range(vectors.shape[0]):
        vectors[j : j + 1] = line(0, j)
    router[...] = jnp.concatenate([line(1, j) for j in range(router.shape[0])], 0).astype(BF)
    at = 4 * rows
    total = sum(128 * e[0:1, at : at + 1] + e[0:1, at + 1 : at + 2] for e in extras)
    count[...] = jnp.broadcast_to(total, count.shape)


def attn_fwd_kernel(heads, n, *refs):
    xs, keeps, outs = refs[:n], refs[n : 2 * n], refs[2 * n :]
    if len(outs[0].shape) == 3:
        unpack(outs[0], *outs[-4:])
        w_ref, gains, outs = outs[-4], outs[-3], outs[1:-4]
    else:
        w_ref, gains, outs = outs[0], outs[1], outs[2:]
    w = w_ref[...]
    gain, shift = gains[0:1], gains[1:2]
    for i in range(n):
        for m in range(xs[i].shape[0]):
            values = one_image(xs[i][m], keeps[i][m] > 0, w, gain, shift, heads)
            for out, value in zip(outs[3 * i : 3 * i + 3], values):
                out[m] = value.astype(out.dtype)


CHEAP = pl.CostEstimate(flops=1 << 20, bytes_accessed=1 << 10, transcendentals=0)
NEAR = pl.CostEstimate(flops=1 << 28, bytes_accessed=8 * MIB, transcendentals=0)
ALL = 61


def whole(shape):
    return pl.BlockSpec(shape, lambda *i: (0,) * len(shape))


def params(vmem):
    return pltpu.CompilerParams(vmem_limit_bytes=vmem * MIB)


def attn_fwd(xs, keeps, part_types, weights, unpacked, heads):
    images, rows, width = xs[0].shape
    c = heads * HD
    outs = []
    for part_type in part_types:
        outs += [((rows, 3 * c), BF), ((rows, c), BF), ((rows, width), part_type)]
    outs = [((images,) + s, d) for s, d in outs] + unpacked
    made = pl.pallas_call(
        functools.partial(attn_fwd_kernel, heads, len(xs)),
        grid=(1,),
        in_specs=[whole(v.shape) for v in (*xs, *keeps, *weights)],
        out_specs=[whole(s) for s, _ in outs],
        out_shape=[jax.ShapeDtypeStruct(s, d) for s, d in outs],
        compiler_params=params(ALL),
        cost_estimate=CHEAP,
    )(*xs, *keeps, *weights)
    return [made[3 * i : 3 * i + 3] for i in range(len(xs))] + list(made[3 * len(xs) :])


def one_image_back(x, ga, qkv, context, keep, w, gain, shift, heads):
    n, _ = norm_parts(x.astype(F32))
    h1 = (n * gain + shift).astype(BF)
    c = heads * HD
    gc_all = dot(ga, w[:, 3 * c :], 1, 0).astype(BF)
    length = x.shape[0]
    at = [lax.broadcasted_iota(jnp.int32, (length, length), i) for i in (0, 1)]
    keep = jnp.sum(jnp.where(at[0] == at[1], jnp.where(keep, 1.0, 0.0), 0.0), -1, keepdims=True) > 0
    parts = [[], [], []]
    for h in range(heads):
        q, k, v = (qkv[:, i * c + h * HD : i * c + (h + 1) * HD] for i in range(3))
        gc = gc_all[:, h * HD : (h + 1) * HD]
        s = jnp.where(keep, dot(k, q, 1, 1) * HD**-0.5, MASKED)
        grown = jnp.exp(s - jnp.max(s, 0, keepdims=True))
        p = grown * (1.0 / jnp.sum(grown, 0, keepdims=True))
        gp = dot(v, gc, 1, 1)
        delta = jnp.sum(p * gp, 0, keepdims=True)
        gs = (p * (gp - delta)).astype(BF)
        parts[0].append((dot(gs, k, 0, 0) * HD**-0.5).astype(BF))
        parts[1].append((dot(gs, q, 1, 0) * HD**-0.5).astype(BF))
        parts[2].append(dot(p.astype(BF), gc, 1, 0).astype(BF))
    gqkv = jnp.concatenate(parts[0] + parts[1] + parts[2], 1)
    gh1 = dot(gqkv, w[:, : 3 * c], 1, 1)
    return gh1, h1, gqkv, col_sum(gh1 * n), col_sum(gh1)


def split_float(v):
    high = v.astype(BF)
    return high, (v - high.astype(F32)).astype(BF)


def attn_bwd_kernel(heads, xa, xb, ga, gb, qa, qb, ca, cb, ka, kb, w_ref, gains, *refs):
    others, (ha, hb, dw_out, vec, h_all, q_all, g_all, c_all) = refs[:-8], refs[-8:]

    vec[...] = others[1][...] if others else jnp.zeros_like(vec)
    w = w_ref[...]
    gain, shift = gains[0:1], gains[1:2]
    length = xa.shape[1]
    groups = ((xa, ga, qa, ca, ka, ha), (xb, gb, qb, cb, kb, hb))
    for i, (x, g, q, c, k, out) in enumerate(groups):
        for m in range(x.shape[0]):
            gh1, h1, gqkv, gg, gs = one_image_back(x[m], g[m], q[m], c[m], k[m] > 0, w, gain, shift, heads)
            out[m] = gh1.astype(out.dtype)
            at = slice((2 * m + i) * length, (2 * m + i + 1) * length)
            h_all[at], q_all[at], g_all[at], c_all[at] = h1, gqkv, g[m], c[m]
            vec[0:1] += gg
            vec[1:2] += gs

    dw = jnp.concatenate([dot(h_all[...], q_all[...], 0, 0), dot(g_all[...], c_all[...], 0, 0)], 1)
    if others:
        dw = dw + others[0][...].astype(F32)
    if not others:
        dw_out[...] = dw.astype(BF)
    else:
        rows = dw.shape[0] // dw_out.shape[0]
        vec_two, router, loss = others[2:]
        experts, width = router.shape
        rest = jnp.zeros((experts - 5, width), F32)
        named = jnp.concatenate([vec[...], vec_two[...], loss[...], rest], 0)
        pieces = [p.astype(F32) for v in (router[...], named) for p in split_float(v)]
        for k in range(dw_out.shape[0]):
            at = slice(k * rows, (k + 1) * rows)
            last = jnp.concatenate([p[:, at] for p in pieces] + [jnp.zeros((experts, width - 4 * rows), F32)], 1)
            dw_out[k] = jnp.concatenate([dw[at], last], 0).astype(BF)


def attn_bwd(xa, xb, ga, gb, qa, qb, ca, cb, ka, kb, w, gains, others, heads, pack):
    images, rows, width = xa.shape
    c = heads * HD
    vec_shape = (2, width)
    specs = [whole((images, rows, k)) for k in (width, width, 3 * c, c) for _ in range(2)] + [whole((images, 1, rows))] * 2
    return pl.pallas_call(
        functools.partial(attn_bwd_kernel, heads),
        grid=(1,),
        in_specs=specs + [whole(v.shape) for v in (w, gains) + others],
        out_specs=[whole((images, rows, width))] * 2 + [whole(pack[0] if pack else w.shape), whole(vec_shape)],
        out_shape=[jax.ShapeDtypeStruct(xa.shape, t) for t in (BF, F32)]
        + [jax.ShapeDtypeStruct(*(pack or (w.shape, BF))), jax.ShapeDtypeStruct(vec_shape, F32)],
        scratch_shapes=[pltpu.VMEM((2 * images * rows, k), BF) for k in (width, 3 * c, width, c)],
        compiler_params=params(ALL),
        cost_estimate=CHEAP,
    )(xa, xb, ga, gb, qa, qb, ca, cb, ka, kb, w, gains, *others)


def chosen(slot_row, slots):
    at = lax.broadcasted_iota(jnp.int32, (slots, slot_row.shape[1]), 0)
    return jnp.where(slot_row == at, 1.0, 0.0).astype(BF)


def dispatch_kernel(slots, x, p0, r1, r2, gains, router, slot, residual, probs, sent):
    res = x[...].astype(F32) + p0[...] + r1[...].astype(F32) + r2[...].astype(F32)
    residual[...] = res
    n, _ = norm_parts(res)
    h2 = (n * gains[2:3] + gains[3:4]).astype(BF)
    logits = dot(h2, router[...], 1, 1)
    grown = jnp.exp(logits - jnp.max(logits, -1, keepdims=True))
    probs[...] = grown / jnp.sum(grown, -1, keepdims=True)
    for e in range(slot.shape[0]):
        at = slice(e * slots, (e + 1) * slots)
        sent[at] = dot(chosen(slot[e : e + 1], slots), h2, 1, 0).astype(BF)


def picks(place, total):
    at = lax.broadcasted_iota(jnp.int32, (place.shape[0], total), 1)
    return jnp.where(place == at, 1.0, 0.0)


def combine_kernel(slots, back, place, ids, probs_in, residual, teacher, mask, factor, slot, out, g_out, gl_out, loss, sent):
    probs = probs_in[...]
    experts = probs.shape[1]
    at = lax.broadcasted_iota(jnp.int32, probs.shape, 1)
    choose = [jnp.where(ids[:, j : j + 1] == at, 1.0, 0.0) for j in range(ids.shape[1])]
    gates = [jnp.sum(c * probs, -1, keepdims=True) for c in choose]
    picked = [dot(picks(place[:, j : j + 1], back.shape[0]).astype(BF), back[...], 1, 0) for j in range(len(gates))]
    result = residual[...]
    result = result + sum(gate * p for gate, p in zip(gates, picked))
    out[...] = result.astype(BF)
    errors = result - teacher[...].astype(F32)
    m = mask[...]
    row_loss = jnp.mean(errors * errors, -1, keepdims=True) * m
    loss[...] = jnp.broadcast_to(col_sum(row_loss), loss.shape)
    g = m * errors * factor[0:1, 0:1]
    g_out[...] = g
    grad_probs = sum(c * jnp.sum(g * p, -1, keepdims=True) for c, p in zip(choose, picked))
    grad_logits = probs * (grad_probs - jnp.sum(probs * grad_probs, -1, keepdims=True))
    gl_out[...] = grad_logits.astype(BF)
    for e in range(experts):
        at = slice(e * slots, (e + 1) * slots)
        gated = (probs[:, e : e + 1] * g).astype(BF)
        sent[at] = dot(chosen(slot[e : e + 1], slots), gated, 1, 0).astype(BF)


def back_kernel(back, place, residual, g, gl, gains, router, grad_residual, grad_attn, vec, grad_router):
    either = sum(picks(place[:, j : j + 1], back.shape[0]) for j in range(place.shape[1])).astype(BF)
    grad_h2 = dot(either, back[...], 1, 0) + dot(gl[...], router[...], 1, 0)
    n, scale = norm_parts(residual[...])
    gain = gains[2:3]
    h2 = (n * gain + gains[3:4]).astype(BF)
    vec[0:1] = col_sum(grad_h2 * n)
    vec[1:2] = col_sum(grad_h2)
    grad_router[...] = dot(gl[...], h2, 0, 0)
    total = g[...] + norm_back(grad_h2, n, scale, gain)
    grad_residual[...] = total
    grad_attn[...] = total.astype(BF)


def last_kernel(images, x, p0, r1, r2, gains, grad_residual, out):
    grad_h1 = p0[...] + r1[...].astype(F32) + r2[...].astype(F32)
    n, scale = norm_parts(x[...].astype(F32))
    total = grad_residual[...] + norm_back(grad_h1, n, scale, gains[0:1])
    padded, length = x.shape[0] // images, out.shape[0] // images
    for i in range(images):
        out[i * length : (i + 1) * length] = total[i * padded : i * padded + length]


def plain(kernel, outs, *args):
    return pl.pallas_call(
        kernel,
        grid=(1,),
        in_specs=[whole(v.shape) for v in args],
        out_specs=[whole(s) for s, _ in outs],
        out_shape=[jax.ShapeDtypeStruct(s, d) for s, d in outs],
        compiler_params=params(ALL),
        cost_estimate=CHEAP,
    )(*args)


class Copies:
    def __init__(self, sems):
        self.sems, self.made = sems, []

    def start(self, source, target):
        copy = pltpu.make_async_copy(source, target, self.sems.at[len(self.made)])
        copy.start()
        self.made.append(copy)
        return copy


def dense_kernel(parts, qkv, proj):
    rows, c = proj.shape
    total = parts[0, :rows].astype(F32)
    for k in range(1, parts.shape[0]):
        total = total + parts[k, :rows].astype(F32)
    qkv[...] = total[:, : 3 * c]
    proj[...] = total[:, 3 * c :]


def shard_kernel(qkv, proj, g1, s1, g2, s2, router, mask, out):
    weights = jnp.concatenate([qkv[:, i, :] for i in range(3)] + [proj[...]], 1)
    rows, width = weights.shape
    count = jnp.sum(jnp.sum(mask[...].astype(F32), 1, keepdims=True), 0, keepdims=True)
    high = jnp.floor(count / 128)
    vectors = [v[...].astype(F32) for v in (g1, s1, g2, s2)] + [high, count - 128 * high]
    vectors.append(jnp.zeros((1, width - 4 * rows - 2), F32))
    turned = router[...].astype(F32)
    last = jnp.concatenate([turned[e : e + 1] for e in range(turned.shape[0])], 1)
    extra = jnp.concatenate([jnp.concatenate(vectors, 1), last], 0)
    block = jnp.concatenate([weights, extra.astype(BF)], 0)
    for k in range(out.shape[0]):
        out[k] = block


def gelu_parts(u):
    phi = 0.5 * lax.erf(u * 0.7071067811865476) + 0.5
    bell = jnp.exp2(u * u * (-0.5 * LOG2E))
    return u * phi, phi + u * bell * 0.3989422804014327


class Pieces:
    def __init__(self, lists):
        self.arrays = [v for pieces in lists for v in pieces]
        self.plan = []
        for pieces in lists:
            ends = [sum(v.shape[0] for v in pieces[: i + 1]) for i in range(len(pieces))]
            self.plan.append([(end - v.shape[0], v.shape[0]) for end, v in zip(ends, pieces)])

    def starter(self, copies, refs, target):
        refs, made = iter(refs), []
        for t, pieces in enumerate(self.plan):
            made.append([(next(refs), target.at[t, slice(at, at + size)]) for at, size in pieces])
        return lambda t: [copies.start(*pair) for pair in made[t]]


def wait_all(copies):
    for copy in copies:
        copy.wait()


def expert_fwd_kernel(ups, downs, step, x, *refs):
    count = len(ups.arrays), len(downs.arrays)
    (out, hidden, slope), (wu, wd, hs, ss, os, sems) = refs[-9:-6], refs[-6:]
    copies = Copies(sems)
    start_up = ups.starter(copies, refs[: count[0]], wu)
    start_down = downs.starter(copies, refs[count[0] : sum(count)], wd)
    n, f = wu.shape[0], wu.shape[2]
    chunks = [slice(row, row + step) for row in range(0, x.shape[0], step)]
    ready, down_in, outgoing = [start_up(t) for t in range(min(2, n))], [], []
    for i, at in enumerate(chunks):
        for t in range(n):
            cols = slice(t * f, (t + 1) * f)
            if i == 0:
                wait_all(ready[t])
                if t + 2 < n:
                    ready.append(start_up(t + 2))
            value, der = gelu_parts(dot(x[at], wu[t], 1, 0))
            hs[at, cols] = value.astype(BF)
            ss[at, cols] = der.astype(BF)
        for t in range(i * n // len(chunks), (i + 1) * n // len(chunks)):
            down_in += start_down(t)
        outgoing.append(copies.start(hs.at[at], hidden.at[at]))
        outgoing.append(copies.start(ss.at[at], slope.at[at]))
    wait_all(down_in)
    for at in chunks:
        os[at] = dot(hs[at], jnp.concatenate([wd[t] for t in range(n)], 1), 1, 1).astype(BF)
        outgoing.append(copies.start(os.at[at], out.at[at]))
    wait_all(outgoing)


def expert_bwd_kernel(ups, downs, step, go, slope, *refs):
    count = len(ups.arrays), len(downs.arrays)
    (grad_up, out), (wu, wd, gs, ss, os, sems) = refs[-8:-6], refs[-6:]
    copies = Copies(sems)
    start_up = ups.starter(copies, refs[: count[0]], wu)
    start_down = downs.starter(copies, refs[count[0] : sum(count)], wd)
    n, f = wu.shape[0], wu.shape[2]
    chunks = [slice(row, row + step) for row in range(0, go.shape[0], step)]
    def start_first(t):
        cols = slice(t * f, (t + 1) * f)
        return start_down(t) + [copies.start(slope.at[chunks[0], cols], ss.at[chunks[0], cols])]

    ready, slope_in = [start_first(t) for t in range(min(2, n))], [None]
    up_in, outgoing = [], []
    for i, at in enumerate(chunks):
        if i > 0:
            slope_in[i].wait()
        if 0 < i and i + 1 < len(chunks):
            slope_in.append(copies.start(slope.at[chunks[i + 1]], ss.at[chunks[i + 1]]))
        for t in range(n):
            cols = slice(t * f, (t + 1) * f)
            if i == 0:
                wait_all(ready[t])
                if t + 2 < n:
                    ready.append(start_first(t + 2))
                elif t + 2 == n and len(chunks) > 1:
                    slope_in.append(copies.start(slope.at[chunks[1]], ss.at[chunks[1]]))
            grad_hidden = dot(go[at], wd[t], 1, 0)
            gs[at, cols] = (grad_hidden * ss[at, cols].astype(F32)).astype(BF)
        for t in range(i * n // len(chunks), (i + 1) * n // len(chunks)):
            up_in += start_up(t)
        outgoing.append(copies.start(gs.at[at], grad_up.at[at]))
    wait_all(up_in)
    for at in chunks:
        os[at] = dot(gs[at], jnp.concatenate([wu[t] for t in range(n)], 1), 1, 1).astype(BF)
        outgoing.append(copies.start(os.at[at], out.at[at]))
    wait_all(outgoing)


def expert_weights_kernel(parts, rows, cols, *refs):
    n = len(parts)
    outs, (rs, cs, os, sems) = refs[:n], refs[n:]
    copies = Copies(sems)
    f = os.shape[2]
    rows_in = copies.start(rows, rs)
    cols_in = [copies.start(cols.at[:, slice(t * f, (t + 1) * f)], cs.at[i]) for i, t in enumerate(parts)]
    rows_in.wait()
    outgoing = []
    for t in range(n):
        cols_in[t].wait()
        os[t] = dot(rs[...], cs[t], 0, 0).astype(BF)
        outgoing.append(copies.start(os.at[t], outs[t]))
    for copy in outgoing:
        copy.wait()


IN_HBM = pl.BlockSpec(memory_space=pltpu.HBM)
IN_VMEM = pl.BlockSpec(memory_space=pltpu.VMEM)


def copying(kernel, ins, in_hbm, outs, out_hbm, scratch, copies, vmem=PLAIN):
    spec = lambda far: IN_HBM if far else IN_VMEM
    return pl.pallas_call(
        kernel,
        in_specs=[spec(far) for far in in_hbm],
        out_specs=[spec(far) for far in out_hbm],
        out_shape=[jax.ShapeDtypeStruct(s, d) for s, d in outs],
        scratch_shapes=[pltpu.VMEM(s, d) for s, d in scratch] + [pltpu.SemaphoreType.DMA((copies,))],
        compiler_params=params(vmem),
        cost_estimate=CHEAP if vmem == ALL else NEAR,
    )(*ins)


def after(value, *others):
    return lax.optimization_barrier((value,) + others)[0]


def local(
    tokens,
    teacher,
    valid_mask,
    expert_ids,
    attn_gain,
    attn_shift,
    qkv_weight,
    proj_weight,
    moe_gain,
    moe_shift,
    router_weight,
    up_weight,
    down_weight,
):
    rows, width = tokens.shape
    length = valid_mask.shape[1]
    images = rows // length
    experts = router_weight.shape[1]
    top = expert_ids.shape[1]
    capacity = max(2, (top * rows + experts - 1) // experts * 5 // 4)
    slots = -(-capacity // 16) * 16
    padded = -(-length // 16) * 16
    own = images * padded
    n_dp = lax.axis_size("dp")
    n_tensor = lax.axis_size("tensor")
    tensor_me = lax.axis_index("tensor")
    heads_width = proj_weight.shape[1]
    heads = heads_width // HD

    def pad(v, value=0):
        v = v.reshape((images, length) + v.shape[1:])
        return jnp.pad(v, ((0, 0), (0, padded - length)) + ((0, 0),) * (v.ndim - 2), constant_values=value)

    def unpad(v):
        return v.reshape(images, padded, -1)[:, :length].reshape(rows, -1)

    x0 = pad(tokens)
    x1 = swap(x0, 1)
    x2 = swap(x0, 2)
    x3 = swap(x2, 1)
    x = (x0, x1, x2, x3)

    dense_rows = proj_weight.shape[0]
    row = lambda v: v.reshape(1, dense_rows)
    [shards] = plain(
        shard_kernel,
        [((n_dp, dense_rows + 2, width), BF)],
        *(qkv_weight, proj_weight, row(attn_gain), row(attn_shift), row(moe_gain), row(moe_shift)),
        *(router_weight.T, valid_mask),
    )
    got = to_all(shards)
    up0, down0 = up_weight[0], down_weight[0]
    part = lambda sixteenths: width * sixteenths // 16
    up2 = [swap(up0[: part(9)], 2)]

    mask = jnp.pad(valid_mask, ((0, 0), (0, padded - length))).reshape(n_tensor, images, 1, padded)
    masks = [lax.dynamic_index_in_dim(mask, tensor_me ^ k, 0, keepdims=False) for k in range(4)]
    row_mask = masks[0].reshape(own, 1).astype(F32)
    ids = pad(expert_ids, -1).reshape(own, top)
    each_expert = lax.iota(jnp.int32, experts)
    named = ids[:, :, None] == each_expert
    names = jnp.any(named, axis=1)
    row_at = lax.iota(jnp.int32, own)
    before = (row_at[:, None] > row_at[None, :]).astype(BF)
    slot = jnp.where(names, dot(before, names.astype(BF), 1, 0).astype(jnp.int32), -1)
    place = jnp.where(ids < 0, -1, ids * slots + jnp.sum(jnp.where(named, slot[:, None, :], 0), -1))
    slot = slot.T

    got, up2[0] = lax.optimization_barrier((got, up2[0]))
    groups = (x3, x2, x1), (masks[3], masks[2], masks[1]), (BF, F32, BF)
    if dense_rows % 16 == 0:
        unpacked = [((width, width), BF), ((4, width), F32), ((experts, width), BF), ((1, 128), F32)]
        third, second, first, w, gains, router, count = attn_fwd(*groups, (got,), unpacked, heads)
        count = count[0, 0]
    else:
        extras = got[:, dense_rows]
        gains = extras[:, : 4 * dense_rows].reshape(n_dp, 4, dense_rows).swapaxes(0, 1).reshape(4, width).astype(F32)
        counts = jnp.sum(extras[:, 4 * dense_rows : 4 * dense_rows + 2].astype(F32), 0)
        count = counts[0] * 128 + counts[1]
        router = got[:, dense_rows + 1].reshape(n_dp, experts, dense_rows).swapaxes(0, 1).reshape(experts, width)
        w = got[:, :dense_rows].reshape(width, width)
        third, second, first = attn_fwd(*groups, (w, gains), [], heads)
    (q3, c3, p3), (q2, c2, p2), (q1, c1, p1) = third, second, first
    far = (p2 + swap(p3, 1).astype(F32)).astype(BF)
    r2 = swap(far, 2)
    [(q0, c0, p0)] = attn_fwd((x0,), (masks[0],), (F32,), (w, gains), [], heads)
    r1 = swap(p1, 1)
    flat = lambda v: v.reshape(own, v.shape[-1])
    row_f32 = ((own, width), F32)
    row_bf = ((own, width), BF)
    all_slots = ((experts * slots, width), BF)
    residual, probs, sent = plain(
        functools.partial(dispatch_kernel, slots),
        [row_f32, ((own, experts), F32), all_slots],
        *(flat(x0), flat(p0), flat(r1), flat(r2), gains, router, slot),
    )
    up2.append(swap(after(up0[part(9) :], r2), 2))
    down2 = [swap(after(down0[: part(12)], r2), 2)]
    down2.append(swap(after(down0[part(12) :], down2[0]), 2))
    beside = lambda v: [swap(piece, 1) for piece in v]
    ups = [[up0], beside([up0]), up2, beside(up2)]
    downs = [[down0], beside([down0]), down2, beside(down2)]

    exchange = lambda v: to_all(v.reshape(n_dp, slots, width)).reshape(n_dp * slots, width)
    arrived = exchange(sent)
    total = n_dp * slots
    step = min(256, total)
    f = up0.shape[1]
    wide = ((total, n_tensor * f), BF)
    weights_in = [((n_tensor, width, f), BF)] * 2
    chunks = total // step
    pieces = Pieces(ups), Pieces(downs)
    weights = pieces[0].arrays + pieces[1].arrays
    out, hidden, slope = copying(
        functools.partial(expert_fwd_kernel, *pieces, step),
        (arrived, *weights),
        (0,) + (1,) * len(weights),
        [all_slots, wide, wide],
        (1, 1, 1),
        weights_in + [wide, wide, all_slots],
        len(weights) + 3 * chunks,
        ALL,
    )
    returned = exchange(out)
    factor = jnp.full((1, 128), rows * n_dp * n_tensor / count, F32)
    result, g, grad_logits, loss_part, grad_sent = plain(
        functools.partial(combine_kernel, slots),
        [row_bf, row_f32, ((own, experts), BF), ((1, width), F32), all_slots],
        *(returned, place, ids, probs, residual, flat(pad(teacher)), row_mask, factor, slot),
    )
    grad_out = exchange(grad_sent)
    grad_up, grad_arrived = copying(
        functools.partial(expert_bwd_kernel, *pieces, min(512, total)),
        (grad_out, slope, *weights),
        (0, 1) + (1,) * len(weights),
        [wide, all_slots],
        (1, 1),
        weights_in + [wide, wide, all_slots],
        len(weights) + n_tensor + 3 * chunks,
        ALL,
    )
    grad_back = exchange(grad_arrived)

    def weight_parts(rows_in, cols_in, parts):
        n = len(parts)
        return copying(
            functools.partial(expert_weights_kernel, parts),
            (rows_in, cols_in),
            (1, 1),
            [((width, f), BF)] * n,
            (1,) * n,
            [all_slots, ((n, total, f), BF), ((n, width, f), BF)],
            2 * n + 1,
            ALL,
        )

    widened = lambda v: v.astype(F32)
    near, far = (0, 1), (2, 3)
    downs_far = weight_parts(grad_out, hidden, far)
    down_far = (widened(downs_far[0]) + widened(swap(downs_far[1], 1))).astype(BF)
    down_got = swap(down_far, 2)
    grad_out, grad_up = lax.optimization_barrier((grad_out, grad_up, downs_far))[:2]
    downs_part = weight_parts(grad_out, hidden, near)
    ups_part = weight_parts(arrived, grad_up, near + far)
    grad_back, down_got, downs_part, ups_part = lax.optimization_barrier((grad_back, down_got, downs_part, ups_part))
    down_near = swap(downs_part[1], 1)
    up_near = swap(ups_part[1], 1)
    up_far = (widened(ups_part[2]) + widened(swap(ups_part[3], 1))).astype(BF)

    grad_residual, grad_attn, vec_two, grad_router = plain(
        back_kernel,
        [row_f32, row_bf, ((2, width), F32), ((experts, width), F32)],
        *(grad_back, place, residual, g, grad_logits, gains, router),
    )

    g0 = grad_attn.reshape(x0.shape)
    g1 = swap(g0, 1)
    g2 = swap(g0, 2)
    packed = ((n_dp, dense_rows + experts, width), BF)
    others = (vec_two, grad_router, loss_part)
    h1, h0, dw, vec_one = attn_bwd(
        *(x1, x0, g1, g0, q1, q0, c1, c0, masks[1], masks[0], w, gains, (), heads, None)
    )
    g2, dw, up_far = lax.optimization_barrier((g2, dw, up_far))
    up_got = [swap(up_far[: part(9)], 2)]
    g3 = swap(g2, 1)
    h3, h2, sums, _ = attn_bwd(
        *(x3, x2, g3, g2, q3, q2, c3, c2, masks[3], masks[2], w, gains, (dw, vec_one) + others, heads, packed)
    )
    sums, up_got[0] = lax.optimization_barrier((sums, up_got[0]))
    t1 = swap(h1, 1)
    t2 = swap((h2 + swap(h3, 1).astype(F32)).astype(BF), 2)
    up_got.append(swap(after(up_far[part(9) :], t2), 2))
    up_got = jnp.concatenate(up_got)
    grad_down_w = widened(downs_part[0]) + widened(down_near) + widened(down_got)
    grad_up_w = widened(ups_part[0]) + widened(up_near) + widened(up_got)
    [grad_tokens] = plain(
        functools.partial(last_kernel, images), [((rows, width), F32)], *(flat(x0), flat(h0), flat(t1), flat(t2), gains, grad_residual)
    )
    gathered, grad_tokens, grad_down_w, grad_up_w, result = lax.optimization_barrier(
        (to_all(sums), grad_tokens, grad_down_w, grad_up_w, unpad(result))
    )
    grad_qkv_w, grad_proj_w = plain(
        dense_kernel,
        [((dense_rows, 3 * heads_width), F32), (proj_weight.shape, F32)],
        gathered if dense_rows % 16 == 0 else gathered[:, :dense_rows],
    )
    last = jnp.sum(gathered[:, dense_rows:, : 4 * dense_rows].astype(F32), 0)
    piece = lambda i: last[:, i * dense_rows : (i + 1) * dense_rows]
    small = jnp.concatenate([piece(0) + piece(1), piece(2) + piece(3)])
    small = small + swap(small, 1) + swap(small, 2) + swap(small, 3)
    vectors = small[experts:]
    loss = vectors[4, 0] / count
    return (
        loss,
        result,
        grad_tokens,
        vectors[0],
        vectors[1],
        grad_qkv_w.reshape(qkv_weight.shape),
        grad_proj_w,
        vectors[2],
        vectors[3],
        small[:experts].T,
        grad_up_w[None],
        grad_down_w[None],
    )


def solution(mesh):
    rows = P(("dp", "tensor"), None)
    experts = P("dp", None, "tensor")
    in_specs = (
        rows,
        rows,
        P("dp", None),
        rows,
        P("dp"),
        P("dp"),
        experts,
        P("dp", "tensor"),
        P("dp"),
        P("dp"),
        P("dp", None),
        experts,
        experts,
    )
    out_specs = (
        P(),
        rows,
        rows,
        P("dp"),
        P("dp"),
        experts,
        P("dp", "tensor"),
        P("dp"),
        P("dp"),
        P("dp", None),
        experts,
        experts,
    )
    return jax.shard_map(local, mesh=mesh, in_specs=in_specs, out_specs=out_specs, check_vma=False)
```
